32 devices in a mesh: ens: 4 (over y, x), space: 8 (over z, core).
Axes of the slice: x: 2, y: 2, z: 4, core: 2. Of those that a mesh axis runs over, the one named last changes fastest.
Arguments:
- latents: bfloat16 [8, 2048, 1024], P('ens', 'space'), may hold values from -6 to 6
- edge_index: int32 [4096, 4], P('space'), may hold values from 0 to 767, as said below
- edge_weight: float32 [4096, 4], P('space'), may hold values from 0.1 to 1
- truth: float32 [100, 4096], P(None, 'space'), may hold values from -6 to 6
- w_hidden: bfloat16 [1024, 1024], replicated, may hold values from -0.1875 to 0.1875
- output_weight: bfloat16 [1024, 100], replicated, may hold values from -0.1875 to 0.1875
Outputs:
- grad_latents: float32 [8, 2048, 1024], P('ens', 'space')
- grad_hidden: float32 [1024, 1024], P('space')
- grad_out: float32 [1024, 100], P('space')
The draws below stay inside these ranges and needn't reach their ends.
Inputs may be any that keep to these rules, and one draw needn't show every extreme that they name: edge_index of a grid point holds 4 distinct values, indexing the nodes of the bands below, own and above; the first band never points below and the last never above.
All inputs are finite; a program needn't handle non-finite values.
Results may differ from the reference program's by a relative error of at most 0.012.
The reference program's roundings to bfloat16 on the way count: a program that leaves them out, or rounds other values in their place, can miss the bound.
Values may be sent and summed in bfloat16 or wider, within the bound.
No kernel may reach another device: no remote copies, remote signals or barrier semaphores. Data moves between devices by JAX's collectives and lax.ppermute only.
A program may use at most 64 MiB of HBM per device.

```python
import math
import jax
import jax.numpy as jnp
from jax import lax

H = 1024
V = 100
K = 4
G_DEV = 512
N_DEV = 256
M = 8
NGRID = 4096
NODES = 2048


def draw_edge_index(key, part):
    key = jax.random.fold_in(key, 11)
    first_key, second_key = jax.random.split(key)
    band_id = jnp.arange(NGRID, dtype=jnp.int32) // G_DEV
    bands = NGRID // G_DEV
    lowest = jnp.where(band_id == 0, N_DEV, 0)
    highest = jnp.where(band_id == bands - 1, 2 * N_DEV, 3 * N_DEV)
    extent = highest - lowest
    offset = jax.random.randint(first_key, (NGRID,), 0, 1 << 20) % extent
    stride = 1 + jax.random.randint(second_key, (NGRID,), 0, 1 << 20) % (extent // 4 - 1)
    steps_k = jnp.arange(K, dtype=jnp.int32)
    return (lowest[:, None] + (offset[:, None] + steps_k[None, :] * stride[:, None]) % extent[:, None]).astype(jnp.int32)


def levels(own_key, shape, cuts, smallest, largest):
    factor_of = 1.0
    for axis_at, parts in cuts:
        draws = jax.random.uniform(jax.random.fold_in(jax.random.fold_in(own_key, 6), axis_at), (parts,), jnp.float32, smallest / len(cuts), largest / len(cuts))
        factor_of = factor_of * jnp.repeat(jnp.exp(draws), shape[axis_at] // parts).reshape((-1,) + (1,) * (len(shape) - 1 - axis_at))
    return factor_of


def noise(own_key, shape, width, limit, pieces=(), kind=jnp.bfloat16):
    entries = jax.random.normal(own_key, shape, jnp.float32) * width
    if len(pieces) > 0:
        entries = levels(own_key, shape, pieces, -0.22, 0.18) * entries
    return jnp.clip(entries, min=-limit, max=limit).astype(kind)


def setup_inputs(seed: int = 0) -> dict:
    arg_keys = jax.random.split(jax.random.key(seed), 7)
    latents = noise(arg_keys[0], (M, NODES, H), 1.0, 6.0, ((0, 4), (1, 8)))
    edge_index = draw_edge_index(jax.random.fold_in(arg_keys[6], 71), 0)
    edge_weight = jnp.clip(jnp.exp(math.log(1.0) - 2.3025851 * jax.random.uniform(arg_keys[2], (NGRID, K), jnp.float32) ** levels(arg_keys[2], (NGRID, K), ((0, 8),), -0.2, 0.2)), 0.1, 1.0)
    truth = noise(arg_keys[3], (V, NGRID), 1.0, 6.0, ((1, 8),), jnp.float32)
    w_hidden = noise(arg_keys[4], (H, H), H ** -0.5, 0.1875)
    output_weight = noise(arg_keys[5], (H, V), H ** -0.5, 0.1875)
    return dict(latents=latents, edge_index=edge_index, edge_weight=edge_weight, truth=truth, w_hidden=w_hidden, output_weight=output_weight)


smoothing = 0.05

def silu_slope(preact):
    logistic = jax.nn.sigmoid(preact)
    return logistic * (1.0 + preact * (1.0 - logistic))

def reference(latents, edge_index, edge_weight, truth, w_hidden, output_weight):
    loss_scale = 1.0 / math.sqrt(NGRID * M)
    padded = jnp.pad(latents, ((0, 0), (N_DEV, N_DEV), (0, 0)))
    rounded = lax.optimization_barrier(edge_weight.astype(jnp.bfloat16)).astype(jnp.float32)
    hidden_f = w_hidden.astype(jnp.float32)
    output_float = output_weight.astype(jnp.float32)

    def band_step(carry, band_id):
        grad_padded, grad_hid, grad_outw = carry
        node_start = (band_id * N_DEV).astype(jnp.int32)
        grid_start = (band_id * G_DEV).astype(jnp.int32)
        window = lax.dynamic_slice_in_dim(padded, node_start, 3 * N_DEV, 1)
        indices = lax.dynamic_slice_in_dim(edge_index, grid_start, G_DEV, 0)
        band_weights = lax.dynamic_slice_in_dim(rounded, grid_start, G_DEV, 0)
        observed_target = lax.dynamic_slice_in_dim(truth, grid_start, G_DEV, 1)
        gathered = window[:, indices, :].astype(jnp.float32)
        aggregate = jnp.einsum('mgkh,gk->mgh', gathered, band_weights).astype(jnp.bfloat16)
        preact = jnp.einsum('mgh,hk->mgk', aggregate.astype(jnp.float32), hidden_f)
        activation_values = jax.nn.silu(preact).astype(jnp.bfloat16)
        member_prediction = jnp.einsum('pak,kc->pca', activation_values.astype(jnp.float32), output_float)
        error_residual = member_prediction - observed_target[None]
        distance = jnp.sqrt(error_residual * error_residual + smoothing * smoothing)
        pairwise_distance = member_prediction[:, None] - member_prediction[None, :]
        ensemble_spread = lax.optimization_barrier(jnp.sum(pairwise_distance / jnp.sqrt(pairwise_distance * pairwise_distance + smoothing * smoothing), axis=1))
        dforecast = (loss_scale * (error_residual / (M * distance) - ensemble_spread / (M * (M - 1)))).astype(jnp.bfloat16)
        dforecast_f = dforecast.astype(jnp.float32)
        grad_outw = grad_outw + jnp.einsum('mgh,mvg->hv', activation_values.astype(jnp.float32), dforecast_f)
        dactivated = jnp.einsum('mvg,hv->mgh', dforecast_f, output_float)
        dpreact = (dactivated * silu_slope(preact)).astype(jnp.bfloat16)
        grad_hid = grad_hid + jnp.einsum('mgh,mgk->hk', aggregate.astype(jnp.float32), dpreact.astype(jnp.float32))
        daggregate = jnp.einsum('mgk,hk->mgh', dpreact.astype(jnp.float32), hidden_f).astype(jnp.bfloat16)
        contrib = jnp.einsum('mgh,gk->mgkh', daggregate.astype(jnp.float32), band_weights)
        grad_window = jnp.zeros((M, 3 * N_DEV, H), jnp.float32).at[:, indices.reshape(-1)].add(contrib.reshape(M, G_DEV * K, H))
        current = lax.dynamic_slice_in_dim(grad_padded, node_start, 3 * N_DEV, 1)
        grad_padded = lax.dynamic_update_slice_in_dim(grad_padded, current + grad_window, node_start, 1)
        return ((grad_padded, grad_hid, grad_outw), None)
    start = (jnp.zeros((M, NODES + 2 * N_DEV, H), jnp.float32), jnp.zeros((H, H), jnp.float32), jnp.zeros((H, V), jnp.float32))
    final, _ = lax.scan(band_step, start, jnp.arange(NGRID // G_DEV, dtype=jnp.int32))
    grad_padded, grad_hidden, grad_out = final
    return (grad_padded[:, N_DEV:N_DEV + NODES], grad_hidden, grad_out)
```

```python
import math

import jax
import jax.numpy as jnp
from jax import lax
from jax.sharding import PartitionSpec as P

smoothing = 0.05


def swap(value, axis, bits):
    count = lax.axis_size(axis)
    return lax.ppermute(value, axis, [(i, i ^ bits) for i in range(count)])


def shift(value, axis, steps):
    count = lax.axis_size(axis)
    first, last = (max(0, -steps), min(count, count - steps))
    return lax.ppermute(value, axis, [(source, source + steps) for source in range(first, last)])


def silu_slope(preact):
    logistic = jax.nn.sigmoid(preact)
    return logistic * (1.0 + preact * (1.0 - logistic))


def relative(blocks, own, axis):
    count = blocks.shape[axis]
    return jnp.concatenate(
        [lax.dynamic_slice_in_dim(blocks, own ^ k, 1, axis) for k in range(count)], axis=axis
    )


def shards(latents, edge_index, edge_weight, truth, w_hidden, output_weight):
    mem_dev, nodes_dev, hidden_width = latents.shape
    variables, grid_dev = truth.shape
    ens, space = lax.axis_size("ens"), lax.axis_size("space")
    members = mem_dev * ens
    loss_scale = 1.0 / math.sqrt(grid_dev * space * members)
    e, s = lax.axis_index("ens"), lax.axis_index("space")
    chunk = grid_dev // ens

    below = shift(latents, "space", 1)
    above = shift(latents, "space", -1)
    window = jnp.concatenate([below, latents, above], axis=1)

    index_t = relative(edge_index.T.reshape(-1, ens, chunk), e, 1).reshape(-1, grid_dev)
    weight_t = relative(edge_weight.T.reshape(-1, ens, chunk), e, 1).reshape(-1, grid_dev)
    rounded = lax.optimization_barrier(weight_t.astype(jnp.bfloat16)).astype(jnp.float32)
    row = lax.broadcasted_iota(jnp.int32, (3 * nodes_dev, 1), 0)
    adjacency = sum(
        jnp.where(index_t[k][None] == row, rounded[k][None], 0.0) for k in range(index_t.shape[0])
    ).astype(jnp.bfloat16)
    aggregate = jnp.einsum(
        "ng,mnh->mgh", adjacency, window, preferred_element_type=jnp.float32
    ).astype(jnp.bfloat16)
    preact = jnp.einsum("mgh,hk->mgk", aggregate, w_hidden, preferred_element_type=jnp.float32)
    activated = jax.nn.silu(preact).astype(jnp.bfloat16)
    forecast = jnp.einsum(
        "mgk,kv->mvg", activated, output_weight, preferred_element_type=jnp.float32
    )

    pieces = [forecast[:, :, k * chunk : (k + 1) * chunk] for k in range(ens)]
    here = jnp.concatenate([pieces[0]] + [swap(pieces[k], "ens", k) for k in range(1, ens)], axis=0)
    truth_here = lax.dynamic_slice_in_dim(truth, e * chunk, chunk, 1)
    residual = here - truth_here[None]
    difference = here[:, None] - here[None, :]
    spread = jnp.sum(
        difference / jnp.sqrt(difference * difference + smoothing * smoothing), axis=1
    )
    dhere = (
        loss_scale
        * (
            residual / (members * jnp.sqrt(residual * residual + smoothing * smoothing))
            - spread / (members * (members - 1))
        )
    ).astype(jnp.bfloat16)
    dpieces = [dhere[k * mem_dev : (k + 1) * mem_dev] for k in range(ens)]
    dforecast = jnp.concatenate(
        [dpieces[0]] + [swap(dpieces[k], "ens", k) for k in range(1, ens)], axis=2
    )

    dactivated = jnp.einsum(
        "mvg,hv->mgh", dforecast, output_weight, preferred_element_type=jnp.float32
    )
    dpreact = (dactivated * silu_slope(preact)).astype(jnp.bfloat16)
    hidden_part = jnp.einsum("mgh,mgk->hk", aggregate, dpreact, preferred_element_type=jnp.float32)
    out_part = jnp.einsum("mgh,mvg->hv", activated, dforecast, preferred_element_type=jnp.float32)
    grad_hidden, grad_out = reduced(hidden_part, out_part, e, s, ens, space)

    daggregate = jnp.einsum(
        "mgk,hk->mgh", dpreact, w_hidden, preferred_element_type=jnp.float32
    ).astype(jnp.bfloat16)
    grad_window = jnp.einsum(
        "ng,mgh->mnh", adjacency, daggregate, preferred_element_type=jnp.float32
    )
    lower = grad_window[:, :nodes_dev].astype(jnp.bfloat16)
    upper = grad_window[:, 2 * nodes_dev :].astype(jnp.bfloat16)
    from_above = shift(lower, "space", -1).astype(jnp.float32)
    from_below = shift(upper, "space", 1).astype(jnp.float32)
    grad_latents = grad_window[:, nodes_dev : 2 * nodes_dev] + from_above + from_below
    return (grad_latents, grad_hidden, grad_out)


def reduced(hidden_part, out_part, e, s, ens, space):
    width = hidden_part.shape[1]
    variables = out_part.shape[1]
    lanes = 128 * ens
    joined = jnp.concatenate(
        [
            hidden_part.reshape(-1, ens, width // ens),
            jnp.pad(out_part, ((0, 0), (0, lanes - variables))).reshape(-1, ens, 128),
        ],
        axis=2,
    )
    chips = space // 2
    rows = hidden_part.shape[0] // space
    total = joined.reshape(chips, 2, rows, ens, -1)
    core = s % 2
    chip = s // 2

    def narrow(value):
        return value.astype(jnp.bfloat16)

    def at(value, place, axis):
        return lax.dynamic_index_in_dim(value, place, axis, keepdims=False)

    total = at(total, core, 1) + swap(narrow(at(total, 1 - core, 1)), "space", 1)
    total = at(total, e, 2) + sum(
        swap(narrow(at(total, e ^ k, 2)), "ens", k).astype(jnp.float32) for k in range(1, ens)
    )
    total = at(total, chip, 0) + sum(
        swap(narrow(at(total, chip ^ k, 0)), "space", 2 * k).astype(jnp.float32)
        for k in range(1, chips)
    )
    sent = narrow(total)
    every = jnp.stack(
        [sent] + [swap(sent, "ens", k) for k in range(1, ens)]
    )
    every = relative(every, e, 0).astype(jnp.float32)
    every = jnp.moveaxis(every, 0, 1)
    hidden = every[:, :, : width // ens].reshape(rows, width)
    out = every[:, :, width // ens :].reshape(rows, lanes)[:, :variables]
    return hidden, out


def solution(mesh):
    placed = (
        P("ens", "space", None),
        P("space", None),
        P("space", None),
        P(None, "space"),
        P(),
        P(),
    )
    return jax.shard_map(
        shards,
        mesh=mesh,
        in_specs=placed,
        out_specs=(P("ens", "space", None), P("space", None), P("space", None)),
        check_vma=False,
    )
```

```python
import functools
import math

import jax
import jax.numpy as jnp
from jax import lax
from jax.experimental import pallas as pl
from jax.experimental.pallas import tpu as pltpu
from jax.sharding import PartitionSpec as P

smoothing = 0.05
f32, bf16 = jnp.float32, jnp.bfloat16
across = (((1,), (0,)), ((), ()))
right_turned = (((1,), (1,)), ((), ()))
left_turned = (((0,), (0,)), ((), ()))


def swap(value, axis, bits):
    count = lax.axis_size(axis)
    return lax.ppermute(value, axis, [(i, i ^ bits) for i in range(count)])


def shift(value, axis, steps):
    count = lax.axis_size(axis)
    first, last = (max(0, -steps), min(count, count - steps))
    return lax.ppermute(value, axis, [(source, source + steps) for source in range(first, last)])


def mul(a, b, dims=across):
    return lax.dot_general(a, b, dims, preferred_element_type=f32)


def call(body, outs, place, *operands):
    vmem = pl.BlockSpec(memory_space=pltpu.VMEM)
    return pl.pallas_call(
        body,
        out_shape=[jax.ShapeDtypeStruct(shape, kind) for shape, kind in outs],
        in_specs=[pl.BlockSpec(memory_space=pltpu.SMEM)] + [vmem] * len(operands),
        out_specs=[vmem] * len(outs),
        compiler_params=pltpu.CompilerParams(vmem_limit_bytes=56 * 1024 * 1024),
    )(place, *operands)


def prepare_body(ens, place, index, weight, w_hidden, adjacency, adjacency_t, w_hidden_t):
    own = place[0]
    edges, grid = index.shape
    chunk = grid // ens
    rows = adjacency_t.shape[0]
    row = lax.broadcasted_iota(jnp.int32, (rows, chunk), 0)
    for k in range(ens):
        lanes = pl.ds(pl.multiple_of((own ^ k) * chunk, chunk), chunk)
        nodes = index[:, lanes]
        weights = weight[:, lanes].astype(bf16).astype(f32)
        block = jnp.zeros((rows, chunk), f32)
        for j in range(edges):
            block += jnp.where(nodes[j : j + 1] == row, weights[j : j + 1], 0.0)
        adjacency_t[:, k * chunk : (k + 1) * chunk] = block.astype(bf16)
        adjacency[k * chunk : (k + 1) * chunk, :] = block.T.astype(bf16)
    w_hidden_t[...] = w_hidden[...].T


def forward_body(
    ens, place, below, own, above, adjacency, w_hidden, w_out_t, aggregate, preact, activated, *pieces
):
    mem, nodes, _ = own.shape
    grid = adjacency.shape[0]
    chunk = grid // ens
    width = w_hidden.shape[1]
    step = 256
    for m in range(mem):
        total = mul(adjacency[:, :nodes], below[m])
        total += mul(adjacency[:, nodes : 2 * nodes], own[m])
        total += mul(adjacency[:, 2 * nodes :], above[m])
        gathered = total.astype(bf16)
        aggregate[m] = gathered
        forecast = jnp.zeros((grid, w_out_t.shape[0]), f32)
        for at in range(0, width, step):
            value = mul(gathered, w_hidden[:, at : at + step])
            preact[m, :, at : at + step] = value
            silu = (value / (1.0 + jnp.exp(-value))).astype(bf16)
            activated[m, :, at : at + step] = silu
            forecast += mul(silu, w_out_t[:, at : at + step], right_turned)
        turned = forecast.T
        for k in range(ens):
            pieces[k][m] = turned[:, k * chunk : (k + 1) * chunk]


def slope_body(place, preact, aggregate, slope, aggregate_t):
    mem, grid, width = preact.shape
    for m in range(mem):
        value = preact[m]
        logistic = 1.0 / (1.0 + jnp.exp(-value))
        slope[m] = logistic * (1.0 + value * (1.0 - logistic))
        aggregate_t[:, m * grid : (m + 1) * grid] = aggregate[m].T


def loss_body(ens, scale, place, truth, *refs):
    here, out = refs[:ens], refs[ens:]
    mem, _, chunk = here[0].shape
    members = mem * ens
    target = truth[:, pl.ds(pl.multiple_of(place[0] * chunk, chunk), chunk)]
    forecasts = [here[k][m] for k in range(ens) for m in range(mem)]

    def ratio(d):
        return d * lax.rsqrt(d * d + smoothing * smoothing)

    spread = [jnp.zeros_like(target) for _ in forecasts]
    for i in range(members):
        for j in range(i + 1, members):
            term = ratio(forecasts[i] - forecasts[j])
            spread[i] += term
            spread[j] -= term
    for i in range(members):
        error = ratio(forecasts[i] - target) * (1.0 / members)
        gradient = scale * (error - spread[i] * (1.0 / (members * (members - 1))))
        out[i // mem][i % mem] = gradient.astype(bf16)


def backward_body(ens, place, w_out_t, slope, activated, *refs):
    dforecast, (dpreact, out_part) = refs[:ens], refs[ens:]
    mem, grid, width = slope.shape
    out_total = None
    for m in range(mem):
        gradient = jnp.concatenate([piece[m] for piece in dforecast], axis=1)
        dactivated = mul(gradient, w_out_t[...], left_turned)
        dpreact[m * grid : (m + 1) * grid] = (dactivated * slope[m]).astype(bf16)
        part = mul(gradient, activated[m])
        out_total = part if out_total is None else out_total + part
    out_part[...] = out_total


def half_body(ens, chips, mine, place, aggregate_t, dpreact, out_part, half):
    e, chip, core = place[0], place[1], place[2]
    core = core if mine else 1 - core
    rows = aggregate_t.shape[2]
    lanes = dpreact.shape[1] // ens
    variables = out_part.shape[0]
    strip = 2 * (half.shape[2] - rows)
    left = aggregate_t[:, core].reshape(chips * rows, -1)
    for k in range(ens):
        columns = pl.ds(pl.multiple_of((e ^ k) * lanes, lanes), lanes)
        block = mul(left, dpreact[:, columns])
        for z in range(chips):
            half[k, z ^ chip, :rows] = block[z * rows : (z + 1) * rows].astype(half.dtype)
    padded = jnp.zeros((ens * strip - variables, rows), f32)
    for z in range(chips):
        columns = pl.ds(pl.multiple_of((2 * z + core) * rows, rows), rows)
        part = jnp.concatenate([out_part[:, columns], padded], axis=0).astype(half.dtype)
        for j in range(ens):
            half[j ^ e, z ^ chip, rows:, :rows] = part[j * strip : j * strip + strip // 2]
            half[j ^ e, z ^ chip, rows:, rows:] = part[j * strip + strip // 2 : (j + 1) * strip]


def window_body(place, dpreact, w_hidden_t, adjacency_t, lower, upper, own):
    mem, nodes, width = own.shape
    grid = adjacency_t.shape[1]
    for m in range(mem):
        total = mul(dpreact[m * grid : (m + 1) * grid], w_hidden_t[...]).astype(bf16)
        lower[m] = mul(adjacency_t[:nodes], total).astype(bf16)
        upper[m] = mul(adjacency_t[2 * nodes :], total).astype(bf16)
        own[m] = mul(adjacency_t[nodes : 2 * nodes], total)


def first_sum_body(place, kept, received, mine, *sent):
    for k in range(kept.shape[0]):
        total = kept[k] + received[k].astype(f32)
        if k == 0:
            mine[...] = total
        else:
            sent[k - 1][...] = total.astype(bf16)


def second_sum_body(count, place, kept, *refs):
    received, mine, sent = refs[:count], refs[count], refs[count + 1 :]
    for q in range(kept.shape[0]):
        total = kept[q]
        for block in received:
            total += block[q].astype(f32)
        if q == 0:
            mine[...] = total
        else:
            sent[q - 1][...] = total.astype(bf16)


def third_sum_body(place, kept, *refs):
    received, out = refs[:-1], refs[-1]
    total = kept[...]
    for block in received:
        total += block[...].astype(f32)
    out[...] = total.astype(bf16)


def assemble_body(ens, place, *refs):
    pieces, hidden, out, joined = refs[:ens], refs[ens], refs[ens + 1], refs[ens + 2]
    rows, width = hidden.shape
    lanes = width // ens
    strip = 2 * (pieces[0].shape[0] - rows)
    for k in range(ens):
        source = place[0] ^ k
        piece = pieces[k][...].astype(f32)
        hidden[:, pl.ds(pl.multiple_of(source * lanes, lanes), lanes)] = piece[:rows]
        start = pl.multiple_of(source * strip, strip)
        joined[pl.ds(start, strip // 2), :] = piece[rows:, :rows]
        joined[pl.ds(start + strip // 2, strip // 2), :] = piece[rows:, rows:]
    out[...] = joined[: out.shape[0]]


def reduced(aggregate_t, dpreact, out_part, place, ens, chips):
    width = dpreact.shape[1]
    variables = out_part.shape[0]
    rows = aggregate_t.shape[0] // (2 * chips)
    lanes = width // ens
    strip = 32 * pl.cdiv(variables, 32 * ens)
    aggregate_t = aggregate_t.reshape(chips, 2, rows, -1)
    block = (rows + strip // 2, lanes)
    half = (ens, chips) + block
    given = call(
        functools.partial(half_body, ens, chips, False), [(half, bf16)],
        place, aggregate_t, dpreact, out_part,
    )[0]
    received = swap(given, "space", 1)
    kept = call(
        functools.partial(half_body, ens, chips, True), [(half, f32)],
        place, aggregate_t, dpreact, out_part,
    )[0]
    kept, *given = call(
        first_sum_body, [(half[1:], f32)] + [(half[1:], bf16)] * (ens - 1), place, kept, received
    )
    received = [swap(given[k - 1], "ens", k) for k in range(1, ens)]
    kept, *given = call(
        functools.partial(second_sum_body, ens - 1),
        [(block, f32)] + [(block, bf16)] * (chips - 1), place, kept, *received,
    )
    received = [swap(given[q - 1], "space", 2 * q) for q in range(1, chips)]
    total = call(third_sum_body, [(block, bf16)], place, kept, *received)[0]
    every = [total] + [swap(total, "ens", k) for k in range(1, ens)]
    vmem = pl.BlockSpec(memory_space=pltpu.VMEM)
    hidden, out = pl.pallas_call(
        functools.partial(assemble_body, ens),
        out_shape=[
            jax.ShapeDtypeStruct((rows, width), f32),
            jax.ShapeDtypeStruct((variables, rows), f32),
        ],
        in_specs=[pl.BlockSpec(memory_space=pltpu.SMEM)] + [vmem] * ens,
        out_specs=[vmem] * 2,
        scratch_shapes=[pltpu.VMEM((ens * strip, rows), f32)],
    )(place, *every)
    return hidden, out.T


def reduced_any(aggregate_t, dpreact, out_part):
    part = mul(aggregate_t, dpreact)
    summed = lax.psum((part, out_part.T), "ens")
    return tuple(
        lax.psum_scatter(value, "space", scatter_dimension=0, tiled=True) for value in summed
    )


def shards(latents, edge_index, edge_weight, truth, w_hidden, output_weight):
    mem, nodes, width = latents.shape
    variables, grid = truth.shape
    ens, space = lax.axis_size("ens"), lax.axis_size("space")
    chips = space // 2
    members = mem * ens
    scale = 1.0 / math.sqrt(grid * space * members)
    e, s = lax.axis_index("ens"), lax.axis_index("space")
    place = jnp.stack([e, s // 2, s % 2]).astype(jnp.int32)
    chunk = grid // ens
    w_out_t = output_weight.T

    below = shift(latents, "space", 1)
    above = shift(latents, "space", -1)
    adjacency, adjacency_t, w_hidden_t = call(
        functools.partial(prepare_body, ens),
        [((grid, 3 * nodes), bf16), ((3 * nodes, grid), bf16), (w_hidden.shape[::-1], bf16)],
        place, edge_index.T, edge_weight.T, w_hidden,
    )
    cells = (mem, grid, width)
    piece = (mem, variables, chunk)
    aggregate, preact, activated, *pieces = call(
        functools.partial(forward_body, ens),
        [(cells, bf16), (cells, f32), (cells, bf16)] + [(piece, f32)] * ens,
        place, below, latents, above, adjacency, w_hidden, w_out_t,
    )
    here = [pieces[0]] + [swap(pieces[k], "ens", k) for k in range(1, ens)]
    slope, aggregate_t = call(
        slope_body, [(cells, f32), ((width, mem * grid), bf16)], place, preact, aggregate
    )
    gradients = call(
        functools.partial(loss_body, ens, scale), [(piece, bf16)] * ens, place, truth, *here
    )
    dforecast = [gradients[0]] + [swap(gradients[k], "ens", k) for k in range(1, ens)]
    dpreact, out_part = call(
        functools.partial(backward_body, ens),
        [((mem * grid, width), bf16), ((variables, width), f32)],
        place, w_out_t, slope, activated, *dforecast,
    )
    if width % (space * 128) == 0 and width // ens == 2 * (width // space):
        grad_hidden, grad_out = reduced(aggregate_t, dpreact, out_part, place, ens, chips)
    else:
        grad_hidden, grad_out = reduced_any(aggregate_t, dpreact, out_part)

    band = (mem, nodes, width)
    lower, upper, own = call(
        window_body, [(band, bf16), (band, bf16), (band, f32)],
        place, dpreact, w_hidden_t, adjacency_t,
    )
    from_above = shift(lower, "space", -1).astype(f32)
    from_below = shift(upper, "space", 1).astype(f32)
    return (own + from_above + from_below, grad_hidden, grad_out)


def solution(mesh):
    placed = (
        P("ens", "space", None),
        P("space", None),
        P("space", None),
        P(None, "space"),
        P(),
        P(),
    )
    return jax.shard_map(
        shards,
        mesh=mesh,
        in_specs=placed,
        out_specs=(P("ens", "space", None), P("space", None), P("space", None)),
        check_vma=False,
    )
```

```python
import functools
import math

import jax
import jax.numpy as jnp
from jax import lax
from jax.experimental import pallas as pl
from jax.experimental.pallas import tpu as pltpu
from jax.sharding import PartitionSpec as P

smoothing = 0.05
f32, bf16 = jnp.float32, jnp.bfloat16
across = (((1,), (0,)), ((), ()))
right_turned = (((1,), (1,)), ((), ()))
left_turned = (((0,), (0,)), ((), ()))


def swap(value, axis, bits):
    count = lax.axis_size(axis)
    return lax.ppermute(value, axis, [(i, i ^ bits) for i in range(count)])


def shift(value, axis, steps):
    count = lax.axis_size(axis)
    first, last = (max(0, -steps), min(count, count - steps))
    return lax.ppermute(value, axis, [(source, source + steps) for source in range(first, last)])


def mul(a, b, dims=across):
    return lax.dot_general(a, b, dims, preferred_element_type=f32)


def call(body, outs, place, *operands, after=()):
    vmem = pl.BlockSpec(memory_space=pltpu.VMEM)
    unread = pl.BlockSpec(memory_space=pl.ANY)
    given = len(operands)

    def kernel(place_ref, *refs):
        body(place_ref, *refs[:given], *refs[given + len(after) :])

    return pl.pallas_call(
        kernel,
        out_shape=[pltpu.VMEM(shape, kind) for shape, kind in outs],
        in_specs=[pl.BlockSpec(memory_space=pltpu.SMEM)] + [vmem] * given + [unread] * len(after),
        out_specs=[vmem] * len(outs),
        compiler_params=pltpu.CompilerParams(vmem_limit_bytes=20 * 1024 * 1024),
    )(place, *[pltpu.with_memory_space_constraint(x, pltpu.VMEM) for x in operands], *after)


def prepare_body(ens, place, index, weight, w_hidden, adjacency, adjacency_t, w_hidden_t):
    own = place[0]
    edges, grid = index.shape
    chunk = grid // ens
    rows = adjacency_t.shape[0]
    row = lax.broadcasted_iota(jnp.int32, (rows, chunk), 0)
    for k in range(ens):
        lanes = pl.ds(pl.multiple_of((own ^ k) * chunk, chunk), chunk)
        nodes = index[:, lanes]
        weights = weight[:, lanes].astype(bf16).astype(f32)
        block = jnp.zeros((rows, chunk), f32)
        for j in range(edges):
            block += jnp.where(nodes[j : j + 1] == row, weights[j : j + 1], 0.0)
        adjacency_t[:, k * chunk : (k + 1) * chunk] = block.astype(bf16)
        adjacency[k * chunk : (k + 1) * chunk, :] = block.T.astype(bf16)
    w_hidden_t[...] = w_hidden[...].T


def forward_body(
    ens, place, below, own, above, adjacency, w_hidden, w_out_t, aggregate, preact, activated, *pieces
):
    mem, nodes, _ = own.shape
    grid = adjacency.shape[0]
    chunk = grid // ens
    width = w_hidden.shape[1]
    step = 256
    for m in range(mem):
        total = mul(adjacency[:, :nodes], below[m])
        total += mul(adjacency[:, nodes : 2 * nodes], own[m])
        total += mul(adjacency[:, 2 * nodes :], above[m])
        gathered = total.astype(bf16)
        aggregate[m] = gathered
        forecast = jnp.zeros((grid, w_out_t.shape[0]), f32)
        for at in range(0, width, step):
            value = mul(gathered, w_hidden[:, at : at + step])
            preact[m, :, at : at + step] = value
            silu = (value / (1.0 + jnp.exp(-value))).astype(bf16)
            activated[m, :, at : at + step] = silu
            forecast += mul(silu, w_out_t[:, at : at + step], right_turned)
        turned = forecast.T
        for k in range(ens):
            pieces[k][m] = turned[:, k * chunk : (k + 1) * chunk]


def slope_body(place, preact, slope):
    for m in range(preact.shape[0]):
        value = preact[m]
        logistic = 1.0 / (1.0 + jnp.exp(-value))
        slope[m] = logistic * (1.0 + value * (1.0 - logistic))


def turn_body(place, aggregate, aggregate_t):
    mem, grid, _ = aggregate.shape
    for m in range(mem):
        aggregate_t[:, m * grid : (m + 1) * grid] = aggregate[m].T


def loss_body(ens, scale, place, truth, *refs):
    here, out = refs[:ens], refs[ens:]
    mem, _, chunk = here[0].shape
    members = mem * ens
    target = truth[:, pl.ds(pl.multiple_of(place[0] * chunk, chunk), chunk)]
    forecasts = [here[k][m] for k in range(ens) for m in range(mem)]

    def ratio(d):
        return d * lax.rsqrt(d * d + smoothing * smoothing)

    spread = [jnp.zeros_like(target) for _ in forecasts]
    for i in range(members):
        for j in range(i + 1, members):
            term = ratio(forecasts[i] - forecasts[j])
            spread[i] += term
            spread[j] -= term
    for i in range(members):
        error = ratio(forecasts[i] - target) * (1.0 / members)
        gradient = scale * (error - spread[i] * (1.0 / (members * (members - 1))))
        out[i // mem][i % mem] = gradient.astype(bf16)


def backward_body(ens, place, w_out_t, slope, activated, *refs):
    dforecast, (dpreact, out_part) = refs[:ens], refs[ens:]
    mem, grid, width = slope.shape
    out_total = None
    for m in range(mem):
        gradient = jnp.concatenate([piece[m] for piece in dforecast], axis=1)
        dactivated = mul(gradient, w_out_t[...], left_turned)
        dpreact[m * grid : (m + 1) * grid] = (dactivated * slope[m]).astype(bf16)
        part = mul(gradient, activated[m])
        out_total = part if out_total is None else out_total + part
    out_part[...] = out_total


def half_body(ens, chips, mine, place, aggregate_t, dpreact, out_part, half):
    e, chip, core = place[0], place[1], place[2]
    core = core if mine else 1 - core
    rows = aggregate_t.shape[2]
    lanes = dpreact.shape[1] // ens
    variables = out_part.shape[0]
    strip = 2 * (half.shape[2] - rows)
    left = aggregate_t[:, core].reshape(chips * rows, -1)
    for k in range(ens):
        columns = pl.ds(pl.multiple_of((e ^ k) * lanes, lanes), lanes)
        block = mul(left, dpreact[:, columns])
        for z in range(chips):
            half[k, z ^ chip, :rows] = block[z * rows : (z + 1) * rows].astype(half.dtype)
    padded = jnp.zeros((ens * strip - variables, rows), f32)
    for z in range(chips):
        columns = pl.ds(pl.multiple_of((2 * z + core) * rows, rows), rows)
        part = jnp.concatenate([out_part[:, columns], padded], axis=0).astype(half.dtype)
        for j in range(ens):
            half[j ^ e, z ^ chip, rows:, :rows] = part[j * strip : j * strip + strip // 2]
            half[j ^ e, z ^ chip, rows:, rows:] = part[j * strip + strip // 2 : (j + 1) * strip]


def window_body(place, dpreact, w_hidden_t, adjacency_t, lower, upper, own):
    mem, nodes, width = own.shape
    grid = adjacency_t.shape[1]
    for m in range(mem):
        total = mul(dpreact[m * grid : (m + 1) * grid], w_hidden_t[...]).astype(bf16)
        lower[m] = mul(adjacency_t[:nodes], total).astype(bf16)
        upper[m] = mul(adjacency_t[2 * nodes :], total).astype(bf16)
        own[m] = mul(adjacency_t[nodes : 2 * nodes], total)


def first_sum_body(place, kept, received, mine, *sent):
    for k in range(kept.shape[0]):
        total = kept[k] + received[k].astype(f32)
        if k == 0:
            mine[...] = total
        else:
            sent[k - 1][...] = total.astype(bf16)


def second_sum_body(count, place, kept, *refs):
    received, mine, sent = refs[:count], refs[count], refs[count + 1 :]
    for q in range(kept.shape[0]):
        total = kept[q]
        for block in received:
            total += block[q].astype(f32)
        if q == 0:
            mine[...] = total
        else:
            sent[q - 1][...] = total.astype(bf16)


def third_sum_body(place, kept, *refs):
    received, out = refs[:-1], refs[-1]
    total = kept[...]
    for block in received:
        total += block[...].astype(f32)
    out[...] = total.astype(bf16)


def assemble_body(ens, place, *refs):
    pieces, hidden, out, joined = refs[:ens], refs[ens], refs[ens + 1], refs[ens + 2]
    rows, width = hidden.shape
    lanes = width // ens
    strip = 2 * (pieces[0].shape[0] - rows)
    for k in range(ens):
        source = place[0] ^ k
        piece = pieces[k][...].astype(f32)
        hidden[:, pl.ds(pl.multiple_of(source * lanes, lanes), lanes)] = piece[:rows]
        start = pl.multiple_of(source * strip, strip)
        joined[pl.ds(start, strip // 2), :] = piece[rows:, :rows]
        joined[pl.ds(start + strip // 2, strip // 2), :] = piece[rows:, rows:]
    out[...] = joined[: out.shape[0]]


def reduced(aggregate_t, dpreact, out_part, place, ens, chips):
    width = dpreact.shape[1]
    variables = out_part.shape[0]
    rows = aggregate_t.shape[0] // (2 * chips)
    lanes = width // ens
    strip = 32 * pl.cdiv(variables, 32 * ens)
    aggregate_t = aggregate_t.reshape(chips, 2, rows, -1)
    block = (rows + strip // 2, lanes)
    half = (ens, chips) + block
    given = call(
        functools.partial(half_body, ens, chips, False), [(half, bf16)],
        place, aggregate_t, dpreact, out_part,
    )[0]
    received = swap(given, "space", 1)
    kept = call(
        functools.partial(half_body, ens, chips, True), [(half, f32)],
        place, aggregate_t, dpreact, out_part,
    )[0]
    kept, *given = call(
        first_sum_body, [(half[1:], f32)] + [(half[1:], bf16)] * (ens - 1), place, kept, received
    )
    received = [swap(given[k - 1], "ens", k) for k in range(1, ens)]
    first = kept
    kept, *given = call(
        functools.partial(second_sum_body, ens - 1),
        [(block, f32)] + [(block, bf16)] * (chips - 1), place, kept, *received,
    )
    received = [swap(given[q - 1], "space", 2 * q) for q in range(1, chips)]
    total = call(third_sum_body, [(block, bf16)], place, kept, *received)[0]
    every = [total] + [swap(total, "ens", k) for k in range(1, ens)]
    vmem = pl.BlockSpec(memory_space=pltpu.VMEM)
    hidden, out = pl.pallas_call(
        functools.partial(assemble_body, ens),
        out_shape=[
            jax.ShapeDtypeStruct((rows, width), f32),
            jax.ShapeDtypeStruct((variables, rows), f32),
        ],
        in_specs=[pl.BlockSpec(memory_space=pltpu.SMEM)] + [vmem] * ens,
        out_specs=[vmem] * 2,
        scratch_shapes=[pltpu.VMEM((ens * strip, rows), f32)],
    )(place, *every)
    return hidden, out.T, first


def reduced_any(aggregate_t, dpreact, out_part):
    part = mul(aggregate_t, dpreact)
    summed = lax.psum((part, out_part.T), "ens")
    return tuple(
        lax.psum_scatter(value, "space", scatter_dimension=0, tiled=True) for value in summed
    )


def shards(latents, edge_index, edge_weight, truth, w_hidden, output_weight):
    mem, nodes, width = latents.shape
    variables, grid = truth.shape
    ens, space = lax.axis_size("ens"), lax.axis_size("space")
    chips = space // 2
    members = mem * ens
    scale = 1.0 / math.sqrt(grid * space * members)
    e, s = lax.axis_index("ens"), lax.axis_index("space")
    place = jnp.stack([e, s // 2, s % 2]).astype(jnp.int32)
    chunk = grid // ens
    w_out_t = output_weight.T

    below = shift(latents, "space", 1)
    above = shift(latents, "space", -1)
    adjacency, adjacency_t, w_hidden_t = call(
        functools.partial(prepare_body, ens),
        [((grid, 3 * nodes), bf16), ((3 * nodes, grid), bf16), (w_hidden.shape[::-1], bf16)],
        place, edge_index.T, edge_weight.T, w_hidden,
    )
    cells = (mem, grid, width)
    piece = (mem, variables, chunk)
    aggregate, preact, activated, *pieces = call(
        functools.partial(forward_body, ens),
        [(cells, bf16), (cells, f32), (cells, bf16)] + [(piece, f32)] * ens,
        place, below, latents, above, adjacency, w_hidden, w_out_t,
    )
    here = [pieces[0]] + [swap(pieces[k], "ens", k) for k in range(1, ens)]
    slope = call(slope_body, [(cells, f32)], place, preact, after=pieces)[0]
    gradients = call(
        functools.partial(loss_body, ens, scale), [(piece, bf16)] * ens, place, truth, *here,
        after=[slope],
    )
    aggregate_t = call(
        turn_body, [((width, mem * grid), bf16)], place, aggregate, after=[gradients[0]]
    )[0]
    dforecast = [gradients[0]] + [swap(gradients[k], "ens", k) for k in range(1, ens)]
    dpreact, out_part = call(
        functools.partial(backward_body, ens),
        [((mem * grid, width), bf16), ((variables, width), f32)],
        place, w_out_t, slope, activated, *dforecast,
    )
    if width % (space * 128) == 0 and width // ens == 2 * (width // space):
        grad_hidden, grad_out, *before = reduced(aggregate_t, dpreact, out_part, place, ens, chips)
    else:
        before = []
        grad_hidden, grad_out = reduced_any(aggregate_t, dpreact, out_part)

    band = (mem, nodes, width)
    lower, upper, own = call(
        window_body, [(band, bf16), (band, bf16), (band, f32)],
        place, dpreact, w_hidden_t, adjacency_t, after=before,
    )
    from_above = shift(lower, "space", -1).astype(f32)
    from_below = shift(upper, "space", 1).astype(f32)
    return (own + from_above + from_below, grad_hidden, grad_out)


def solution(mesh):
    placed = (
        P("ens", "space", None),
        P("space", None),
        P("space", None),
        P(None, "space"),
        P(),
        P(),
    )
    return jax.shard_map(
        shards,
        mesh=mesh,
        in_specs=placed,
        out_specs=(P("ens", "space", None), P("space", None), P("space", None)),
        check_vma=False,
    )
```

```python
import functools
import math

import jax
import jax.numpy as jnp
from jax import lax
from jax.experimental import pallas as pl
from jax.experimental.pallas import tpu as pltpu
from jax.sharding import PartitionSpec as P

smoothing = 0.05
f32, bf16 = jnp.float32, jnp.bfloat16
across = (((1,), (0,)), ((), ()))
right_turned = (((1,), (1,)), ((), ()))
left_turned = (((0,), (0,)), ((), ()))


def swap(value, axis, bits):
    count = lax.axis_size(axis)
    return lax.ppermute(value, axis, [(i, i ^ bits) for i in range(count)])


def shift(value, axis, steps):
    count = lax.axis_size(axis)
    first, last = (max(0, -steps), min(count, count - steps))
    return lax.ppermute(value, axis, [(source, source + steps) for source in range(first, last)])


def mul(a, b, dims=across):
    return lax.dot_general(a, b, dims, preferred_element_type=f32)


def call(body, outs, place, *operands, after=(), flops=0):
    vmem = pl.BlockSpec(memory_space=pltpu.VMEM)
    unread = pl.BlockSpec(memory_space=pl.ANY)
    given = len(operands)

    def kernel(place_ref, *refs):
        body(place_ref, *refs[:given], *refs[given + len(after) :])

    return pl.pallas_call(
        kernel,
        out_shape=[pltpu.VMEM(shape, kind) for shape, kind in outs],
        in_specs=[pl.BlockSpec(memory_space=pltpu.SMEM)] + [vmem] * given + [unread] * len(after),
        out_specs=[vmem] * len(outs),
        cost_estimate=pl.CostEstimate(
            flops=flops,
            transcendentals=0,
            bytes_accessed=sum(x.size * x.dtype.itemsize for x in operands)
            + sum(math.prod(shape) * jnp.dtype(kind).itemsize for shape, kind in outs),
        ),
        compiler_params=pltpu.CompilerParams(vmem_limit_bytes=20 * 1024 * 1024),
    )(place, *[pltpu.with_memory_space_constraint(x, pltpu.VMEM) for x in operands], *after)


def prepare_body(
    ens, place, index, weight, w_hidden, latents, w_out_t, adjacency, adjacency_t, w_hidden_t, *copies
):
    own = place[0]
    edges, grid = index.shape
    chunk = grid // ens
    rows = adjacency_t.shape[0]
    row = lax.broadcasted_iota(jnp.int32, (rows, chunk), 0)
    for k in range(ens):
        lanes = pl.ds(pl.multiple_of((own ^ k) * chunk, chunk), chunk)
        nodes = index[:, lanes]
        weights = weight[:, lanes].astype(bf16).astype(f32)
        block = jnp.zeros((rows, chunk), f32)
        for j in range(edges):
            block += jnp.where(nodes[j : j + 1] == row, weights[j : j + 1], 0.0)
        adjacency_t[:, k * chunk : (k + 1) * chunk] = block.astype(bf16)
        adjacency[k * chunk : (k + 1) * chunk, :] = block.T.astype(bf16)
    w_hidden_t[...] = w_hidden[...].T
    for source, copy in zip((latents, w_out_t, w_hidden), copies):
        copy[...] = source[...]


def forward_body(
    ens, m, place, below, own, above, adjacency, w_hidden, w_out_t,
    aggregate, preact, activated, *pieces
):
    nodes = own.shape[1]
    grid = adjacency.shape[0]
    chunk = grid // ens
    width = w_hidden.shape[1]
    step = 256
    total = mul(adjacency[:, :nodes], below[...])
    total += mul(adjacency[:, nodes : 2 * nodes], own[m])
    total += mul(adjacency[:, 2 * nodes :], above[...])
    gathered = total.astype(bf16)
    aggregate[...] = gathered
    forecast = jnp.zeros((grid, w_out_t.shape[0]), f32)
    for at in range(0, width, step):
        value = mul(gathered, w_hidden[:, at : at + step])
        preact[:, at : at + step] = value
        silu = (value / (1.0 + jnp.exp(-value))).astype(bf16)
        activated[:, at : at + step] = silu
        forecast += mul(silu, w_out_t[:, at : at + step], right_turned)
    turned = forecast.T
    for k in range(ens):
        pieces[k][...] = turned[:, k * chunk : (k + 1) * chunk]


def slope_body(place, *refs):
    half = len(refs) // 2
    for preact, slope in zip(refs[:half], refs[half:]):
        value = preact[...]
        logistic = 1.0 / (1.0 + jnp.exp(-value))
        slope[...] = logistic * (1.0 + value * (1.0 - logistic))


def turn_body(place, *refs):
    aggregates, aggregate_t = refs[:-1], refs[-1]
    grid = aggregates[0].shape[0]
    for m, aggregate in enumerate(aggregates):
        aggregate_t[:, m * grid : (m + 1) * grid] = aggregate[...].T


def loss_body(ens, scale, place, truth, *refs):
    here, out = refs[:-ens], refs[-ens:]
    members = len(here)
    mem = members // ens
    chunk = here[0].shape[1]
    target = truth[:, pl.ds(pl.multiple_of(place[0] * chunk, chunk), chunk)]
    forecasts = [ref[...] for ref in here]

    def ratio(d):
        return d * lax.rsqrt(d * d + smoothing * smoothing)

    spread = [jnp.zeros_like(target) for _ in forecasts]
    for i in range(members):
        for j in range(i + 1, members):
            term = ratio(forecasts[i] - forecasts[j])
            spread[i] += term
            spread[j] -= term
    for i in range(members):
        error = ratio(forecasts[i] - target) * (1.0 / members)
        gradient = scale * (error - spread[i] * (1.0 / (members * (members - 1))))
        out[i // mem][i % mem] = gradient.astype(bf16)


def backward_body(ens, mem, place, w_out_t, *refs):
    slopes, activated, refs = refs[:mem], refs[mem : 2 * mem], refs[2 * mem :]
    dforecast, (dpreact, out_part) = refs[:ens], refs[ens:]
    grid = slopes[0].shape[0]
    out_total = None
    for m in range(mem):
        gradient = jnp.concatenate([piece[m] for piece in dforecast], axis=1)
        dactivated = mul(gradient, w_out_t[...], left_turned)
        dpreact[m * grid : (m + 1) * grid] = (dactivated * slopes[m][...]).astype(bf16)
        part = mul(gradient, activated[m][...])
        out_total = part if out_total is None else out_total + part
    out_part[...] = out_total


def half_body(ens, chips, mine, place, aggregate_t, dpreact, out_part, half):
    e, chip, core = place[0], place[1], place[2]
    core = core if mine else 1 - core
    rows = aggregate_t.shape[2]
    lanes = dpreact.shape[1] // ens
    variables = out_part.shape[0]
    strip = 2 * (half.shape[2] - rows)
    left = aggregate_t[:, core].reshape(chips * rows, -1)
    for k in range(ens):
        columns = pl.ds(pl.multiple_of((e ^ k) * lanes, lanes), lanes)
        block = mul(left, dpreact[:, columns])
        for z in range(chips):
            half[k, z ^ chip, :rows] = block[z * rows : (z + 1) * rows].astype(half.dtype)
    padded = jnp.zeros((ens * strip - variables, rows), f32)
    for z in range(chips):
        columns = pl.ds(pl.multiple_of((2 * z + core) * rows, rows), rows)
        part = jnp.concatenate([out_part[:, columns], padded], axis=0).astype(half.dtype)
        for j in range(ens):
            half[j ^ e, z ^ chip, rows:, :rows] = part[j * strip : j * strip + strip // 2]
            half[j ^ e, z ^ chip, rows:, rows:] = part[j * strip + strip // 2 : (j + 1) * strip]


def window_body(place, dpreact, w_hidden_t, adjacency_t, lower, upper, own):
    mem, nodes, width = own.shape
    grid = adjacency_t.shape[1]
    for m in range(mem):
        total = mul(dpreact[m * grid : (m + 1) * grid], w_hidden_t[...]).astype(bf16)
        lower[m] = mul(adjacency_t[:nodes], total).astype(bf16)
        upper[m] = mul(adjacency_t[2 * nodes :], total).astype(bf16)
        own[m] = mul(adjacency_t[nodes : 2 * nodes], total)


def first_sum_body(place, kept, received, mine, *sent):
    for k in range(kept.shape[0]):
        total = kept[k] + received[k].astype(f32)
        if k == 0:
            mine[...] = total
        else:
            sent[k - 1][...] = total.astype(bf16)


def second_sum_body(count, place, kept, *refs):
    received, mine, sent = refs[:count], refs[count], refs[count + 1 :]
    for q in range(kept.shape[0]):
        total = kept[q]
        for block in received:
            total += block[q].astype(f32)
        if q == 0:
            mine[...] = total
        else:
            sent[q - 1][...] = total.astype(bf16)


def third_sum_body(place, kept, *refs):
    received, out = refs[:-1], refs[-1]
    total = kept[...]
    for block in received:
        total += block[...].astype(f32)
    out[...] = total.astype(bf16)


def assemble_body(ens, place, *refs):
    pieces, hidden, out, joined = refs[:ens], refs[ens], refs[ens + 1], refs[ens + 2]
    rows, width = hidden.shape
    lanes = width // ens
    strip = 2 * (pieces[0].shape[0] - rows)
    for k in range(ens):
        source = place[0] ^ k
        piece = pieces[k][...].astype(f32)
        hidden[:, pl.ds(pl.multiple_of(source * lanes, lanes), lanes)] = piece[:rows]
        start = pl.multiple_of(source * strip, strip)
        joined[pl.ds(start, strip // 2), :] = piece[rows:, :rows]
        joined[pl.ds(start + strip // 2, strip // 2), :] = piece[rows:, rows:]
    out[...] = joined[: out.shape[0]]


def reduced(aggregate_t, dpreact, out_part, place, ens, chips, window):
    width = dpreact.shape[1]
    variables = out_part.shape[0]
    rows = aggregate_t.shape[0] // (2 * chips)
    lanes = width // ens
    strip = 32 * pl.cdiv(variables, 32 * ens)
    aggregate_t = aggregate_t.reshape(chips, 2, rows, -1)
    block = (rows + strip // 2, lanes)
    half = (ens, chips) + block
    given = call(
        functools.partial(half_body, ens, chips, False), [(half, bf16)],
        place, aggregate_t, dpreact, out_part,
    )[0]
    received = swap(given, "space", 1)
    kept = call(
        functools.partial(half_body, ens, chips, True), [(half, f32)],
        place, aggregate_t, dpreact, out_part,
    )[0]
    kept, *given = call(
        first_sum_body, [(half[1:], f32)] + [(half[1:], bf16)] * (ens - 1), place, kept, received
    )
    received = [swap(given[k - 1], "ens", k) for k in range(1, ens)]
    grad_latents = window([kept])
    kept, *given = call(
        functools.partial(second_sum_body, ens - 1),
        [(block, f32)] + [(block, bf16)] * (chips - 1), place, kept, *received,
    )
    received = [swap(given[q - 1], "space", 2 * q) for q in range(1, chips)]
    total = call(third_sum_body, [(block, bf16)], place, kept, *received)[0]
    every = [total] + [swap(total, "ens", k) for k in range(1, ens)]
    vmem = pl.BlockSpec(memory_space=pltpu.VMEM)

    def kernel(place_ref, unread_ref, *refs):
        assemble_body(ens, place_ref, *refs)

    hidden, out = pl.pallas_call(
        kernel,
        out_shape=[
            jax.ShapeDtypeStruct((rows, width), f32),
            jax.ShapeDtypeStruct((variables, rows), f32),
        ],
        in_specs=[
            pl.BlockSpec(memory_space=pltpu.SMEM),
            pl.BlockSpec(memory_space=pl.ANY),
        ] + [vmem] * ens,
        out_specs=[vmem] * 2,
        scratch_shapes=[pltpu.VMEM((ens * strip, rows), f32)],
    )(place, grad_latents, *[pltpu.with_memory_space_constraint(x, pltpu.VMEM) for x in every])
    return grad_latents, hidden, out.T


def reduced_any(aggregate_t, dpreact, out_part):
    part = mul(aggregate_t, dpreact)
    summed = lax.psum((part, out_part.T), "ens")
    return tuple(
        lax.psum_scatter(value, "space", scatter_dimension=0, tiled=True) for value in summed
    )


def shards(latents, edge_index, edge_weight, truth, w_hidden, output_weight):
    mem, nodes, width = latents.shape
    variables, grid = truth.shape
    ens, space = lax.axis_size("ens"), lax.axis_size("space")
    chips = space // 2
    members = mem * ens
    scale = 1.0 / math.sqrt(grid * space * members)
    e, s = lax.axis_index("ens"), lax.axis_index("space")
    place = jnp.stack([e, s // 2, s % 2]).astype(jnp.int32)
    chunk = grid // ens
    w_out_t = output_weight.T

    band = (nodes, width)
    halo = [(shift(latents[m], "space", 1), shift(latents[m], "space", -1)) for m in range(mem)]
    adjacency, adjacency_t, w_hidden_t, own, w_out_here, w_hidden_here = call(
        functools.partial(prepare_body, ens),
        [((grid, 3 * nodes), bf16), ((3 * nodes, grid), bf16), (w_hidden.shape[::-1], bf16)]
        + [(x.shape, bf16) for x in (latents, w_out_t, w_hidden)],
        place, edge_index.T, edge_weight.T, w_hidden, latents, w_out_t,
    )
    cells = (grid, width)
    piece = (variables, chunk)
    aggregates, preacts, activated, pieces = [], [], [], []
    for m, (below, above) in enumerate(halo):
        aggregate, preact, silu, *forecast = call(
            functools.partial(forward_body, ens, m),
            [(cells, bf16), (cells, f32), (cells, bf16)] + [(piece, f32)] * ens,
            place, below, own, above, adjacency, w_hidden_here, w_out_here,
            flops=2 * grid * width * (3 * nodes + width + 128),
        )
        aggregates.append(aggregate)
        preacts.append(preact)
        activated.append(silu)
        pieces.append(forecast)
    here = [pieces[m][0] for m in range(mem)]
    for k in range(1, ens):
        here += [swap(pieces[m][k], "ens", k) for m in range(mem)]
    slopes = call(slope_body, [(cells, f32)] * mem, place, *preacts, after=pieces[-1])
    gradients = call(
        functools.partial(loss_body, ens, scale), [((mem,) + piece, bf16)] * ens, place, truth,
        *here, after=slopes,
    )
    aggregate_t = call(
        turn_body, [((width, mem * grid), bf16)], place, *aggregates, after=[gradients[0]]
    )[0]
    dforecast = [gradients[0]] + [swap(gradients[k], "ens", k) for k in range(1, ens)]
    dpreact, out_part = call(
        functools.partial(backward_body, ens, mem),
        [((mem * grid, width), bf16), ((variables, width), f32)],
        place, w_out_here, *slopes, *activated, *dforecast,
        flops=4 * mem * grid * width * 128,
    )
    def window(before):
        lower, upper, middle = call(
            window_body, [((mem,) + band, bf16)] * 2 + [((mem,) + band, f32)],
            place, dpreact, w_hidden_t, adjacency_t, after=before,
            flops=2 * mem * grid * width * (width + 3 * nodes),
        )
        from_above = shift(lower, "space", -1)
        from_below = shift(upper, "space", 1)
        return middle + from_above.astype(f32) + from_below.astype(f32)

    if width % (space * 128) == 0 and width // ens == 2 * (width // space):
        return reduced(aggregate_t, dpreact, out_part, place, ens, chips, window)
    return (window([]), *reduced_any(aggregate_t, dpreact, out_part))


def solution(mesh):
    placed = (
        P("ens", "space", None),
        P("space", None),
        P("space", None),
        P(None, "space"),
        P(),
        P(),
    )
    return jax.shard_map(
        shards,
        mesh=mesh,
        in_specs=placed,
        out_specs=(P("ens", "space", None), P("space", None), P("space", None)),
        check_vma=False,
    )
```

```python
import functools
import math

import jax
import jax.numpy as jnp
from jax import lax
from jax.experimental import pallas as pl
from jax.experimental.pallas import tpu as pltpu
from jax.sharding import PartitionSpec as P

smoothing = 0.05
f32, bf16 = jnp.float32, jnp.bfloat16
across = (((1,), (0,)), ((), ()))
right_turned = (((1,), (1,)), ((), ()))
left_turned = (((0,), (0,)), ((), ()))


def chip_swap(value):
    count = lax.axis_size("space")
    return lax.ppermute(value, "space", [(i, i ^ 1) for i in range(count)])


def link_swap(value):
    count = lax.axis_size("space")
    pairs = [(i, i + 1) for i in range(1, count - 1, 2)]
    return lax.ppermute(value, "space", pairs + [(j, i) for i, j in pairs])


def ens_swap(value, bits):
    ens, space = lax.axis_size("ens"), lax.axis_size("space")
    return lax.ppermute(
        value,
        ("ens", "space"),
        [(e * space + s, (e ^ bits[s % 2]) * space + s) for e in range(ens) for s in range(space)],
    )


def mul(a, b, dims=across):
    return lax.dot_general(a, b, dims, preferred_element_type=f32)


def call(body, outs, place, *operands, after=(), flops=0, last=False, scratch=()):
    vmem = pl.BlockSpec(memory_space=pltpu.VMEM)
    unread = pl.BlockSpec(memory_space=pl.ANY)

    def kernel(place_ref, *refs):
        body(place_ref, *refs[len(after) :])

    return pl.pallas_call(
        kernel,
        out_shape=[
            jax.ShapeDtypeStruct(shape, kind) if last else pltpu.VMEM(shape, kind)
            for shape, kind in outs
        ],
        in_specs=[pl.BlockSpec(memory_space=pltpu.SMEM)]
        + [unread] * len(after)
        + [vmem] * len(operands),
        out_specs=[vmem] * len(outs),
        scratch_shapes=scratch,
        cost_estimate=pl.CostEstimate(
            flops=flops,
            transcendentals=0,
            bytes_accessed=sum(x.size * x.dtype.itemsize for x in operands)
            + sum(math.prod(shape) * jnp.dtype(kind).itemsize for shape, kind in outs),
        ),
        compiler_params=pltpu.CompilerParams(vmem_limit_bytes=20 * 1024 * 1024),
    )(place, *after, *[pltpu.with_memory_space_constraint(x, pltpu.VMEM) for x in operands])


def split(latents):
    mem = latents.shape[0]

    def kernel(source, *refs):
        targets, sems = refs[:mem], refs[mem]
        copies = [
            pltpu.make_async_copy(source.at[m], targets[m], sems.at[m]) for m in range(mem)
        ]
        for copy in copies:
            copy.start()
        for copy in copies:
            copy.wait()

    return pl.pallas_call(
        kernel,
        out_shape=[pltpu.VMEM(latents.shape[1:], latents.dtype)] * mem,
        in_specs=[pl.BlockSpec(memory_space=pltpu.HBM)],
        out_specs=[pl.BlockSpec(memory_space=pltpu.VMEM)] * mem,
        scratch_shapes=[pltpu.SemaphoreType.DMA((mem,))],
    )(pltpu.with_memory_space_constraint(latents, pltpu.HBM))


def sides(core, nodes):
    above, below = 2 * nodes, 0
    return (
        pl.multiple_of(jnp.where(core == 0, above, below), nodes),
        pl.multiple_of(jnp.where(core == 0, below, above), nodes),
    )


def padded(value, rows):
    zeros = jnp.zeros((rows - value.shape[0], value.shape[1]), value.dtype)
    return jnp.concatenate([value, zeros], axis=0)


def prepare_body(
    ens, place, index, weight, w_hidden, w_out_t, truth,
    adjacency, adjacency_t, w_hidden_t, w_hidden_here, w_out_here, truth_here
):
    edges, grid = index.shape
    chunk = grid // ens
    rows = adjacency_t.shape[0]
    row = lax.broadcasted_iota(jnp.int32, (rows, chunk), 0)
    for k in range(ens):
        lanes = slice(k * chunk, (k + 1) * chunk)
        nodes = index[:, lanes]
        weights = weight[:, lanes].astype(bf16).astype(f32)
        block = jnp.zeros((rows, chunk), f32)
        for j in range(edges):
            block += jnp.where(nodes[j : j + 1] == row, weights[j : j + 1], 0.0)
        adjacency_t[:, lanes] = block.astype(bf16)
        adjacency[lanes, :] = block.T.astype(bf16)
    w_hidden_t[...] = w_hidden[...].T
    w_hidden_here[...] = w_hidden[...]
    w_out_here[...] = padded(w_out_t[...].astype(f32), w_out_here.shape[0]).astype(bf16)
    truth_here[...] = padded(truth[...], truth_here.shape[0])


def forward_body(
    ens, m, place, on_chip, own, on_link, adjacency, w_hidden, w_out_t, *refs
):
    *earlier, aggregate, preact, activated, forecasts = refs
    nodes = own.shape[0]
    variables = w_out_t.shape[0]
    grid = adjacency.shape[0]
    chunk = grid // ens
    width = w_hidden.shape[1]
    step = 256
    first, second = sides(place[2], nodes)
    total = mul(adjacency[:, nodes : 2 * nodes], own[...])
    total += mul(adjacency[:, pl.ds(first, nodes)], on_chip[m])
    total += mul(adjacency[:, pl.ds(second, nodes)], on_link[...])
    gathered = total.astype(bf16)
    aggregate[...] = gathered
    forecast = jnp.zeros((grid, w_out_t.shape[0]), f32)
    for at in range(0, width, step):
        value = mul(gathered, w_hidden[:, at : at + step])
        preact[:, at : at + step] = value
        silu = (value / (1.0 + jnp.exp(-value))).astype(bf16)
        activated[:, at : at + step] = silu
        forecast += mul(silu, w_out_t[:, at : at + step], right_turned)
    turned = forecast.T
    for ref in earlier:
        forecasts[:, : m * variables] = ref[...]
    for k in range(ens):
        forecasts[k, m * variables :] = turned[:, k * chunk : (k + 1) * chunk]


def spare_body(place, preact, aggregate, slope, aggregate_t):
    value = preact[...]
    logistic = 1.0 / (1.0 + jnp.exp(-value))
    slope[...] = logistic * (1.0 + value * (1.0 - logistic))
    aggregate_t[...] = aggregate[...].T


def loss_body(mem, scale, place, truth, here, out):
    ens, _, chunk = here.shape
    members = mem * ens
    variables = truth.shape[0]
    target = truth[:, pl.ds(pl.multiple_of(place[0] * chunk, chunk), chunk)]
    forecasts = [
        here[k, m * variables : (m + 1) * variables] for k in range(ens) for m in range(mem)
    ]

    def ratio(d):
        return d * lax.rsqrt(d * d + smoothing * smoothing)

    spread = [jnp.zeros_like(target) for _ in forecasts]
    for i in range(members):
        for j in range(i + 1, members):
            term = ratio(forecasts[i] - forecasts[j])
            spread[i] += term
            spread[j] -= term
    gradients = [
        scale
        * (
            ratio(forecasts[i] - target) * (1.0 / members)
            - spread[i] * (1.0 / (members * (members - 1)))
        )
        for i in range(members)
    ]
    for k in range(ens):
        out[k] = jnp.concatenate(gradients[k * mem : (k + 1) * mem], axis=0).astype(bf16)


def backward_body(mem, place, w_out_t, dforecast, *refs):
    slopes, activated, (dpreact, out_part) = refs[:mem], refs[mem : 2 * mem], refs[2 * mem :]
    variables = w_out_t.shape[0]
    gradients = jnp.concatenate([dforecast[k] for k in range(dforecast.shape[0])], axis=1)
    gradients = gradients.astype(f32)
    out_total = None
    for m in range(mem):
        gradient = gradients[m * variables : (m + 1) * variables].astype(bf16)
        dactivated = mul(gradient, w_out_t[...], left_turned)
        dpreact[m] = (dactivated * slopes[m][...]).astype(bf16)
        part = mul(gradient, activated[m][...])
        out_total = part if out_total is None else out_total + part
    out_part[...] = out_total


def half_body(ens, chips, mine, place, dpreact, out_part, *refs):
    aggregates, half = refs[:-1], refs[-1]
    e, chip, core = place[0], place[1], place[2]
    core = core if mine else 1 - core
    rows = aggregates[0].shape[2]
    lanes = dpreact.shape[2] // ens
    variables = out_part.shape[0]
    strip = 2 * (half.shape[2] - rows)
    left = [ref[:, core].reshape(chips * rows, -1) for ref in aggregates]
    for z in range(chips):
        columns = pl.ds(pl.multiple_of((2 * z + core) * rows, rows), rows)
        part = padded(out_part[:, columns], ens * strip).astype(half.dtype)
        for j in range(ens):
            k = j ^ e
            slot = jnp.where(k == 1 + core, 2, jnp.where(k == 2 - core, 1, k))
            half[slot, z ^ chip, rows:, :rows] = part[j * strip : j * strip + strip // 2]
            half[slot, z ^ chip, rows:, rows:] = part[j * strip + strip // 2 : (j + 1) * strip]
    for slot, k in ((0, 0), (1, 2 - core), (2, 1 + core), (3, 3)):
        columns = pl.ds(pl.multiple_of((e ^ k) * lanes, lanes), lanes)
        block = sum(mul(a, dpreact[m, :, columns]) for m, a in enumerate(left))
        for z in range(chips):
            half[slot, z ^ chip, :rows] = block[z * rows : (z + 1) * rows].astype(half.dtype)


def window_body(place, dpreact, w_hidden_t, adjacency_t, on_chip, on_link, own):
    mem, nodes, width = own.shape
    first, second = sides(place[2], nodes)
    for m in range(mem):
        total = mul(dpreact[m], w_hidden_t[...]).astype(bf16)
        on_link[m] = mul(adjacency_t[pl.ds(second, nodes)], total).astype(bf16)
        on_chip[m] = mul(adjacency_t[pl.ds(first, nodes)], total).astype(bf16)
        own[m] = mul(adjacency_t[nodes : 2 * nodes], total)


def latents_body(place, own, above, below, total):
    for m in range(own.shape[0]):
        total[m] = own[m] + above[m].astype(f32) + below[m].astype(f32)


def ens_sum_body(place, kept, received, mine, sent):
    staying = mine.shape[0]
    for k in range(kept.shape[0]):
        total = kept[k] + received[k].astype(f32)
        if k < staying:
            mine[k] = total
        else:
            sent[k - staying] = total.astype(bf16)


def chip_slots_body(place, kept, received, mine, sent):
    for q in range(kept.shape[1]):
        total = kept[0, q] + received[0, q].astype(f32)
        if q == 0:
            mine[...] = total
        sent[place[1] ^ q] = total.astype(bf16)


def chip_sum_body(place, kept, received, out):
    total = kept[...]
    for q in range(1, received.shape[0]):
        total += received[place[1] ^ q].astype(f32)
    total = total.astype(bf16)
    for k in range(out.shape[0]):
        out[k] = total


def assemble_body(place, pieces, hidden, out, joined):
    rows, width = hidden.shape
    ens = pieces.shape[0]
    lanes = width // ens
    strip = 2 * (pieces.shape[1] - rows)
    for k in range(ens):
        hidden[:, k * lanes : (k + 1) * lanes] = pieces[k, :rows].astype(f32)
        start = k * strip
        joined[start : start + strip // 2, :] = pieces[k, rows:, :rows].astype(f32)
        joined[start + strip // 2 : start + strip, :] = pieces[k, rows:, rows:].astype(f32)
    out[...] = joined[: out.shape[0]]


def reduced(aggregates_t, dpreact, out_part, variables, place, ens, chips, window):
    width = dpreact.shape[2]
    rows = width // (2 * chips)
    lanes = width // ens
    strip = 32 * pl.cdiv(out_part.shape[0], 32 * ens)
    aggregates_t = [x.reshape(chips, 2, rows, -1) for x in aggregates_t]
    block = (rows + strip // 2, lanes)

    def half(mine, kind):
        return call(
            functools.partial(half_body, ens, chips, mine), [((ens, chips) + block, kind)],
            place, dpreact, out_part, *aggregates_t, flops=dpreact.size * width,
        )[0]

    received = chip_swap(half(False, bf16))
    kept = half(True, f32)
    for staying, bits in ((2, (1, 2)), (1, (2, 1))):
        shape = (staying, chips) + block
        kept, given = call(
            ens_sum_body, [(shape, f32), (shape, bf16)], place, kept, received
        )
        received = ens_swap(given, bits)
        if staying == 2:
            latents_sum = window(kept)
    kept, given = call(
        chip_slots_body, [(block, f32), ((chips,) + block, bf16)], place, kept, received
    )
    received = lax.all_to_all(
        given, "space", 0, 0, tiled=True,
        axis_index_groups=[[2 * z + c for z in range(chips)] for c in range(2)],
    )
    total = call(chip_sum_body, [((ens,) + block, bf16)], place, kept, received)[0]
    grad_latents = latents_sum(kept)
    every = lax.all_to_all(total, "ens", 0, 0, tiled=True)
    hidden, out = call(
        assemble_body, [((rows, width), f32), ((variables, rows), f32)],
        place, every, last=True, scratch=[pltpu.VMEM((ens * strip, rows), f32)],
    )
    return grad_latents, hidden, out.T


def reduced_any(aggregates_t, dpreact, out_part, variables):
    part = sum(mul(a, dpreact[m]) for m, a in enumerate(aggregates_t))
    summed = lax.psum((part, out_part[:variables].T), "ens")
    return tuple(
        lax.psum_scatter(value, "space", scatter_dimension=0, tiled=True) for value in summed
    )


def shards(latents, edge_index, edge_weight, truth, w_hidden, output_weight):
    mem, nodes, width = latents.shape
    variables, grid = truth.shape
    ens, space = lax.axis_size("ens"), lax.axis_size("space")
    chips = space // 2
    members = mem * ens
    scale = 1.0 / math.sqrt(grid * space * members)
    e, s = lax.axis_index("ens"), lax.axis_index("space")
    place = jnp.stack([e, s // 2, s % 2]).astype(jnp.int32)
    chunk = grid // ens
    w_out_t = output_weight.T

    own = split(latents)
    on_link = [link_swap(part) for part in own]
    on_chip = chip_swap(latents)
    rows = 8 * pl.cdiv(variables, 8)
    adjacency, adjacency_t, w_hidden_t, w_hidden_here, w_out_here, truth_here = call(
        functools.partial(prepare_body, ens),
        [((grid, 3 * nodes), bf16), ((3 * nodes, grid), bf16), (w_hidden.shape[::-1], bf16)]
        + [(w_hidden.shape, bf16), ((rows, width), bf16), ((rows, grid), f32)],
        place, edge_index.T, edge_weight.T, w_hidden, w_out_t, truth,
    )
    cells = (grid, width)
    activated, slopes, aggregates_t, forecasts = [], [], [], []
    for m in range(mem):
        aggregate, preact, silu, *forecasts = call(
            functools.partial(forward_body, ens, m),
            [(cells, bf16), (cells, f32), (cells, bf16), ((ens, (m + 1) * rows, chunk), f32)],
            place, on_chip, own[m], on_link[m], adjacency, w_hidden_here, w_out_here, *forecasts,
            after=slopes[-1:], flops=2 * grid * width * (3 * nodes + width + 128),
        )
        activated.append(silu)
        if m < mem - 1:
            slope, turned = call(
                spare_body, [(cells, f32), (cells[::-1], bf16)], place, preact, aggregate
            )
            slopes.append(slope)
            aggregates_t.append(turned)
    here = lax.all_to_all(forecasts[0], "ens", 0, 0, tiled=True)
    gradients = call(
        functools.partial(loss_body, mem, scale), [((ens, mem * rows, chunk), bf16)],
        place, truth_here, here,
    )[0]
    dforecast = lax.all_to_all(gradients, "ens", 0, 0, tiled=True)
    slope, turned = call(
        spare_body, [(cells, f32), (cells[::-1], bf16)], place, preact, aggregate,
        after=[gradients],
    )
    slopes.append(slope)
    aggregates_t.append(turned)
    dpreact, out_part = call(
        functools.partial(backward_body, mem),
        [((mem, grid, width), bf16), ((rows, width), f32)],
        place, w_out_here, dforecast, *slopes, *activated,
        flops=4 * mem * grid * width * 128,
    )
    band = (mem, nodes, width)

    def window(*before):
        on_chip, on_link, middle = call(
            window_body, [(band, bf16)] * 2 + [(band, f32)],
            place, dpreact, w_hidden_t, adjacency_t, after=before,
            flops=2 * mem * grid * width * (width + 3 * nodes),
        )
        on_chip, on_link = chip_swap(on_chip), link_swap(on_link)

        def total(*before):
            return call(
                latents_body, [(band, f32)], place, middle, on_chip, on_link,
                after=before, last=True,
            )[0]

        return total

    if width % (space * 128) == 0 and width // ens == 2 * (width // space) and ens == 4:
        return reduced(aggregates_t, dpreact, out_part, variables, place, ens, chips, window)
    return (window()(), *reduced_any(aggregates_t, dpreact, out_part, variables))


def solution(mesh):
    placed = (
        P("ens", "space", None),
        P("space", None),
        P("space", None),
        P(None, "space"),
        P(),
        P(),
    )
    return jax.shard_map(
        shards,
        mesh=mesh,
        in_specs=placed,
        out_specs=(P("ens", "space", None), P("space", None), P("space", None)),
        check_vma=False,
    )
```

```python
import functools
import math

import jax
import jax.numpy as jnp
from jax import lax
from jax.experimental import pallas as pl
from jax.experimental.pallas import tpu as pltpu
from jax.sharding import PartitionSpec as P

smoothing = 0.05
f32, bf16 = jnp.float32, jnp.bfloat16
across = (((1,), (0,)), ((), ()))
right_turned = (((1,), (1,)), ((), ()))
left_turned = (((0,), (0,)), ((), ()))


def chip_swap(value):
    count = lax.axis_size("space")
    return lax.ppermute(value, "space", [(i, i ^ 1) for i in range(count)])


def link_swap(value):
    count = lax.axis_size("space")
    pairs = [(i, i + 1) for i in range(1, count - 1, 2)]
    return lax.ppermute(value, "space", pairs + [(j, i) for i, j in pairs])


def swap(value, axis, bits):
    count = lax.axis_size(axis)
    return lax.ppermute(value, axis, [(i, i ^ bits) for i in range(count)])


def ens_swap(value, bits):
    ens, space = lax.axis_size("ens"), lax.axis_size("space")
    return lax.ppermute(
        value,
        ("ens", "space"),
        [(e * space + s, (e ^ bits[s % 2]) * space + s) for e in range(ens) for s in range(space)],
    )


def mul(a, b, dims=across):
    return lax.dot_general(a, b, dims, preferred_element_type=f32)


def call(body, outs, place, *operands, after=(), far=(), flops=0, last=False, scratch=()):
    vmem = pl.BlockSpec(memory_space=pltpu.VMEM)
    unread = pl.BlockSpec(memory_space=pl.ANY)

    def kernel(place_ref, *refs):
        body(place_ref, *refs[len(after) :])

    return pl.pallas_call(
        kernel,
        out_shape=[
            jax.ShapeDtypeStruct(shape, kind) if last else pltpu.VMEM(shape, kind)
            for shape, kind in outs
        ],
        in_specs=[pl.BlockSpec(memory_space=pltpu.SMEM)]
        + [unread] * len(after)
        + [pl.BlockSpec(memory_space=pltpu.HBM)] * len(far)
        + [vmem] * len(operands),
        out_specs=[vmem] * len(outs),
        scratch_shapes=scratch,
        cost_estimate=pl.CostEstimate(
            flops=flops,
            transcendentals=0,
            bytes_accessed=sum(x.size * x.dtype.itemsize for x in operands)
            + sum(math.prod(shape) * jnp.dtype(kind).itemsize for shape, kind in outs),
        ),
        compiler_params=pltpu.CompilerParams(vmem_limit_bytes=20 * 1024 * 1024),
    )(
        place,
        *after,
        *[pltpu.with_memory_space_constraint(x, pltpu.HBM) for x in far],
        *[pltpu.with_memory_space_constraint(x, pltpu.VMEM) for x in operands],
    )


def sides(core, nodes):
    above, below = 2 * nodes, 0
    return (
        pl.multiple_of(jnp.where(core == 0, above, below), nodes),
        pl.multiple_of(jnp.where(core == 0, below, above), nodes),
    )


def padded(value, rows):
    zeros = jnp.zeros((rows - value.shape[0], value.shape[1]), value.dtype)
    return jnp.concatenate([value, zeros], axis=0)


def prepare_body(
    ens, place, latents, w_hidden, index, weight, w_out_t, truth,
    adjacency, adjacency_t, w_hidden_t, own, w_hidden_here, w_out_here, truth_here, sems
):
    copies = [
        pltpu.make_async_copy(w_hidden, w_hidden_here, sems.at[0]),
        pltpu.make_async_copy(latents, own, sems.at[1]),
    ]
    for copy in copies:
        copy.start()
    edges, grid = index.shape
    chunk = grid // ens
    rows = adjacency_t.shape[0]
    row = lax.broadcasted_iota(jnp.int32, (rows, chunk), 0)
    for k in range(ens):
        lanes = pl.ds(pl.multiple_of((place[0] ^ k) * chunk, chunk), chunk)
        nodes = index[:, lanes]
        weights = weight[:, lanes].astype(bf16).astype(f32)
        block = jnp.zeros((rows, chunk), f32)
        for j in range(edges):
            block += jnp.where(nodes[j : j + 1] == row, weights[j : j + 1], 0.0)
        adjacency_t[:, k * chunk : (k + 1) * chunk] = block.astype(bf16)
        adjacency[k * chunk : (k + 1) * chunk, :] = block.T.astype(bf16)
    w_out_here[...] = padded(w_out_t[...].astype(f32), w_out_here.shape[0]).astype(bf16)
    truth_here[...] = padded(truth[...], truth_here.shape[0])
    for copy in copies:
        copy.wait()
    w_hidden_t[...] = w_hidden_here[...].T


def partial_body(place, own, on_chip, adjacency, partial):
    mem, nodes, _ = own.shape
    first, _ = sides(place[2], nodes)
    for m in range(mem):
        total = mul(adjacency[:, nodes : 2 * nodes], own[m])
        partial[m] = total + mul(adjacency[:, pl.ds(first, nodes)], on_chip[m])


def forward_body(
    ens, place, partial, on_link, adjacency, w_hidden, w_out_t, aggregate, preact, activated, *pieces
):
    mem, nodes, width = on_link.shape
    variables = w_out_t.shape[0]
    grid = adjacency.shape[0]
    chunk = grid // ens
    step = 256
    _, second = sides(place[2], nodes)
    for m in range(mem):
        total = partial[m] + mul(adjacency[:, pl.ds(second, nodes)], on_link[m])
        gathered = total.astype(bf16)
        aggregate[m] = gathered
        forecast = jnp.zeros((grid, variables), f32)
        for at in range(0, width, step):
            value = mul(gathered, w_hidden[:, at : at + step])
            preact[m, :, at : at + step] = value
            silu = (value / (1.0 + jnp.exp(-value))).astype(bf16)
            activated[m, :, at : at + step] = silu
            forecast += mul(silu, w_out_t[:, at : at + step], right_turned)
        turned = forecast.T
        for k in range(ens):
            rows = slice(m * variables, (m + 1) * variables)
            pieces[k][rows] = turned[:, k * chunk : (k + 1) * chunk]


def slope_body(place, preact, slope):
    for m in range(preact.shape[0]):
        value = preact[m]
        logistic = 1.0 / (1.0 + jnp.exp(-value))
        slope[m] = logistic * (1.0 + value * (1.0 - logistic))


def turn_body(place, aggregate, aggregate_t):
    mem, grid, _ = aggregate.shape
    for m in range(mem):
        aggregate_t[:, m * grid : (m + 1) * grid] = aggregate[m].T


def loss_body(ens, scale, place, truth, *refs):
    here, out = refs[:ens], refs[ens:]
    rows, chunk = here[0].shape
    mem = rows // truth.shape[0]
    members = mem * ens
    variables = truth.shape[0]
    target = truth[:, pl.ds(pl.multiple_of(place[0] * chunk, chunk), chunk)]
    forecasts = [
        here[k][m * variables : (m + 1) * variables] for k in range(ens) for m in range(mem)
    ]

    def ratio(d):
        return d * lax.rsqrt(d * d + smoothing * smoothing)

    spread = [jnp.zeros_like(target) for _ in forecasts]
    for i in range(members):
        for j in range(i + 1, members):
            term = ratio(forecasts[i] - forecasts[j])
            spread[i] += term
            spread[j] -= term
    gradients = [
        scale
        * (
            ratio(forecasts[i] - target) * (1.0 / members)
            - spread[i] * (1.0 / (members * (members - 1)))
        )
        for i in range(members)
    ]
    for k in range(ens):
        total = jnp.concatenate(gradients[k * mem : (k + 1) * mem], axis=0)
        out[k][...] = total.astype(bf16)


def backward_body(ens, place, w_out_t, slope, activated, *refs):
    dforecast, (dpreact, out_part) = refs[:ens], refs[ens:]
    mem, grid, _ = slope.shape
    variables = w_out_t.shape[0]
    gradients = jnp.concatenate([piece[...] for piece in dforecast], axis=1)
    gradients = gradients.astype(f32)
    out_total = None
    for m in range(mem):
        gradient = gradients[m * variables : (m + 1) * variables].astype(bf16)
        dactivated = mul(gradient, w_out_t[...], left_turned)
        dpreact[m * grid : (m + 1) * grid] = (dactivated * slope[m]).astype(bf16)
        part = mul(gradient, activated[m])
        out_total = part if out_total is None else out_total + part
    out_part[...] = out_total


def half_body(ens, chips, mine, place, dpreact, out_part, aggregate_t, half):
    e, chip, core = place[0], place[1], place[2]
    core = core if mine else 1 - core
    rows = aggregate_t.shape[2]
    lanes = dpreact.shape[1] // ens
    variables = out_part.shape[0]
    strip = 2 * (half.shape[2] - rows)
    left = aggregate_t[:, core].reshape(chips * rows, -1)
    for z in range(chips):
        columns = pl.ds(pl.multiple_of((2 * z + core) * rows, rows), rows)
        part = padded(out_part[:, columns], ens * strip).astype(half.dtype)
        for j in range(ens):
            k = j ^ e
            slot = jnp.where(k == 1 + core, 2, jnp.where(k == 2 - core, 1, k))
            half[slot, z ^ chip, rows:, :rows] = part[j * strip : j * strip + strip // 2]
            half[slot, z ^ chip, rows:, rows:] = part[j * strip + strip // 2 : (j + 1) * strip]
    for slot, k in ((0, 0), (1, 2 - core), (2, 1 + core), (3, 3)):
        columns = pl.ds(pl.multiple_of((e ^ k) * lanes, lanes), lanes)
        block = mul(left, dpreact[:, columns])
        for z in range(chips):
            half[slot, z ^ chip, :rows] = block[z * rows : (z + 1) * rows].astype(half.dtype)


def window_body(place, dpreact, w_hidden_t, adjacency_t, on_chip, on_link, own):
    mem, nodes, width = own.shape
    grid = adjacency_t.shape[1]
    first, second = sides(place[2], nodes)
    for m in range(mem):
        total = mul(dpreact[m * grid : (m + 1) * grid], w_hidden_t[...]).astype(bf16)
        on_link[m] = mul(adjacency_t[pl.ds(second, nodes)], total).astype(bf16)
        on_chip[m] = mul(adjacency_t[pl.ds(first, nodes)], total).astype(bf16)
        own[m] = mul(adjacency_t[nodes : 2 * nodes], total)


def latents_body(place, own, above, below, total):
    for m in range(own.shape[0]):
        total[m] = own[m] + above[m].astype(f32) + below[m].astype(f32)


def ens_sum_body(place, kept, received, mine, sent):
    staying = mine.shape[0]
    for k in range(kept.shape[0]):
        total = kept[k] + received[k].astype(f32)
        if k < staying:
            mine[k] = total
        else:
            sent[k - staying] = total.astype(bf16)


def chip_slots_body(place, kept, received, mine, *sent):
    for q in range(kept.shape[1]):
        total = kept[0, q] + received[0, q].astype(f32)
        if q == 0:
            mine[...] = total
        else:
            sent[q - 1][...] = total.astype(bf16)


def chip_sum_body(place, kept, *refs):
    received, out = refs[:-1], refs[-1]
    total = kept[...]
    for block in received:
        total += block[...].astype(f32)
    out[...] = total.astype(bf16)


def assemble_body(ens, place, *refs):
    pieces, (hidden, out, joined) = refs[:ens], refs[ens:]
    rows, width = hidden.shape
    lanes = width // ens
    strip = 2 * (pieces[0].shape[0] - rows)
    for k in range(ens):
        source = place[0] ^ k
        piece = pieces[k][...].astype(f32)
        hidden[:, pl.ds(pl.multiple_of(source * lanes, lanes), lanes)] = piece[:rows]
        start = pl.multiple_of(source * strip, strip)
        joined[pl.ds(start, strip // 2), :] = piece[rows:, :rows]
        joined[pl.ds(start + strip // 2, strip // 2), :] = piece[rows:, rows:]
    out[...] = joined[: out.shape[0]]


def reduced(aggregate_t, dpreact, out_part, variables, place, ens, chips, window):
    width = dpreact.shape[1]
    rows = width // (2 * chips)
    lanes = width // ens
    strip = 32 * pl.cdiv(out_part.shape[0], 32 * ens)
    aggregate_t = aggregate_t.reshape(chips, 2, rows, -1)
    block = (rows + strip // 2, lanes)

    def half(mine, kind):
        return call(
            functools.partial(half_body, ens, chips, mine), [((ens, chips) + block, kind)],
            place, dpreact, out_part, aggregate_t, flops=dpreact.size * width,
        )[0]

    received = chip_swap(half(False, bf16))
    kept = half(True, f32)
    for staying, bits in ((2, (1, 2)), (1, (2, 1))):
        shape = (staying, chips) + block
        kept, given = call(
            ens_sum_body, [(shape, f32), (shape, bf16)], place, kept, received
        )
        received = ens_swap(given, bits)
        if staying == 2:
            latents_sum = window(kept)
    kept, *given = call(
        chip_slots_body, [(block, f32)] + [(block, bf16)] * (chips - 1), place, kept, received,
        flops=10**9,
    )
    received = [swap(given[q - 1], "space", 2 * q) for q in range(1, chips)]
    total = call(chip_sum_body, [(block, bf16)], place, kept, *received, flops=10**9)[0]
    every = [total] + [swap(total, "ens", k) for k in range(1, ens)]
    grad_latents = latents_sum(total)
    hidden, out = call(
        functools.partial(assemble_body, ens), [((rows, width), f32), ((variables, rows), f32)],
        place, *every, after=[grad_latents], last=True,
        scratch=[pltpu.VMEM((ens * strip, rows), f32)],
    )
    return grad_latents, hidden, out.T


def reduced_any(aggregate_t, dpreact, out_part, variables):
    part = mul(aggregate_t, dpreact)
    summed = lax.psum((part, out_part[:variables].T), "ens")
    return tuple(
        lax.psum_scatter(value, "space", scatter_dimension=0, tiled=True) for value in summed
    )


def shards(latents, edge_index, edge_weight, truth, w_hidden, output_weight):
    mem, nodes, width = latents.shape
    variables, grid = truth.shape
    ens, space = lax.axis_size("ens"), lax.axis_size("space")
    chips = space // 2
    members = mem * ens
    scale = 1.0 / math.sqrt(grid * space * members)
    e, s = lax.axis_index("ens"), lax.axis_index("space")
    place = jnp.stack([e, s // 2, s % 2]).astype(jnp.int32)
    chunk = grid // ens
    w_out_t = output_weight.T

    on_link = link_swap(latents)
    on_chip = chip_swap(latents)
    rows = 8 * pl.cdiv(variables, 8)
    adjacency, adjacency_t, w_hidden_t, own, w_hidden_here, w_out_here, truth_here = call(
        functools.partial(prepare_body, ens),
        [((grid, 3 * nodes), bf16), ((3 * nodes, grid), bf16), (w_hidden.shape[::-1], bf16)]
        + [(latents.shape, bf16), (w_hidden.shape, bf16)]
        + [((rows, width), bf16), ((rows, grid), f32)],
        place, edge_index.T, edge_weight.T, w_out_t, truth, far=[latents, w_hidden],
        scratch=[pltpu.SemaphoreType.DMA((2,))],
    )
    cells = (mem, grid, width)
    partial = call(partial_body, [(cells, f32)], place, own, on_chip, adjacency)[0]
    piece = (mem * rows, chunk)
    aggregate, preact, activated, *pieces = call(
        functools.partial(forward_body, ens),
        [(cells, bf16), (cells, f32), (cells, bf16)] + [(piece, f32)] * ens,
        place, partial, on_link, adjacency, w_hidden_here, w_out_here,
        flops=2 * mem * grid * width * (nodes + width + 128),
    )
    here = [pieces[0]] + [swap(pieces[k], "ens", k) for k in range(1, ens)]
    slope = call(slope_body, [(cells, f32)], place, preact, after=pieces)[0]
    gradients = call(
        functools.partial(loss_body, ens, scale), [(piece, bf16)] * ens, place, truth_here, *here,
        after=[slope],
    )
    dforecast = [gradients[0]] + [swap(gradients[k], "ens", k) for k in range(1, ens)]
    aggregate_t = call(
        turn_body, [((width, mem * grid), bf16)], place, aggregate, after=gradients
    )[0]
    dpreact, out_part = call(
        functools.partial(backward_body, ens),
        [((mem * grid, width), bf16), ((rows, width), f32)],
        place, w_out_here, slope, activated, *dforecast,
        flops=4 * mem * grid * width * 128,
    )
    band = (mem, nodes, width)

    def window(*before):
        on_chip, on_link, middle = call(
            window_body, [(band, bf16)] * 2 + [(band, f32)],
            place, dpreact, w_hidden_t, adjacency_t, after=before,
            flops=2 * mem * grid * width * (width + 3 * nodes),
        )
        on_chip, on_link = chip_swap(on_chip), link_swap(on_link)

        def total(*before):
            return call(
                latents_body, [(band, f32)], place, middle, on_chip, on_link,
                after=before, last=True,
            )[0]

        return total

    if width % (space * 128) == 0 and width // ens == 2 * (width // space) and ens == 4:
        return reduced(aggregate_t, dpreact, out_part, variables, place, ens, chips, window)
    return (window()(), *reduced_any(aggregate_t, dpreact, out_part, variables))


def solution(mesh):
    placed = (
        P("ens", "space", None),
        P("space", None),
        P("space", None),
        P(None, "space"),
        P(),
        P(),
    )
    return jax.shard_map(
        shards,
        mesh=mesh,
        in_specs=placed,
        out_specs=(P("ens", "space", None), P("space", None), P("space", None)),
        check_vma=False,
    )
```

```python
import functools
import math

import jax
import jax.numpy as jnp
from jax import lax
from jax.experimental import pallas as pl
from jax.experimental.pallas import tpu as pltpu
from jax.sharding import PartitionSpec as P

smoothing = 0.05
f32, bf16 = jnp.float32, jnp.bfloat16
across = (((1,), (0,)), ((), ()))
right_turned = (((1,), (1,)), ((), ()))
left_turned = (((0,), (0,)), ((), ()))


def chip_swap(value):
    count = lax.axis_size("space")
    return lax.ppermute(value, "space", [(i, i ^ 1) for i in range(count)])


def link_swap(value):
    count = lax.axis_size("space")
    pairs = [(i, i + 1) for i in range(1, count - 1, 2)]
    return lax.ppermute(value, "space", pairs + [(j, i) for i, j in pairs])


def swap(value, axis, bits):
    count = lax.axis_size(axis)
    return lax.ppermute(value, axis, [(i, i ^ bits) for i in range(count)])


def core_swap(value, axis, bits):
    ens, space = lax.axis_size("ens"), lax.axis_size("space")

    def partner(e, s):
        bit = bits[s % 2]
        return (e ^ bit) * space + s if axis == "ens" else e * space + (s ^ (2 * bit))

    return lax.ppermute(
        value,
        ("ens", "space"),
        [(e * space + s, partner(e, s)) for e in range(ens) for s in range(space)],
    )


def far_first(ens):
    return [0] + sorted(range(1, ens), key=lambda k: -bin(k).count("1"))


def mul(a, b, dims=across):
    return lax.dot_general(a, b, dims, preferred_element_type=f32)


def call(body, outs, place, *operands, after=(), far=(), flops=0, last=False, scratch=()):
    vmem = pl.BlockSpec(memory_space=pltpu.VMEM)
    unread = pl.BlockSpec(memory_space=pl.ANY)

    def kernel(place_ref, *refs):
        body(place_ref, *refs[len(after) :])

    return pl.pallas_call(
        kernel,
        out_shape=[
            jax.ShapeDtypeStruct(shape, kind) if last else pltpu.VMEM(shape, kind)
            for shape, kind in outs
        ],
        in_specs=[pl.BlockSpec(memory_space=pltpu.SMEM)]
        + [unread] * len(after)
        + [pl.BlockSpec(memory_space=pltpu.HBM)] * len(far)
        + [vmem] * len(operands),
        out_specs=[vmem] * len(outs),
        scratch_shapes=scratch,
        cost_estimate=pl.CostEstimate(
            flops=flops,
            transcendentals=0,
            bytes_accessed=sum(x.size * x.dtype.itemsize for x in operands)
            + sum(math.prod(shape) * jnp.dtype(kind).itemsize for shape, kind in outs),
        ),
        compiler_params=pltpu.CompilerParams(vmem_limit_bytes=20 * 1024 * 1024),
    )(
        place,
        *after,
        *[pltpu.with_memory_space_constraint(x, pltpu.HBM) for x in far],
        *[pltpu.with_memory_space_constraint(x, pltpu.VMEM) for x in operands],
    )


def sides(core, nodes):
    above, below = 2 * nodes, 0
    return (
        pl.multiple_of(jnp.where(core == 0, above, below), nodes),
        pl.multiple_of(jnp.where(core == 0, below, above), nodes),
    )


def padded(value, rows):
    zeros = jnp.zeros((rows - value.shape[0], value.shape[1]), value.dtype)
    return jnp.concatenate([value, zeros], axis=0)


def prepare_body(
    ens, place, latents, w_hidden, index, weight, w_out_t, truth,
    adjacency, adjacency_t, w_hidden_t, own, w_hidden_here, w_out_here, truth_here, sems
):
    copies = [
        pltpu.make_async_copy(w_hidden, w_hidden_here, sems.at[0]),
        pltpu.make_async_copy(latents, own, sems.at[1]),
    ]
    for copy in copies:
        copy.start()
    edges, grid = index.shape
    chunk = grid // ens
    rows = adjacency_t.shape[0]
    row = lax.broadcasted_iota(jnp.int32, (rows, chunk), 0)
    for k in range(ens):
        lanes = pl.ds(pl.multiple_of((place[0] ^ k) * chunk, chunk), chunk)
        nodes = index[:, lanes]
        weights = weight[:, lanes].astype(bf16).astype(f32)
        block = jnp.zeros((rows, chunk), f32)
        for j in range(edges):
            block += jnp.where(nodes[j : j + 1] == row, weights[j : j + 1], 0.0)
        adjacency_t[:, k * chunk : (k + 1) * chunk] = block.astype(bf16)
        adjacency[k * chunk : (k + 1) * chunk, :] = block.T.astype(bf16)
    w_out_here[...] = padded(w_out_t[...].astype(f32), w_out_here.shape[0]).astype(bf16)
    truth_here[...] = padded(truth[...], truth_here.shape[0])
    for copy in copies:
        copy.wait()
    w_hidden_t[...] = w_hidden_here[...].T


def partial_body(place, own, on_chip, adjacency, partial):
    mem, nodes, _ = own.shape
    first, _ = sides(place[2], nodes)
    for m in range(mem):
        total = mul(adjacency[:, nodes : 2 * nodes], own[m])
        partial[m] = total + mul(adjacency[:, pl.ds(first, nodes)], on_chip[m])


def forward_body(
    ens, place, partial, on_link, adjacency, w_hidden, w_out_t, aggregate, preact, activated, *pieces
):
    mem, nodes, width = on_link.shape
    variables = w_out_t.shape[0]
    grid = adjacency.shape[0]
    chunk = grid // ens
    step = 256
    _, second = sides(place[2], nodes)
    for m in range(mem):
        total = partial[m] + mul(adjacency[:, pl.ds(second, nodes)], on_link[m])
        gathered = total.astype(bf16)
        aggregate[m] = gathered
        forecast = jnp.zeros((grid, variables), f32)
        for at in range(0, width, step):
            value = mul(gathered, w_hidden[:, at : at + step])
            preact[m, :, at : at + step] = value
            silu = (value / (1.0 + jnp.exp(-value))).astype(bf16)
            activated[m, :, at : at + step] = silu
            forecast += mul(silu, w_out_t[:, at : at + step], right_turned)
        turned = forecast.T
        for k in range(ens):
            rows = slice(m * variables, (m + 1) * variables)
            pieces[k][rows] = turned[:, k * chunk : (k + 1) * chunk]


def slope_body(place, preact, slope):
    for m in range(preact.shape[0]):
        value = preact[m]
        logistic = 1.0 / (1.0 + jnp.exp(-value))
        slope[m] = logistic * (1.0 + value * (1.0 - logistic))


def turn_body(place, aggregate, aggregate_t):
    mem, grid, _ = aggregate.shape
    for m in range(mem):
        aggregate_t[:, m * grid : (m + 1) * grid] = aggregate[m].T


def loss_body(ens, scale, place, truth, *refs):
    here, out = refs[:ens], refs[ens:]
    rows, chunk = here[0].shape
    mem = rows // truth.shape[0]
    members = mem * ens
    variables = truth.shape[0]
    target = truth[:, pl.ds(pl.multiple_of(place[0] * chunk, chunk), chunk)]
    forecasts = [
        here[k][m * variables : (m + 1) * variables] for k in range(ens) for m in range(mem)
    ]

    def ratio(d):
        return d * lax.rsqrt(d * d + smoothing * smoothing)

    spread = [jnp.zeros_like(target) for _ in forecasts]
    for i in range(members):
        for j in range(i + 1, members):
            term = ratio(forecasts[i] - forecasts[j])
            spread[i] += term
            spread[j] -= term
    gradients = [
        scale
        * (
            ratio(forecasts[i] - target) * (1.0 / members)
            - spread[i] * (1.0 / (members * (members - 1)))
        )
        for i in range(members)
    ]
    for k in range(ens):
        total = jnp.concatenate(gradients[k * mem : (k + 1) * mem], axis=0)
        out[k][...] = total.astype(bf16)


def backward_body(ens, place, w_out_t, slope, activated, *refs):
    dforecast, (dpreact, out_part) = refs[:ens], refs[ens:]
    mem, grid, _ = slope.shape
    variables = w_out_t.shape[0]
    order = far_first(ens)
    gradients = jnp.concatenate([dforecast[order.index(k)][...] for k in range(ens)], axis=1)
    gradients = gradients.astype(f32)
    out_total = None
    for m in range(mem):
        gradient = gradients[m * variables : (m + 1) * variables].astype(bf16)
        dactivated = mul(gradient, w_out_t[...], left_turned)
        dpreact[m * grid : (m + 1) * grid] = (dactivated * slope[m]).astype(bf16)
        part = mul(gradient, activated[m])
        out_total = part if out_total is None else out_total + part
    out_part[...] = out_total


def slot_of(core, k):
    return jnp.where(k == 1 + core, 2, jnp.where(k == 2 - core, 1, k))


def half_body(ens, chips, mine, span, place, dpreact, out_part, aggregate_t, half):
    e, chip, core = place[0], place[1], place[2]
    core = core if mine else 1 - core
    rows = aggregate_t.shape[2]
    lanes = dpreact.shape[1] // ens
    first, last = span
    height = last - first
    if first == 0:
        strip = 2 * (half.shape[2] - height)
        for z in range(chips):
            columns = pl.ds(pl.multiple_of((2 * z + core) * rows, rows), rows)
            part = padded(out_part[:, columns], ens * strip).astype(half.dtype)
            to = slot_of(core, z ^ chip)
            for j in range(ens):
                slot = slot_of(core, j ^ e)
                half[slot, to, height:, :rows] = part[j * strip : j * strip + strip // 2]
                half[slot, to, height:, rows:] = part[j * strip + strip // 2 : (j + 1) * strip]
    left = aggregate_t[:, core, first:last].reshape(chips * height, -1)
    for slot, k in ((0, 0), (1, 2 - core), (2, 1 + core), (3, 3)):
        columns = pl.ds(pl.multiple_of((e ^ k) * lanes, lanes), lanes)
        block = mul(left, dpreact[:, columns]).astype(half.dtype)
        for z in range(chips):
            half[slot, slot_of(core, z ^ chip), :height] = block[z * height : (z + 1) * height]


def window_body(place, dpreact, w_hidden_t, adjacency_t, on_chip, on_link, own):
    mem, nodes, width = own.shape
    grid = adjacency_t.shape[1]
    first, second = sides(place[2], nodes)
    for m in range(mem):
        total = mul(dpreact[m * grid : (m + 1) * grid], w_hidden_t[...]).astype(bf16)
        on_link[m] = mul(adjacency_t[pl.ds(second, nodes)], total).astype(bf16)
        on_chip[m] = mul(adjacency_t[pl.ds(first, nodes)], total).astype(bf16)
        own[m] = mul(adjacency_t[nodes : 2 * nodes], total)


def latents_body(place, own, above, below, total, token):
    for m in range(own.shape[0]):
        total[m] = own[m] + above[m].astype(f32) + below[m].astype(f32)
    token[...] = jnp.zeros_like(token)


def sum_body(place, kept, received, mine, sent):
    staying = mine.shape[0]
    for k in range(kept.shape[0]):
        total = kept[k] + received[k].astype(f32)
        if k < staying:
            mine[k] = total
        else:
            sent[k - staying] = total.astype(bf16)


def last_sum_body(place, kept, received, out):
    out[...] = (kept[0] + received[0].astype(f32)).astype(bf16)


def assemble_body(ens, spans, place, *refs):
    pieces, (hidden, out, joined) = refs[: ens * len(spans)], refs[ens * len(spans) :]
    rows, width = hidden.shape
    lanes = width // ens
    for at, (first, last) in enumerate(spans):
        height = last - first
        for k in range(ens):
            source = place[0] ^ k
            piece = pieces[at * ens + k][...].astype(f32)
            columns = pl.ds(pl.multiple_of(source * lanes, lanes), lanes)
            hidden[first:last, columns] = piece[:height]
            if first == 0:
                strip = 2 * (piece.shape[0] - height)
                start = pl.multiple_of(source * strip, strip)
                joined[pl.ds(start, strip // 2), :] = piece[height:, :rows]
                joined[pl.ds(start + strip // 2, strip // 2), :] = piece[height:, rows:]
    out[...] = joined[: out.shape[0]]


def reduced(aggregate_t, dpreact, out_part, variables, place, ens, chips, window):
    width = dpreact.shape[1]
    rows = width // (2 * chips)
    lanes = width // ens
    strip = 32 * pl.cdiv(out_part.shape[0], 32 * ens)
    aggregate_t = aggregate_t.reshape(chips, 2, rows, -1)
    spans = [(0, rows // 2), (rows // 2, rows)]
    blocks = [(last - first + (strip // 2 if first == 0 else 0), lanes) for first, last in spans]
    both = range(len(spans))

    def half(mine, kind):
        return [
            call(
                functools.partial(half_body, ens, chips, mine, spans[at]),
                [((ens, chips) + blocks[at], kind)],
                place, dpreact, out_part, aggregate_t, flops=dpreact.size * width // 2,
            )[0]
            for at in both
        ]

    received = [chip_swap(given) for given in half(False, bf16)]
    kept = half(True, f32)
    stages = [("ens", (1, 2), 2), ("ens", (2, 1), 1), ("chip", (1, 2), 2), ("chip", (2, 1), 1)]
    for stage, (axis, bits, staying) in enumerate(stages):
        for at in both:
            shape = (staying, chips) + blocks[at] if axis == "ens" else (staying,) + blocks[at]
            if stage == 2:
                kept[at], received[at] = kept[at][0], received[at][0]
            kept[at], given = call(
                sum_body, [(shape, f32), (shape, bf16)], place, kept[at], received[at],
                flops=10**9,
            )
            received[at] = core_swap(given, axis, bits)
        if stage == 0:
            latents_sum = window(*kept)
    every = []
    totals = []
    for at in both:
        total = call(
            last_sum_body, [(blocks[at], bf16)], place, kept[at], received[at], flops=10**9
        )[0]
        totals.append(total)
        every += [total] + [swap(total, "ens", k) for k in range(1, ens)]
    grad_latents, token = latents_sum(totals[0])
    hidden, out = call(
        functools.partial(assemble_body, ens, spans),
        [((rows, width), f32), ((variables, rows), f32)],
        place, *every, after=[token], last=True,
        scratch=[pltpu.VMEM((ens * strip, rows), f32)],
    )
    return grad_latents, hidden, out.T


def reduced_any(aggregate_t, dpreact, out_part, variables):
    part = mul(aggregate_t, dpreact)
    summed = lax.psum((part, out_part[:variables].T), "ens")
    return tuple(
        lax.psum_scatter(value, "space", scatter_dimension=0, tiled=True) for value in summed
    )


def shards(latents, edge_index, edge_weight, truth, w_hidden, output_weight):
    mem, nodes, width = latents.shape
    variables, grid = truth.shape
    ens, space = lax.axis_size("ens"), lax.axis_size("space")
    chips = space // 2
    members = mem * ens
    scale = 1.0 / math.sqrt(grid * space * members)
    e, s = lax.axis_index("ens"), lax.axis_index("space")
    place = jnp.stack([e, s // 2, s % 2]).astype(jnp.int32)
    chunk = grid // ens
    w_out_t = output_weight.T

    on_link = link_swap(latents)
    on_chip = chip_swap(latents)
    rows = 8 * pl.cdiv(variables, 8)
    adjacency, adjacency_t, w_hidden_t, own, w_hidden_here, w_out_here, truth_here = call(
        functools.partial(prepare_body, ens),
        [((grid, 3 * nodes), bf16), ((3 * nodes, grid), bf16), (w_hidden.shape[::-1], bf16)]
        + [(latents.shape, bf16), (w_hidden.shape, bf16)]
        + [((rows, width), bf16), ((rows, grid), f32)],
        place, edge_index.T, edge_weight.T, w_out_t, truth, far=[latents, w_hidden],
        scratch=[pltpu.SemaphoreType.DMA((2,))],
    )
    cells = (mem, grid, width)
    partial = call(partial_body, [(cells, f32)], place, own, on_chip, adjacency)[0]
    piece = (mem * rows, chunk)
    aggregate, preact, activated, *pieces = call(
        functools.partial(forward_body, ens),
        [(cells, bf16), (cells, f32), (cells, bf16)] + [(piece, f32)] * ens,
        place, partial, on_link, adjacency, w_hidden_here, w_out_here,
        flops=2 * mem * grid * width * (nodes + width + 128),
    )
    order = far_first(ens)
    here = [pieces[0]] + [swap(pieces[k], "ens", k) for k in order[1:]]
    slope = call(slope_body, [(cells, f32)], place, preact, after=pieces)[0]
    gradients = call(
        functools.partial(loss_body, ens, scale), [(piece, bf16)] * ens, place, truth_here, *here,
        after=[slope],
    )
    dforecast = [gradients[0]]
    dforecast += [swap(gradients[at], "ens", order[at]) for at in range(1, ens)]
    aggregate_t = call(
        turn_body, [((width, mem * grid), bf16)], place, aggregate, after=gradients
    )[0]
    dpreact, out_part = call(
        functools.partial(backward_body, ens),
        [((mem * grid, width), bf16), ((rows, width), f32)],
        place, w_out_here, slope, activated, *dforecast,
        flops=4 * mem * grid * width * 128,
    )
    band = (mem, nodes, width)

    def window(*before):
        on_chip, on_link, middle = call(
            window_body, [(band, bf16)] * 2 + [(band, f32)],
            place, dpreact, w_hidden_t, adjacency_t, after=before,
            flops=2 * mem * grid * width * (width + 3 * nodes),
        )
        on_chip, on_link = chip_swap(on_chip), link_swap(on_link)

        def total(*before):
            return call(
                latents_body, [(band, f32), ((8, 128), f32)], place, middle, on_chip, on_link,
                after=before, last=True,
            )

        return total

    if width % (space * 128) == 0 and width // ens == 2 * (width // space) and ens == chips == 4:
        return reduced(aggregate_t, dpreact, out_part, variables, place, ens, chips, window)
    return (window()()[0], *reduced_any(aggregate_t, dpreact, out_part, variables))


def solution(mesh):
    placed = (
        P("ens", "space", None),
        P("space", None),
        P("space", None),
        P(None, "space"),
        P(),
        P(),
    )
    return jax.shard_map(
        shards,
        mesh=mesh,
        in_specs=placed,
        out_specs=(P("ens", "space", None), P("space", None), P("space", None)),
        check_vma=False,
    )
```

```python
import functools
import math

import jax
import jax.numpy as jnp
from jax import lax
from jax.experimental import pallas as pl
from jax.experimental.pallas import tpu as pltpu
from jax.sharding import PartitionSpec as P

smoothing = 0.05
f32, bf16 = jnp.float32, jnp.bfloat16
across = (((1,), (0,)), ((), ()))
right_turned = (((1,), (1,)), ((), ()))
left_turned = (((0,), (0,)), ((), ()))


def chip_swap(value):
    count = lax.axis_size("space")
    return lax.ppermute(value, "space", [(i, i ^ 1) for i in range(count)])


def link_swap(value):
    count = lax.axis_size("space")
    pairs = [(i, i + 1) for i in range(1, count - 1, 2)]
    return lax.ppermute(value, "space", pairs + [(j, i) for i, j in pairs])


def core_swap(value, axis, bits):
    ens, space = lax.axis_size("ens"), lax.axis_size("space")

    def partner(e, s):
        bit = bits[s % 2]
        return (e ^ bit) * space + s if axis == "ens" else e * space + (s ^ (2 * bit))

    return lax.ppermute(
        value,
        ("ens", "space"),
        [(e * space + s, partner(e, s)) for e in range(ens) for s in range(space)],
    )


def routes(ens):
    if ens == 4:
        return [(0, 0), (1, 2), (2, 1), (3, 3)]
    return [(k, k) for k in range(ens)]


def exchanged(values):
    others = zip(values[1:], routes(len(values))[1:])
    return [values[0]] + [core_swap(value, "ens", bits) for value, bits in others]


def neighbour(place, bits):
    return place[0] ^ jnp.where(place[2] == 0, bits[0], bits[1])


def mul(a, b, dims=across):
    return lax.dot_general(a, b, dims, preferred_element_type=f32)


def call(body, outs, place, *operands, after=(), far=(), flops=0, last=False, scratch=()):
    vmem = pl.BlockSpec(memory_space=pltpu.VMEM)
    unread = pl.BlockSpec(memory_space=pl.ANY)

    def kernel(place_ref, *refs):
        body(place_ref, *refs[len(after) :])

    return pl.pallas_call(
        kernel,
        out_shape=[
            jax.ShapeDtypeStruct(shape, kind) if last else pltpu.VMEM(shape, kind)
            for shape, kind in outs
        ],
        in_specs=[pl.BlockSpec(memory_space=pltpu.SMEM)]
        + [unread] * len(after)
        + [pl.BlockSpec(memory_space=pltpu.HBM)] * len(far)
        + [vmem] * len(operands),
        out_specs=[vmem] * len(outs),
        scratch_shapes=scratch,
        cost_estimate=pl.CostEstimate(
            flops=flops,
            transcendentals=0,
            bytes_accessed=sum(x.size * x.dtype.itemsize for x in operands)
            + sum(math.prod(shape) * jnp.dtype(kind).itemsize for shape, kind in outs),
        ),
        compiler_params=pltpu.CompilerParams(vmem_limit_bytes=20 * 1024 * 1024),
    )(
        place,
        *after,
        *[pltpu.with_memory_space_constraint(x, pltpu.HBM) for x in far],
        *[pltpu.with_memory_space_constraint(x, pltpu.VMEM) for x in operands],
    )


def sides(core, nodes):
    above, below = 2 * nodes, 0
    return (
        pl.multiple_of(jnp.where(core == 0, above, below), nodes),
        pl.multiple_of(jnp.where(core == 0, below, above), nodes),
    )


def padded(value, rows):
    zeros = jnp.zeros((rows - value.shape[0], value.shape[1]), value.dtype)
    return jnp.concatenate([value, zeros], axis=0)


def prepare_body(
    ens, place, latents, w_hidden, index, weight, w_out_t, truth,
    adjacency, adjacency_t, w_hidden_t, own, w_hidden_here, w_out_here, truth_here, sems
):
    copies = [
        pltpu.make_async_copy(w_hidden, w_hidden_here, sems.at[0]),
        pltpu.make_async_copy(latents, own, sems.at[1]),
    ]
    for copy in copies:
        copy.start()
    edges, grid = index.shape
    chunk = grid // ens
    rows = adjacency_t.shape[0]
    row = lax.broadcasted_iota(jnp.int32, (rows, chunk), 0)
    for k, bits in enumerate(routes(ens)):
        lanes = pl.ds(pl.multiple_of(neighbour(place, bits) * chunk, chunk), chunk)
        nodes = index[:, lanes]
        weights = weight[:, lanes].astype(bf16).astype(f32)
        block = jnp.zeros((rows, chunk), f32)
        for j in range(edges):
            block += jnp.where(nodes[j : j + 1] == row, weights[j : j + 1], 0.0)
        adjacency_t[:, k * chunk : (k + 1) * chunk] = block.astype(bf16)
        adjacency[k * chunk : (k + 1) * chunk, :] = block.T.astype(bf16)
    w_out_here[...] = padded(w_out_t[...].astype(f32), w_out_here.shape[0]).astype(bf16)
    truth_here[...] = padded(truth[...], truth_here.shape[0])
    for copy in copies:
        copy.wait()
    w_hidden_t[...] = w_hidden_here[...].T


def partial_body(place, own, on_chip, adjacency, partial):
    mem, nodes, _ = own.shape
    first, _ = sides(place[2], nodes)
    for m in range(mem):
        total = mul(adjacency[:, nodes : 2 * nodes], own[m])
        partial[m] = total + mul(adjacency[:, pl.ds(first, nodes)], on_chip[m])


def forward_body(
    ens, place, partial, on_link, adjacency, w_hidden, w_out_t, aggregate, preact, activated, *pieces
):
    mem, nodes, width = on_link.shape
    variables = w_out_t.shape[0]
    grid = adjacency.shape[0]
    chunk = grid // ens
    step = 256
    _, second = sides(place[2], nodes)
    for m in range(mem):
        total = partial[m] + mul(adjacency[:, pl.ds(second, nodes)], on_link[m])
        gathered = total.astype(bf16)
        aggregate[m] = gathered
        forecast = jnp.zeros((grid, variables), f32)
        for at in range(0, width, step):
            value = mul(gathered, w_hidden[:, at : at + step])
            preact[m, :, at : at + step] = value
            silu = (value / (1.0 + jnp.exp(-value))).astype(bf16)
            activated[m, :, at : at + step] = silu
            forecast += mul(silu, w_out_t[:, at : at + step], right_turned)
        turned = forecast.T
        for k in range(ens):
            rows = slice(m * variables, (m + 1) * variables)
            pieces[k][rows] = turned[:, k * chunk : (k + 1) * chunk]


def slope_body(place, preact, slope):
    for m in range(preact.shape[0]):
        value = preact[m]
        logistic = 1.0 / (1.0 + jnp.exp(-value))
        slope[m] = logistic * (1.0 + value * (1.0 - logistic))


def turn_body(place, aggregate, aggregate_t):
    mem, grid, _ = aggregate.shape
    for m in range(mem):
        aggregate_t[:, m * grid : (m + 1) * grid] = aggregate[m].T


def loss_body(ens, scale, place, truth, *refs):
    here, out = refs[:ens], refs[ens:]
    rows, chunk = here[0].shape
    mem = rows // truth.shape[0]
    members = mem * ens
    variables = truth.shape[0]
    target = truth[:, pl.ds(pl.multiple_of(place[0] * chunk, chunk), chunk)]
    forecasts = [
        here[k][m * variables : (m + 1) * variables] for k in range(ens) for m in range(mem)
    ]

    def ratio(d):
        return d * lax.rsqrt(d * d + smoothing * smoothing)

    spread = [jnp.zeros_like(target) for _ in forecasts]
    for i in range(members):
        for j in range(i + 1, members):
            term = ratio(forecasts[i] - forecasts[j])
            spread[i] += term
            spread[j] -= term
    gradients = [
        scale
        * (
            ratio(forecasts[i] - target) * (1.0 / members)
            - spread[i] * (1.0 / (members * (members - 1)))
        )
        for i in range(members)
    ]
    for k in range(ens):
        total = jnp.concatenate(gradients[k * mem : (k + 1) * mem], axis=0)
        out[k][...] = total.astype(bf16)


def backward_body(ens, place, w_out_t, slope, activated, *refs):
    dforecast, (dpreact, out_part) = refs[:ens], refs[ens:]
    mem, grid, _ = slope.shape
    variables = w_out_t.shape[0]
    gradients = jnp.concatenate([piece[...] for piece in dforecast], axis=1)
    gradients = gradients.astype(f32)
    out_total = None
    for m in range(mem):
        gradient = gradients[m * variables : (m + 1) * variables].astype(bf16)
        dactivated = mul(gradient, w_out_t[...], left_turned)
        dpreact[m * grid : (m + 1) * grid] = (dactivated * slope[m]).astype(bf16)
        part = mul(gradient, activated[m])
        out_total = part if out_total is None else out_total + part
    out_part[...] = out_total


def slot_of(core, k):
    return jnp.where(k == 1 + core, 2, jnp.where(k == 2 - core, 1, k))


def gradient_blocks(ens, chips, core, spans, place, dpreact, out_part, aggregate_t, joined, emit):
    e, chip = place[0], place[1]
    rows = aggregate_t.shape[2]
    lanes = dpreact.shape[1] // ens
    first, last = spans[0][0], spans[-1][1]
    strip = joined.shape[1] // ens
    half = strip // 2
    end = spans[0][1]
    if first == 0:
        for z in range(chips):
            columns = pl.ds(pl.multiple_of((2 * z + core) * rows, rows), rows)
            joined[z] = padded(out_part[:, columns], ens * strip)
    left = aggregate_t[:, core, first:last].reshape(chips * (last - first), -1)
    for slot, k in ((0, 0), (1, 2 - core), (2, 1 + core), (3, 3)):
        source = e ^ k
        columns = pl.ds(pl.multiple_of(source * lanes, lanes), lanes)
        block = mul(left, dpreact[:, columns])
        start = pl.multiple_of(source * strip, strip)
        for z in range(chips):
            to = slot_of(core, z ^ chip)
            base = z * (last - first) - first
            for at, (a, b) in enumerate(spans):
                emit(at, slot, to, slice(0, b - a), slice(0, lanes), block[base + a : base + b])
            if first == 0:
                upper = joined[z, pl.ds(start, half)]
                lower = joined[z, pl.ds(start + half, half)]
                emit(0, slot, to, slice(end, end + half), slice(0, rows), upper)
                emit(0, slot, to, slice(end, end + half), slice(rows, lanes), lower)


def half_body(ens, chips, spans, place, dpreact, out_part, aggregate_t, *refs):
    outs, joined = refs[:-1], refs[-1]

    def emit(at, slot, to, rows, lanes, value):
        outs[at][slot, to, rows, lanes] = value.astype(bf16)

    core = 1 - place[2]
    gradient_blocks(ens, chips, core, spans, place, dpreact, out_part, aggregate_t, joined, emit)


def chip_sum_body(
    ens, chips, span, place, dpreact, out_part, aggregate_t, received, mine, sent, joined
):
    staying = mine.shape[0]

    def emit(at, slot, to, rows, lanes, value):
        total = value + received[slot, to, rows, lanes].astype(f32)
        if slot < staying:
            mine[slot, to, rows, lanes] = total
        else:
            sent[slot - staying, to, rows, lanes] = total.astype(bf16)

    core = place[2]
    gradient_blocks(ens, chips, core, [span], place, dpreact, out_part, aggregate_t, joined, emit)


def link_window_body(place, dpreact, w_hidden_t, adjacency_t, on_link, daggregate):
    mem, nodes, _ = on_link.shape
    grid = adjacency_t.shape[1]
    _, second = sides(place[2], nodes)
    for m in range(mem):
        total = mul(dpreact[m * grid : (m + 1) * grid], w_hidden_t[...]).astype(bf16)
        daggregate[m] = total
        on_link[m] = mul(adjacency_t[pl.ds(second, nodes)], total).astype(bf16)


def near_window_body(place, daggregate, adjacency_t, on_chip, own):
    mem, nodes, _ = own.shape
    first, _ = sides(place[2], nodes)
    for m in range(mem):
        on_chip[m] = mul(adjacency_t[pl.ds(first, nodes)], daggregate[m]).astype(bf16)
        own[m] = mul(adjacency_t[nodes : 2 * nodes], daggregate[m])


def latents_body(place, own, above, below, total, token):
    for m in range(own.shape[0]):
        total[m] = own[m] + above[m].astype(f32) + below[m].astype(f32)
    token[...] = jnp.zeros_like(token)


def sum_body(place, kept, received, mine, sent):
    staying = mine.shape[0]
    for k in range(kept.shape[0]):
        total = kept[k] + received[k].astype(f32)
        if k < staying:
            mine[k] = total
        else:
            sent[k - staying] = total.astype(bf16)


def last_sum_body(place, kept, received, out):
    out[...] = (kept[0] + received[0].astype(f32)).astype(bf16)


def assemble_body(ens, spans, place, *refs):
    pieces, (hidden, out, joined) = refs[: ens * len(spans)], refs[ens * len(spans) :]
    rows, width = hidden.shape
    lanes = width // ens
    for at, (first, last) in enumerate(spans):
        height = last - first
        for k, bits in enumerate(routes(ens)):
            source = neighbour(place, bits)
            piece = pieces[at * ens + k][...].astype(f32)
            columns = pl.ds(pl.multiple_of(source * lanes, lanes), lanes)
            hidden[first:last, columns] = piece[:height]
            if first == 0:
                strip = 2 * (piece.shape[0] - height)
                start = pl.multiple_of(source * strip, strip)
                joined[pl.ds(start, strip // 2), :] = piece[height:, :rows]
                joined[pl.ds(start + strip // 2, strip // 2), :] = piece[height:, rows:]
    out[...] = joined[: out.shape[0]]


def reduced(aggregate_t, dpreact, out_part, variables, place, ens, chips, link_window, near_window):
    width = dpreact.shape[1]
    rows = width // (2 * chips)
    lanes = width // ens
    strip = 32 * pl.cdiv(out_part.shape[0], 32 * ens)
    joined = pltpu.VMEM((chips, ens * strip, rows), f32)
    aggregate_t = aggregate_t.reshape(chips, 2, rows, -1)
    spans = [(0, rows // 2), (rows // 2, rows)]
    blocks = [(last - first + (strip // 2 if first == 0 else 0), lanes) for first, last in spans]
    both = range(len(spans))
    flops = dpreact.size * width

    given = call(
        functools.partial(half_body, ens, chips, spans),
        [((ens, chips) + block, bf16) for block in blocks],
        place, dpreact, out_part, aggregate_t, flops=flops, scratch=[joined],
    )
    received = [chip_swap(value) for value in given]
    on_link, daggregate = link_window(*given)
    kept, sent = [None, None], [None, None]
    for at in both:
        shape = (2, chips) + blocks[at]
        kept[at], sent[at] = call(
            functools.partial(chip_sum_body, ens, chips, spans[at]),
            [(shape, f32), (shape, bf16)],
            place, dpreact, out_part, aggregate_t, received[at], after=[on_link],
            flops=flops // 2, scratch=[joined],
        )
        received[at] = core_swap(sent[at], "ens", (1, 2))
    latents_sum = near_window(on_link, daggregate, *kept)
    stages = [("ens", (2, 1), (1, chips)), ("chip", (1, 2), (2,)), ("chip", (2, 1), (1,))]
    for axis, bits, slots in stages:
        for at in both:
            shape = slots + blocks[at]
            if slots == (2,):
                kept[at], received[at] = kept[at][0], received[at][0]
            kept[at], given = call(
                sum_body, [(shape, f32), (shape, bf16)], place, kept[at], received[at],
                flops=10**9,
            )
            received[at] = core_swap(given, axis, bits)
    every, totals = [], []
    for at in both:
        total = call(
            last_sum_body, [(blocks[at], bf16)], place, kept[at], received[at], flops=10**9
        )[0]
        totals.append(total)
        every += exchanged([total] * ens)
    grad_latents, token = latents_sum(totals[0])
    hidden, out = call(
        functools.partial(assemble_body, ens, spans),
        [((rows, width), f32), ((variables, rows), f32)],
        place, *every, after=[token], last=True,
        scratch=[pltpu.VMEM((ens * strip, rows), f32)],
    )
    return grad_latents, hidden, out.T


def reduced_any(aggregate_t, dpreact, out_part, variables):
    part = mul(aggregate_t, dpreact)
    summed = lax.psum((part, out_part[:variables].T), "ens")
    return tuple(
        lax.psum_scatter(value, "space", scatter_dimension=0, tiled=True) for value in summed
    )


def shards(latents, edge_index, edge_weight, truth, w_hidden, output_weight):
    mem, nodes, width = latents.shape
    variables, grid = truth.shape
    ens, space = lax.axis_size("ens"), lax.axis_size("space")
    chips = space // 2
    members = mem * ens
    scale = 1.0 / math.sqrt(grid * space * members)
    e, s = lax.axis_index("ens"), lax.axis_index("space")
    place = jnp.stack([e, s // 2, s % 2]).astype(jnp.int32)
    chunk = grid // ens
    w_out_t = output_weight.T

    on_link = link_swap(latents)
    on_chip = chip_swap(latents)
    rows = 8 * pl.cdiv(variables, 8)
    adjacency, adjacency_t, w_hidden_t, own, w_hidden_here, w_out_here, truth_here = call(
        functools.partial(prepare_body, ens),
        [((grid, 3 * nodes), bf16), ((3 * nodes, grid), bf16), (w_hidden.shape[::-1], bf16)]
        + [(latents.shape, bf16), (w_hidden.shape, bf16)]
        + [((rows, width), bf16), ((rows, grid), f32)],
        place, edge_index.T, edge_weight.T, w_out_t, truth, far=[latents, w_hidden],
        scratch=[pltpu.SemaphoreType.DMA((2,))],
    )
    cells = (mem, grid, width)
    partial = call(partial_body, [(cells, f32)], place, own, on_chip, adjacency)[0]
    piece = (mem * rows, chunk)
    aggregate, preact, activated, *pieces = call(
        functools.partial(forward_body, ens),
        [(cells, bf16), (cells, f32), (cells, bf16)] + [(piece, f32)] * ens,
        place, partial, on_link, adjacency, w_hidden_here, w_out_here,
        flops=2 * mem * grid * width * (nodes + width + 128),
    )
    here = exchanged(pieces)
    slope = call(slope_body, [(cells, f32)], place, preact, after=pieces)[0]
    gradients = call(
        functools.partial(loss_body, ens, scale), [(piece, bf16)] * ens, place, truth_here, *here,
        after=[slope],
    )
    dforecast = exchanged(gradients)
    aggregate_t = call(
        turn_body, [((width, mem * grid), bf16)], place, aggregate, after=gradients
    )[0]
    dpreact, out_part = call(
        functools.partial(backward_body, ens),
        [((mem * grid, width), bf16), ((rows, width), f32)],
        place, w_out_here, slope, activated, *dforecast,
        flops=4 * mem * grid * width * 128,
    )
    band = (mem, nodes, width)

    def link_window(*before):
        return call(
            link_window_body, [(band, bf16), (cells, bf16)], place, dpreact, w_hidden_t,
            adjacency_t, after=before, flops=2 * mem * grid * width * (width + nodes),
        )

    def near_window(on_link, daggregate, *before):
        on_link = link_swap(on_link)
        on_chip, middle = call(
            near_window_body, [(band, bf16), (band, f32)], place, daggregate, adjacency_t,
            after=before, flops=4 * mem * grid * width * nodes,
        )
        on_chip = chip_swap(on_chip)

        def total(*before):
            return call(
                latents_body, [(band, f32), ((8, 128), f32)], place, middle, on_chip, on_link,
                after=before, last=True,
            )

        return total

    if width % (space * 128) == 0 and width // ens == 2 * (width // space) and ens == chips == 4:
        return reduced(
            aggregate_t, dpreact, out_part, variables, place, ens, chips, link_window, near_window
        )
    grad_latents = near_window(*link_window())()[0]
    return (grad_latents, *reduced_any(aggregate_t, dpreact, out_part, variables))


def solution(mesh):
    placed = (
        P("ens", "space", None),
        P("space", None),
        P("space", None),
        P(None, "space"),
        P(),
        P(),
    )
    return jax.shard_map(
        shards,
        mesh=mesh,
        in_specs=placed,
        out_specs=(P("ens", "space", None), P("space", None), P("space", None)),
        check_vma=False,
    )
```

```python
import functools
import math

import jax
import jax.numpy as jnp
from jax import lax
from jax.experimental import pallas as pl
from jax.experimental.pallas import tpu as pltpu
from jax.sharding import PartitionSpec as P

smoothing = 0.05
f32, bf16 = jnp.float32, jnp.bfloat16
across = (((1,), (0,)), ((), ()))
right_turned = (((1,), (1,)), ((), ()))
left_turned = (((0,), (0,)), ((), ()))


def chip_swap(value):
    count = lax.axis_size("space")
    return lax.ppermute(value, "space", [(i, i ^ 1) for i in range(count)])


def link_swap(value):
    count = lax.axis_size("space")
    pairs = [(i, i + 1) for i in range(1, count - 1, 2)]
    return lax.ppermute(value, "space", pairs + [(j, i) for i, j in pairs])


def core_swap(value, axis, bits):
    ens, space = lax.axis_size("ens"), lax.axis_size("space")

    def partner(e, s):
        bit = bits[s % 2]
        return (e ^ bit) * space + s if axis == "ens" else e * space + (s ^ (2 * bit))

    return lax.ppermute(
        value,
        ("ens", "space"),
        [(e * space + s, partner(e, s)) for e in range(ens) for s in range(space)],
    )


def routes(ens):
    if ens == 4:
        return [(0, 0), (1, 2), (2, 1), (3, 3)]
    return [(k, k) for k in range(ens)]


def exchanged(values):
    others = zip(values[1:], routes(len(values))[1:])
    return [values[0]] + [core_swap(value, "ens", bits) for value, bits in others]


def neighbour(place, bits):
    return place[0] ^ jnp.where(place[2] == 0, bits[0], bits[1])


def mul(a, b, dims=across):
    return lax.dot_general(a, b, dims, preferred_element_type=f32)


def call(body, outs, place, *operands, after=(), far=(), flops=0, last=False, scratch=()):
    vmem = pl.BlockSpec(memory_space=pltpu.VMEM)
    unread = pl.BlockSpec(memory_space=pl.ANY)

    def kernel(place_ref, *refs):
        body(place_ref, *refs[len(after) :])

    return pl.pallas_call(
        kernel,
        out_shape=[
            jax.ShapeDtypeStruct(shape, kind) if last else pltpu.VMEM(shape, kind)
            for shape, kind in outs
        ],
        in_specs=[pl.BlockSpec(memory_space=pltpu.SMEM)]
        + [unread] * len(after)
        + [pl.BlockSpec(memory_space=pltpu.HBM)] * len(far)
        + [vmem] * len(operands),
        out_specs=[vmem] * len(outs),
        scratch_shapes=scratch,
        cost_estimate=pl.CostEstimate(
            flops=flops,
            transcendentals=0,
            bytes_accessed=sum(x.size * x.dtype.itemsize for x in operands)
            + sum(math.prod(shape) * jnp.dtype(kind).itemsize for shape, kind in outs),
        ),
        compiler_params=pltpu.CompilerParams(vmem_limit_bytes=20 * 1024 * 1024),
    )(
        place,
        *after,
        *[pltpu.with_memory_space_constraint(x, pltpu.HBM) for x in far],
        *[pltpu.with_memory_space_constraint(x, pltpu.VMEM) for x in operands],
    )


def sides(core, nodes):
    above, below = 2 * nodes, 0
    return (
        pl.multiple_of(jnp.where(core == 0, above, below), nodes),
        pl.multiple_of(jnp.where(core == 0, below, above), nodes),
    )


def padded(value, rows):
    zeros = jnp.zeros((rows - value.shape[0], value.shape[1]), value.dtype)
    return jnp.concatenate([value, zeros], axis=0)


def prepare_body(
    ens, place, latents, w_hidden, index, weight, w_out_t, truth,
    adjacency, adjacency_t, w_hidden_t, own, w_hidden_here, w_out_here, truth_here, sems
):
    copies = [
        pltpu.make_async_copy(w_hidden, w_hidden_here, sems.at[0]),
        pltpu.make_async_copy(latents, own, sems.at[1]),
    ]
    for copy in copies:
        copy.start()
    edges, grid = index.shape
    chunk = grid // ens
    rows = adjacency_t.shape[0]
    row = lax.broadcasted_iota(jnp.int32, (rows, chunk), 0)
    for k, bits in enumerate(routes(ens)):
        lanes = pl.ds(pl.multiple_of(neighbour(place, bits) * chunk, chunk), chunk)
        nodes = index[:, lanes]
        weights = weight[:, lanes].astype(bf16).astype(f32)
        block = jnp.zeros((rows, chunk), f32)
        for j in range(edges):
            block += jnp.where(nodes[j : j + 1] == row, weights[j : j + 1], 0.0)
        adjacency_t[:, k * chunk : (k + 1) * chunk] = block.astype(bf16)
        adjacency[k * chunk : (k + 1) * chunk, :] = block.T.astype(bf16)
    w_out_here[...] = padded(w_out_t[...].astype(f32), w_out_here.shape[0]).astype(bf16)
    truth_here[...] = padded(truth[...], truth_here.shape[0])
    for copy in copies:
        copy.wait()
    w_hidden_t[...] = w_hidden_here[...].T


def partial_body(place, own, on_chip, adjacency, partial):
    mem, nodes, _ = own.shape
    first, _ = sides(place[2], nodes)
    for m in range(mem):
        total = mul(adjacency[:, nodes : 2 * nodes], own[m])
        partial[m] = total + mul(adjacency[:, pl.ds(first, nodes)], on_chip[m])


def forward_body(
    ens, place, partial, on_link, adjacency, w_hidden, w_out_t, aggregate, preact, activated, *pieces
):
    mem, nodes, width = on_link.shape
    variables = w_out_t.shape[0]
    grid = adjacency.shape[0]
    chunk = grid // ens
    step = 256
    _, second = sides(place[2], nodes)
    for m in range(mem):
        total = partial[m] + mul(adjacency[:, pl.ds(second, nodes)], on_link[m])
        gathered = total.astype(bf16)
        aggregate[m] = gathered
        forecast = jnp.zeros((grid, variables), f32)
        for at in range(0, width, step):
            value = mul(gathered, w_hidden[:, at : at + step])
            preact[m, :, at : at + step] = value
            silu = (value / (1.0 + jnp.exp(-value))).astype(bf16)
            activated[m, :, at : at + step] = silu
            forecast += mul(silu, w_out_t[:, at : at + step], right_turned)
        turned = forecast.T
        for k in range(ens):
            rows = slice(m * variables, (m + 1) * variables)
            pieces[k][rows] = turned[:, k * chunk : (k + 1) * chunk]


def slope_body(place, preact, slope):
    for m in range(preact.shape[0]):
        value = preact[m]
        logistic = 1.0 / (1.0 + jnp.exp(-value))
        slope[m] = logistic * (1.0 + value * (1.0 - logistic))


def turn_body(place, aggregate, aggregate_t):
    mem, grid, _ = aggregate.shape
    for m in range(mem):
        aggregate_t[:, m * grid : (m + 1) * grid] = aggregate[m].T


def loss_body(ens, scale, place, truth, *refs):
    here, out = refs[:ens], refs[ens:]
    rows, chunk = here[0].shape
    mem = rows // truth.shape[0]
    members = mem * ens
    variables = truth.shape[0]
    target = truth[:, pl.ds(pl.multiple_of(place[0] * chunk, chunk), chunk)]
    forecasts = [
        here[k][m * variables : (m + 1) * variables] for k in range(ens) for m in range(mem)
    ]

    def ratio(d):
        return d * lax.rsqrt(d * d + smoothing * smoothing)

    spread = [jnp.zeros_like(target) for _ in forecasts]
    for i in range(members):
        for j in range(i + 1, members):
            term = ratio(forecasts[i] - forecasts[j])
            spread[i] += term
            spread[j] -= term
    gradients = [
        scale
        * (
            ratio(forecasts[i] - target) * (1.0 / members)
            - spread[i] * (1.0 / (members * (members - 1)))
        )
        for i in range(members)
    ]
    for k in range(ens):
        total = jnp.concatenate(gradients[k * mem : (k + 1) * mem], axis=0)
        out[k][...] = total.astype(bf16)


def backward_body(ens, place, w_out_t, slope, activated, *refs):
    dforecast, (dpreact, out_part) = refs[:ens], refs[ens:]
    mem, grid, _ = slope.shape
    variables = w_out_t.shape[0]
    gradients = jnp.concatenate([piece[...] for piece in dforecast], axis=1)
    gradients = gradients.astype(f32)
    out_total = None
    for m in range(mem):
        gradient = gradients[m * variables : (m + 1) * variables].astype(bf16)
        dactivated = mul(gradient, w_out_t[...], left_turned)
        dpreact[m * grid : (m + 1) * grid] = (dactivated * slope[m]).astype(bf16)
        part = mul(gradient, activated[m])
        out_total = part if out_total is None else out_total + part
    out_part[...] = out_total


def slot_of(core, k):
    return jnp.where(k == 1 + core, 2, jnp.where(k == 2 - core, 1, k))


def half_body(ens, chips, mine, place, dpreact, out_part, aggregate_t, half):
    e, chip, core = place[0], place[1], place[2]
    core = core if mine else 1 - core
    rows = aggregate_t.shape[2]
    lanes = dpreact.shape[1] // ens
    strip = 2 * (half.shape[2] - rows)
    for z in range(chips):
        columns = pl.ds(pl.multiple_of((2 * z + core) * rows, rows), rows)
        part = padded(out_part[:, columns], ens * strip).astype(half.dtype)
        for j in range(ens):
            slot = slot_of(core, j ^ e)
            half[slot, z ^ chip, rows:, :rows] = part[j * strip : j * strip + strip // 2]
            half[slot, z ^ chip, rows:, rows:] = part[j * strip + strip // 2 : (j + 1) * strip]
    left = aggregate_t[:, core].reshape(chips * rows, -1)
    for slot, k in ((0, 0), (1, 2 - core), (2, 1 + core), (3, 3)):
        columns = pl.ds(pl.multiple_of((e ^ k) * lanes, lanes), lanes)
        block = mul(left, dpreact[:, columns]).astype(half.dtype)
        for z in range(chips):
            half[slot, z ^ chip, :rows] = block[z * rows : (z + 1) * rows]


def window_body(place, dpreact, w_hidden_t, adjacency_t, on_link, on_chip, own):
    mem, nodes, _ = own.shape
    grid = adjacency_t.shape[1]
    first, second = sides(place[2], nodes)
    for m in range(mem):
        total = mul(dpreact[m * grid : (m + 1) * grid], w_hidden_t[...]).astype(bf16)
        on_link[m] = mul(adjacency_t[pl.ds(second, nodes)], total).astype(bf16)
        on_chip[m] = mul(adjacency_t[pl.ds(first, nodes)], total).astype(bf16)
        own[m] = mul(adjacency_t[nodes : 2 * nodes], total)


def latents_body(place, own, on_chip, on_link, total, token):
    for m in range(own.shape[0]):
        total[m] = own[m] + on_chip[m].astype(f32) + on_link[m].astype(f32)
    token[...] = jnp.zeros_like(token)


def sum_body(place, kept, received, mine, sent):
    staying = mine.shape[0]
    for k in range(kept.shape[0]):
        total = kept[k] + received[k].astype(f32)
        if k < staying:
            mine[k] = total
        else:
            sent[k - staying] = total.astype(bf16)


def chip_slots_body(place, kept, received, mine, *sent):
    count = kept.shape[1]
    for q in range(count):
        total = kept[0, q] + received[0, q].astype(f32)
        if q == 0:
            mine[...] = total
        else:
            sent[count - 1 - q][...] = total.astype(bf16)


def chip_sum_body(place, kept, *refs):
    received, out = refs[:-1], refs[-1]
    total = kept[...]
    for block in received:
        total += block[...].astype(f32)
    out[...] = total.astype(bf16)


def assemble_body(ens, place, *refs):
    pieces, (hidden, out, joined) = refs[:ens], refs[ens:]
    rows, width = hidden.shape
    lanes = width // ens
    strip = 2 * (pieces[0].shape[0] - rows)
    for k, bits in enumerate(routes(ens)):
        source = neighbour(place, bits)
        piece = pieces[k][...].astype(f32)
        hidden[:, pl.ds(pl.multiple_of(source * lanes, lanes), lanes)] = piece[:rows]
        start = pl.multiple_of(source * strip, strip)
        joined[pl.ds(start, strip // 2), :] = piece[rows:, :rows]
        joined[pl.ds(start + strip // 2, strip // 2), :] = piece[rows:, rows:]
    out[...] = joined[: out.shape[0]]


def reduced(aggregate_t, dpreact, out_part, variables, place, ens, chips, window):
    width = dpreact.shape[1]
    rows = width // (2 * chips)
    lanes = width // ens
    strip = 32 * pl.cdiv(out_part.shape[0], 32 * ens)
    aggregate_t = aggregate_t.reshape(chips, 2, rows, -1)
    block = (rows + strip // 2, lanes)

    def half(mine, kind):
        return call(
            functools.partial(half_body, ens, chips, mine), [((ens, chips) + block, kind)],
            place, dpreact, out_part, aggregate_t, flops=dpreact.size * width,
        )[0]

    received = chip_swap(half(False, bf16))
    kept = half(True, f32)
    for staying, bits in ((2, (1, 2)), (1, (2, 1))):
        shape = (staying, chips) + block
        kept, given = call(sum_body, [(shape, f32), (shape, bf16)], place, kept, received)
        received = core_swap(given, "ens", bits)
        if staying == 2:
            latents_sum = window(kept)
    kept, *given = call(
        chip_slots_body, [(block, f32)] + [(block, bf16)] * (chips - 1), place, kept, received,
        flops=10**9,
    )
    received = [core_swap(given[chips - 1 - q], "chip", (q, q)) for q in range(chips - 1, 0, -1)]
    total = call(chip_sum_body, [(block, bf16)], place, kept, *received, flops=10**9)[0]
    every = exchanged([total] * ens)
    grad_latents, token = latents_sum(total)
    hidden, out = call(
        functools.partial(assemble_body, ens), [((rows, width), f32), ((variables, rows), f32)],
        place, *every, after=[token], last=True, scratch=[pltpu.VMEM((ens * strip, rows), f32)],
    )
    return grad_latents, hidden, out.T


def reduced_any(aggregate_t, dpreact, out_part, variables):
    part = mul(aggregate_t, dpreact)
    summed = lax.psum((part, out_part[:variables].T), "ens")
    return tuple(
        lax.psum_scatter(value, "space", scatter_dimension=0, tiled=True) for value in summed
    )


def shards(latents, edge_index, edge_weight, truth, w_hidden, output_weight):
    mem, nodes, width = latents.shape
    variables, grid = truth.shape
    ens, space = lax.axis_size("ens"), lax.axis_size("space")
    chips = space // 2
    members = mem * ens
    scale = 1.0 / math.sqrt(grid * space * members)
    e, s = lax.axis_index("ens"), lax.axis_index("space")
    place = jnp.stack([e, s // 2, s % 2]).astype(jnp.int32)
    chunk = grid // ens
    w_out_t = output_weight.T

    on_link = link_swap(latents)
    on_chip = chip_swap(latents)
    rows = 8 * pl.cdiv(variables, 8)
    adjacency, adjacency_t, w_hidden_t, own, w_hidden_here, w_out_here, truth_here = call(
        functools.partial(prepare_body, ens),
        [((grid, 3 * nodes), bf16), ((3 * nodes, grid), bf16), (w_hidden.shape[::-1], bf16)]
        + [(latents.shape, bf16), (w_hidden.shape, bf16)]
        + [((rows, width), bf16), ((rows, grid), f32)],
        place, edge_index.T, edge_weight.T, w_out_t, truth, far=[latents, w_hidden],
        scratch=[pltpu.SemaphoreType.DMA((2,))],
    )
    cells = (mem, grid, width)
    partial = call(partial_body, [(cells, f32)], place, own, on_chip, adjacency)[0]
    piece = (mem * rows, chunk)
    aggregate, preact, activated, *pieces = call(
        functools.partial(forward_body, ens),
        [(cells, bf16), (cells, f32), (cells, bf16)] + [(piece, f32)] * ens,
        place, partial, on_link, adjacency, w_hidden_here, w_out_here,
        flops=2 * mem * grid * width * (nodes + width + 128),
    )
    here = exchanged(pieces)
    slope = call(slope_body, [(cells, f32)], place, preact, after=pieces)[0]
    gradients = call(
        functools.partial(loss_body, ens, scale), [(piece, bf16)] * ens, place, truth_here, *here,
        after=[slope],
    )
    dforecast = exchanged(gradients)
    aggregate_t = call(
        turn_body, [((width, mem * grid), bf16)], place, aggregate, after=gradients
    )[0]
    dpreact, out_part = call(
        functools.partial(backward_body, ens),
        [((mem * grid, width), bf16), ((rows, width), f32)],
        place, w_out_here, slope, activated, *dforecast,
        flops=4 * mem * grid * width * 128,
    )
    band = (mem, nodes, width)

    def window(*before):
        on_link, on_chip, middle = call(
            window_body, [(band, bf16)] * 2 + [(band, f32)],
            place, dpreact, w_hidden_t, adjacency_t, after=before,
            flops=2 * mem * grid * width * (width + 3 * nodes),
        )
        on_link, on_chip = link_swap(on_link), chip_swap(on_chip)

        def total(*before):
            return call(
                latents_body, [(band, f32), ((8, 128), f32)], place, middle, on_chip, on_link,
                after=before, last=True,
            )

        return total

    if width % (space * 128) == 0 and width // ens == 2 * (width // space) and ens == 4:
        return reduced(aggregate_t, dpreact, out_part, variables, place, ens, chips, window)
    return (window()()[0], *reduced_any(aggregate_t, dpreact, out_part, variables))


def solution(mesh):
    placed = (
        P("ens", "space", None),
        P("space", None),
        P("space", None),
        P(None, "space"),
        P(),
        P(),
    )
    return jax.shard_map(
        shards,
        mesh=mesh,
        in_specs=placed,
        out_specs=(P("ens", "space", None), P("space", None), P("space", None)),
        check_vma=False,
    )
```

```python
import functools
import math

import jax
import jax.numpy as jnp
from jax import lax
from jax.experimental import pallas as pl
from jax.experimental.pallas import tpu as pltpu
from jax.sharding import PartitionSpec as P

smoothing = 0.05
f32, bf16 = jnp.float32, jnp.bfloat16
across = (((1,), (0,)), ((), ()))
right_turned = (((1,), (1,)), ((), ()))
left_turned = (((0,), (0,)), ((), ()))


def chip_swap(value):
    count = lax.axis_size("space")
    return lax.ppermute(value, "space", [(i, i ^ 1) for i in range(count)])


def link_swap(value):
    count = lax.axis_size("space")
    pairs = [(i, i + 1) for i in range(1, count - 1, 2)]
    return lax.ppermute(value, "space", pairs + [(j, i) for i, j in pairs])


def core_swap(value, axis, bits):
    ens, space = lax.axis_size("ens"), lax.axis_size("space")

    def partner(e, s):
        bit = bits[s % 2]
        return (e ^ bit) * space + s if axis == "ens" else e * space + (s ^ (2 * bit))

    return lax.ppermute(
        value,
        ("ens", "space"),
        [(e * space + s, partner(e, s)) for e in range(ens) for s in range(space)],
    )


def routes(ens):
    if ens == 4:
        return [(0, 0), (1, 2), (2, 1), (3, 3)]
    return [(k, k) for k in range(ens)]


def exchanged(values):
    others = zip(values[1:], routes(len(values))[1:])
    return [values[0]] + [core_swap(value, "ens", bits) for value, bits in others]


def neighbour(place, bits):
    return place[0] ^ jnp.where(place[2] == 0, bits[0], bits[1])


def mul(a, b, dims=across):
    return lax.dot_general(a, b, dims, preferred_element_type=f32)


def call(body, outs, place, *operands, after=(), far=(), flops=0, last=False, scratch=()):
    vmem = pl.BlockSpec(memory_space=pltpu.VMEM)
    unread = pl.BlockSpec(memory_space=pl.ANY)

    def kernel(place_ref, *refs):
        body(place_ref, *refs[len(after) :])

    return pl.pallas_call(
        kernel,
        out_shape=[
            jax.ShapeDtypeStruct(shape, kind) if last else pltpu.VMEM(shape, kind)
            for shape, kind in outs
        ],
        in_specs=[pl.BlockSpec(memory_space=pltpu.SMEM)]
        + [unread] * len(after)
        + [pl.BlockSpec(memory_space=pltpu.HBM)] * len(far)
        + [vmem] * len(operands),
        out_specs=[vmem] * len(outs),
        scratch_shapes=scratch,
        cost_estimate=pl.CostEstimate(
            flops=flops,
            transcendentals=0,
            bytes_accessed=sum(x.size * x.dtype.itemsize for x in operands)
            + sum(math.prod(shape) * jnp.dtype(kind).itemsize for shape, kind in outs),
        ),
        compiler_params=pltpu.CompilerParams(vmem_limit_bytes=20 * 1024 * 1024),
    )(
        place,
        *after,
        *[pltpu.with_memory_space_constraint(x, pltpu.HBM) for x in far],
        *[pltpu.with_memory_space_constraint(x, pltpu.VMEM) for x in operands],
    )


def sides(core, nodes):
    above, below = 2 * nodes, 0
    return (
        pl.multiple_of(jnp.where(core == 0, above, below), nodes),
        pl.multiple_of(jnp.where(core == 0, below, above), nodes),
    )


def padded(value, rows):
    zeros = jnp.zeros((rows - value.shape[0], value.shape[1]), value.dtype)
    return jnp.concatenate([value, zeros], axis=0)


def prepare_body(
    ens, place, latents, w_hidden, index, weight, w_out_t, truth,
    adjacency, adjacency_t, w_hidden_t, own, w_hidden_here, w_out_here, truth_here, sems
):
    copies = [
        pltpu.make_async_copy(w_hidden, w_hidden_here, sems.at[0]),
        pltpu.make_async_copy(latents, own, sems.at[1]),
    ]
    for copy in copies:
        copy.start()
    edges, grid = index.shape
    chunk = grid // ens
    rows = adjacency_t.shape[0]
    row = lax.broadcasted_iota(jnp.int32, (rows, chunk), 0)
    for k, bits in enumerate(routes(ens)):
        lanes = pl.ds(pl.multiple_of(neighbour(place, bits) * chunk, chunk), chunk)
        nodes = index[:, lanes]
        weights = weight[:, lanes].astype(bf16).astype(f32)
        block = jnp.zeros((rows, chunk), f32)
        for j in range(edges):
            block += jnp.where(nodes[j : j + 1] == row, weights[j : j + 1], 0.0)
        adjacency_t[:, k * chunk : (k + 1) * chunk] = block.astype(bf16)
        adjacency[k * chunk : (k + 1) * chunk, :] = block.T.astype(bf16)
    w_out_here[...] = padded(w_out_t[...].astype(f32), w_out_here.shape[0]).astype(bf16)
    truth_here[...] = padded(truth[...], truth_here.shape[0])
    for copy in copies:
        copy.wait()
    w_hidden_t[...] = w_hidden_here[...].T


def partial_body(place, own, on_chip, adjacency, partial):
    mem, nodes, _ = own.shape
    first, _ = sides(place[2], nodes)
    for m in range(mem):
        total = mul(adjacency[:, nodes : 2 * nodes], own[m])
        partial[m] = total + mul(adjacency[:, pl.ds(first, nodes)], on_chip[m])


def forward_body(
    ens, place, partial, on_link, adjacency, w_hidden, w_out_t, aggregate, preact, activated, *pieces
):
    mem, nodes, width = on_link.shape
    variables = w_out_t.shape[0]
    grid = adjacency.shape[0]
    chunk = grid // ens
    step = 256
    _, second = sides(place[2], nodes)
    for m in range(mem):
        total = partial[m] + mul(adjacency[:, pl.ds(second, nodes)], on_link[m])
        gathered = total.astype(bf16)
        aggregate[m] = gathered
        forecast = jnp.zeros((grid, variables), f32)
        for at in range(0, width, step):
            value = mul(gathered, w_hidden[:, at : at + step])
            preact[m, :, at : at + step] = value
            silu = (value / (1.0 + jnp.exp(-value))).astype(bf16)
            activated[m, :, at : at + step] = silu
            forecast += mul(silu, w_out_t[:, at : at + step], right_turned)
        turned = forecast.T
        for k in range(ens):
            rows = slice(m * variables, (m + 1) * variables)
            pieces[k][rows] = turned[:, k * chunk : (k + 1) * chunk]


def slope_body(place, preact, slope):
    for m in range(preact.shape[0]):
        value = preact[m]
        logistic = 1.0 / (1.0 + jnp.exp(-value))
        slope[m] = logistic * (1.0 + value * (1.0 - logistic))


def turn_body(place, aggregate, aggregate_t):
    mem, grid, _ = aggregate.shape
    for m in range(mem):
        aggregate_t[:, m * grid : (m + 1) * grid] = aggregate[m].T


def loss_body(ens, scale, place, truth, *refs):
    here, out = refs[:ens], refs[ens:]
    rows, chunk = here[0].shape
    mem = rows // truth.shape[0]
    members = mem * ens
    variables = truth.shape[0]
    target = truth[:, pl.ds(pl.multiple_of(place[0] * chunk, chunk), chunk)]
    forecasts = [
        here[k][m * variables : (m + 1) * variables] for k in range(ens) for m in range(mem)
    ]

    def ratio(d):
        return d * lax.rsqrt(d * d + smoothing * smoothing)

    spread = [jnp.zeros_like(target) for _ in forecasts]
    for i in range(members):
        for j in range(i + 1, members):
            term = ratio(forecasts[i] - forecasts[j])
            spread[i] += term
            spread[j] -= term
    gradients = [
        scale
        * (
            ratio(forecasts[i] - target) * (1.0 / members)
            - spread[i] * (1.0 / (members * (members - 1)))
        )
        for i in range(members)
    ]
    for k in range(ens):
        total = jnp.concatenate(gradients[k * mem : (k + 1) * mem], axis=0)
        out[k][...] = total.astype(bf16)


def backward_body(ens, place, w_out_t, slope, activated, *refs):
    dforecast, (dpreact, out_part) = refs[:ens], refs[ens:]
    mem, grid, _ = slope.shape
    variables = w_out_t.shape[0]
    gradients = jnp.concatenate([piece[...] for piece in dforecast], axis=1)
    gradients = gradients.astype(f32)
    out_total = None
    for m in range(mem):
        gradient = gradients[m * variables : (m + 1) * variables].astype(bf16)
        dactivated = mul(gradient, w_out_t[...], left_turned)
        dpreact[m * grid : (m + 1) * grid] = (dactivated * slope[m]).astype(bf16)
        part = mul(gradient, activated[m])
        out_total = part if out_total is None else out_total + part
    out_part[...] = out_total


def slot_of(core, k):
    return jnp.where(k == 1 + core, 2, jnp.where(k == 2 - core, 1, k))


def half_body(ens, chips, mine, place, dpreact, out_part, aggregate_t, half):
    e, chip, core = place[0], place[1], place[2]
    core = core if mine else 1 - core
    rows = aggregate_t.shape[2]
    lanes = dpreact.shape[1] // ens
    strip = 2 * (half.shape[2] - rows)
    for z in range(chips):
        columns = pl.ds(pl.multiple_of((2 * z + core) * rows, rows), rows)
        part = padded(out_part[:, columns], ens * strip).astype(half.dtype)
        for j in range(ens):
            slot = slot_of(core, j ^ e)
            half[slot, z ^ chip, rows:, :rows] = part[j * strip : j * strip + strip // 2]
            half[slot, z ^ chip, rows:, rows:] = part[j * strip + strip // 2 : (j + 1) * strip]
    left = aggregate_t[:, core].reshape(chips * rows, -1)
    for slot, k in ((0, 0), (1, 2 - core), (2, 1 + core), (3, 3)):
        columns = pl.ds(pl.multiple_of((e ^ k) * lanes, lanes), lanes)
        block = mul(left, dpreact[:, columns]).astype(half.dtype)
        for z in range(chips):
            half[slot, z ^ chip, :rows] = block[z * rows : (z + 1) * rows]


def link_window_body(m, place, dpreact, w_hidden_t, adjacency_t, on_link, daggregate):
    nodes = on_link.shape[0]
    grid = adjacency_t.shape[1]
    _, second = sides(place[2], nodes)
    total = mul(dpreact[m * grid : (m + 1) * grid], w_hidden_t[...]).astype(bf16)
    daggregate[...] = total
    on_link[...] = mul(adjacency_t[pl.ds(second, nodes)], total).astype(bf16)


def near_window_body(place, adjacency_t, *refs):
    daggregates, (on_chip, own) = refs[:-2], refs[-2:]
    mem, nodes, _ = own.shape
    first, _ = sides(place[2], nodes)
    for m in range(mem):
        total = daggregates[m][...]
        on_chip[m] = mul(adjacency_t[pl.ds(first, nodes)], total).astype(bf16)
        own[m] = mul(adjacency_t[nodes : 2 * nodes], total)


def latents_body(place, own, on_chip, *refs):
    on_link, (total, token) = refs[:-2], refs[-2:]
    for m in range(own.shape[0]):
        total[m] = own[m] + on_chip[m].astype(f32) + on_link[m][...].astype(f32)
    token[...] = jnp.zeros_like(token)


def sum_body(place, kept, received, mine, sent):
    staying = mine.shape[0]
    for k in range(kept.shape[0]):
        total = kept[k] + received[k].astype(f32)
        if k < staying:
            mine[k] = total
        else:
            sent[k - staying] = total.astype(bf16)


def chip_slots_body(place, kept, received, mine, *sent):
    count = kept.shape[1]
    for q in range(count):
        total = kept[0, q] + received[0, q].astype(f32)
        if q == 0:
            mine[...] = total
        else:
            sent[count - 1 - q][...] = total.astype(bf16)


def chip_sum_body(place, kept, *refs):
    received, out = refs[:-1], refs[-1]
    total = kept[...]
    for block in received:
        total += block[...].astype(f32)
    out[...] = total.astype(bf16)


def assemble_body(ens, place, *refs):
    pieces, (hidden, out, joined) = refs[:ens], refs[ens:]
    rows, width = hidden.shape
    lanes = width // ens
    strip = 2 * (pieces[0].shape[0] - rows)
    for k, bits in enumerate(routes(ens)):
        source = neighbour(place, bits)
        piece = pieces[k][...].astype(f32)
        hidden[:, pl.ds(pl.multiple_of(source * lanes, lanes), lanes)] = piece[:rows]
        start = pl.multiple_of(source * strip, strip)
        joined[pl.ds(start, strip // 2), :] = piece[rows:, :rows]
        joined[pl.ds(start + strip // 2, strip // 2), :] = piece[rows:, rows:]
    out[...] = joined[: out.shape[0]]


def reduced(aggregate_t, dpreact, out_part, variables, place, mem, ens, chips, window):
    width = dpreact.shape[1]
    rows = width // (2 * chips)
    lanes = width // ens
    strip = 32 * pl.cdiv(out_part.shape[0], 32 * ens)
    aggregate_t = aggregate_t.reshape(chips, 2, rows, -1)
    block = (rows + strip // 2, lanes)

    def half(mine, kind, *before):
        return call(
            functools.partial(half_body, ens, chips, mine), [((ens, chips) + block, kind)],
            place, dpreact, out_part, aggregate_t, after=before, flops=dpreact.size * width,
        )[0]

    given = half(False, bf16)
    received = chip_swap(given)
    link_window, near_window = window
    parts = [link_window(0, given)]
    kept = half(True, f32, parts[0][1])
    before = []
    for staying, bits in ((2, (1, 2)), (1, (2, 1))):
        shape = (staying, chips) + block
        kept, given = call(
            sum_body, [(shape, f32), (shape, bf16)], place, kept, received, after=before
        )
        received = core_swap(given, "ens", bits)
        if staying == 2:
            later = [link_window(m, kept) for m in range(1, mem)]
            middle, latents_sum = near_window(parts + later)
            before = [middle]
    kept, *given = call(
        chip_slots_body, [(block, f32)] + [(block, bf16)] * (chips - 1), place, kept, received,
        after=[arrived for arrived, _ in parts + later], flops=4 * 10**9,
    )
    received = [core_swap(given[chips - 1 - q], "chip", (q, q)) for q in range(chips - 1, 0, -1)]
    total = call(chip_sum_body, [(block, bf16)], place, kept, *received, flops=4 * 10**9)[0]
    every = exchanged([total] * ens)
    grad_latents, token = latents_sum(total)
    hidden, out = call(
        functools.partial(assemble_body, ens), [((rows, width), f32), ((variables, rows), f32)],
        place, *every, after=[token], last=True, scratch=[pltpu.VMEM((ens * strip, rows), f32)],
    )
    return grad_latents, hidden, out.T


def reduced_any(aggregate_t, dpreact, out_part, variables):
    part = mul(aggregate_t, dpreact)
    summed = lax.psum((part, out_part[:variables].T), "ens")
    return tuple(
        lax.psum_scatter(value, "space", scatter_dimension=0, tiled=True) for value in summed
    )


def shards(latents, edge_index, edge_weight, truth, w_hidden, output_weight):
    mem, nodes, width = latents.shape
    variables, grid = truth.shape
    ens, space = lax.axis_size("ens"), lax.axis_size("space")
    chips = space // 2
    members = mem * ens
    scale = 1.0 / math.sqrt(grid * space * members)
    e, s = lax.axis_index("ens"), lax.axis_index("space")
    place = jnp.stack([e, s // 2, s % 2]).astype(jnp.int32)
    chunk = grid // ens
    w_out_t = output_weight.T

    on_link = link_swap(latents)
    on_chip = chip_swap(latents)
    rows = 8 * pl.cdiv(variables, 8)
    adjacency, adjacency_t, w_hidden_t, own, w_hidden_here, w_out_here, truth_here = call(
        functools.partial(prepare_body, ens),
        [((grid, 3 * nodes), bf16), ((3 * nodes, grid), bf16), (w_hidden.shape[::-1], bf16)]
        + [(latents.shape, bf16), (w_hidden.shape, bf16)]
        + [((rows, width), bf16), ((rows, grid), f32)],
        place, edge_index.T, edge_weight.T, w_out_t, truth, far=[latents, w_hidden],
        scratch=[pltpu.SemaphoreType.DMA((2,))],
    )
    cells = (mem, grid, width)
    partial = call(partial_body, [(cells, f32)], place, own, on_chip, adjacency)[0]
    piece = (mem * rows, chunk)
    aggregate, preact, activated, *pieces = call(
        functools.partial(forward_body, ens),
        [(cells, bf16), (cells, f32), (cells, bf16)] + [(piece, f32)] * ens,
        place, partial, on_link, adjacency, w_hidden_here, w_out_here,
        flops=2 * mem * grid * width * (nodes + width + 128),
    )
    here = exchanged(pieces)
    slope = call(slope_body, [(cells, f32)], place, preact, after=pieces)[0]
    gradients = call(
        functools.partial(loss_body, ens, scale), [(piece, bf16)] * ens, place, truth_here, *here,
        after=[slope],
    )
    dforecast = exchanged(gradients)
    aggregate_t = call(
        turn_body, [((width, mem * grid), bf16)], place, aggregate, after=gradients
    )[0]
    dpreact, out_part = call(
        functools.partial(backward_body, ens),
        [((mem * grid, width), bf16), ((rows, width), f32)],
        place, w_out_here, slope, activated, *dforecast,
        flops=4 * mem * grid * width * 128,
    )
    band = (mem, nodes, width)

    def link_window(m, *before):
        given, daggregate = call(
            functools.partial(link_window_body, m), [(band[1:], bf16), (cells[1:], bf16)],
            place, dpreact, w_hidden_t, adjacency_t, after=before,
            flops=2 * grid * width * (width + nodes),
        )
        return link_swap(given), daggregate

    def near_window(parts):
        on_link, daggregates = zip(*parts)
        on_chip, middle = call(
            near_window_body, [(band, bf16), (band, f32)], place, adjacency_t, *daggregates,
            flops=4 * mem * grid * width * nodes,
        )
        on_chip = chip_swap(on_chip)

        def total(*before):
            return call(
                latents_body, [(band, f32), ((8, 128), f32)], place, middle, on_chip, *on_link,
                after=before, last=True,
            )

        return middle, total

    if width % (space * 128) == 0 and width // ens == 2 * (width // space) and ens == 4:
        window = link_window, near_window
        return reduced(aggregate_t, dpreact, out_part, variables, place, mem, ens, chips, window)
    grad_latents = near_window([link_window(m) for m in range(mem)])[1]()[0]
    return (grad_latents, *reduced_any(aggregate_t, dpreact, out_part, variables))


def solution(mesh):
    placed = (
        P("ens", "space", None),
        P("space", None),
        P("space", None),
        P(None, "space"),
        P(),
        P(),
    )
    return jax.shard_map(
        shards,
        mesh=mesh,
        in_specs=placed,
        out_specs=(P("ens", "space", None), P("space", None), P("space", None)),
        check_vma=False,
    )
```

```python
import functools
import math

import jax
import jax.numpy as jnp
from jax import lax
from jax.experimental import pallas as pl
from jax.experimental.pallas import tpu as pltpu
from jax.sharding import PartitionSpec as P

smoothing = 0.05
f32, bf16 = jnp.float32, jnp.bfloat16
across = (((1,), (0,)), ((), ()))
right_turned = (((1,), (1,)), ((), ()))
left_turned = (((0,), (0,)), ((), ()))


def chip_swap(value):
    count = lax.axis_size("space")
    return lax.ppermute(value, "space", [(i, i ^ 1) for i in range(count)])


def link_swap(value):
    count = lax.axis_size("space")
    pairs = [(i, i + 1) for i in range(1, count - 1, 2)]
    return lax.ppermute(value, "space", pairs + [(j, i) for i, j in pairs])


def core_swap(value, axis, bits):
    ens, space = lax.axis_size("ens"), lax.axis_size("space")

    def partner(e, s):
        bit = bits[s % 2]
        return (e ^ bit) * space + s if axis == "ens" else e * space + (s ^ (2 * bit))

    return lax.ppermute(
        value,
        ("ens", "space"),
        [(e * space + s, partner(e, s)) for e in range(ens) for s in range(space)],
    )


def routes(ens):
    if ens == 4:
        return [(0, 0), (3, 3), (1, 2), (2, 1)]
    return [(k, k) for k in range(ens)]


def backward_routes(ens):
    return routes(ens)[:1] + routes(ens)[:0:-1]


def exchanged(values, paths):
    others = zip(values[1:], paths[1:])
    return [values[0]] + [core_swap(value, "ens", bits) for value, bits in others]


def neighbour(place, bits):
    return place[0] ^ jnp.where(place[2] == 0, bits[0], bits[1])


def mul(a, b, dims=across):
    return lax.dot_general(a, b, dims, preferred_element_type=f32)


def call(body, outs, place, *operands, after=(), far=(), flops=0, last=False, scratch=()):
    vmem = pl.BlockSpec(memory_space=pltpu.VMEM)
    unread = pl.BlockSpec(memory_space=pl.ANY)

    def kernel(place_ref, *refs):
        body(place_ref, *refs[len(after) :])

    return pl.pallas_call(
        kernel,
        out_shape=[
            jax.ShapeDtypeStruct(shape, kind) if last else pltpu.VMEM(shape, kind)
            for shape, kind in outs
        ],
        in_specs=[pl.BlockSpec(memory_space=pltpu.SMEM)]
        + [unread] * len(after)
        + [pl.BlockSpec(memory_space=pltpu.HBM)] * len(far)
        + [vmem] * len(operands),
        out_specs=[vmem] * len(outs),
        scratch_shapes=scratch,
        cost_estimate=pl.CostEstimate(
            flops=flops,
            transcendentals=0,
            bytes_accessed=sum(x.size * x.dtype.itemsize for x in operands)
            + sum(math.prod(shape) * jnp.dtype(kind).itemsize for shape, kind in outs),
        ),
        compiler_params=pltpu.CompilerParams(vmem_limit_bytes=20 * 1024 * 1024),
    )(
        place,
        *after,
        *[pltpu.with_memory_space_constraint(x, pltpu.HBM) for x in far],
        *[pltpu.with_memory_space_constraint(x, pltpu.VMEM) for x in operands],
    )


def sides(core, nodes):
    above, below = 2 * nodes, 0
    return (
        pl.multiple_of(jnp.where(core == 0, above, below), nodes),
        pl.multiple_of(jnp.where(core == 0, below, above), nodes),
    )


def padded(value, rows):
    zeros = jnp.zeros((rows - value.shape[0], value.shape[1]), value.dtype)
    return jnp.concatenate([value, zeros], axis=0)


def prepare_body(
    ens, place, latents, w_hidden, index, weight, w_out_t, truth,
    adjacency, adjacency_t, w_hidden_t, own, w_hidden_here, w_out_here, truth_here, sems
):
    copies = [
        pltpu.make_async_copy(w_hidden, w_hidden_here, sems.at[0]),
        pltpu.make_async_copy(latents, own, sems.at[1]),
    ]
    for copy in copies:
        copy.start()
    edges, grid = index.shape
    chunk = grid // ens
    rows = adjacency_t.shape[0]
    row = lax.broadcasted_iota(jnp.int32, (rows, chunk), 0)
    for k, bits in enumerate(routes(ens)):
        lanes = pl.ds(pl.multiple_of(neighbour(place, bits) * chunk, chunk), chunk)
        nodes = index[:, lanes]
        weights = weight[:, lanes].astype(bf16).astype(f32)
        block = jnp.zeros((rows, chunk), f32)
        for j in range(edges):
            block += jnp.where(nodes[j : j + 1] == row, weights[j : j + 1], 0.0)
        adjacency_t[:, k * chunk : (k + 1) * chunk] = block.astype(bf16)
        adjacency[k * chunk : (k + 1) * chunk, :] = block.T.astype(bf16)
    w_out_here[...] = padded(w_out_t[...].astype(f32), w_out_here.shape[0]).astype(bf16)
    truth_here[...] = padded(truth[...], truth_here.shape[0])
    for copy in copies:
        copy.wait()
    w_hidden_t[...] = w_hidden_here[...].T


def partial_body(place, own, on_chip, adjacency, partial):
    mem, nodes, _ = own.shape
    first, _ = sides(place[2], nodes)
    for m in range(mem):
        total = mul(adjacency[:, nodes : 2 * nodes], own[m])
        partial[m] = total + mul(adjacency[:, pl.ds(first, nodes)], on_chip[m])


def forward_body(
    ens, place, partial, on_link, adjacency, w_hidden, w_out_t, aggregate, preact, activated, *pieces
):
    mem, nodes, width = on_link.shape
    variables = w_out_t.shape[0]
    grid = adjacency.shape[0]
    chunk = grid // ens
    step = 256
    _, second = sides(place[2], nodes)
    for m in range(mem):
        total = partial[m] + mul(adjacency[:, pl.ds(second, nodes)], on_link[m])
        gathered = total.astype(bf16)
        aggregate[m] = gathered
        forecast = jnp.zeros((grid, variables), f32)
        for at in range(0, width, step):
            value = mul(gathered, w_hidden[:, at : at + step])
            preact[m, :, at : at + step] = value
            silu = (value / (1.0 + jnp.exp(-value))).astype(bf16)
            activated[m, :, at : at + step] = silu
            forecast += mul(silu, w_out_t[:, at : at + step], right_turned)
        turned = forecast.T
        for k in range(ens):
            rows = slice(m * variables, (m + 1) * variables)
            pieces[k][rows] = turned[:, k * chunk : (k + 1) * chunk]


def slope_body(place, preact, slope):
    for m in range(preact.shape[0]):
        value = preact[m]
        logistic = 1.0 / (1.0 + jnp.exp(-value))
        slope[m] = logistic * (1.0 + value * (1.0 - logistic))


def turn_body(place, aggregate, aggregate_t):
    mem, grid, _ = aggregate.shape
    for m in range(mem):
        aggregate_t[:, m * grid : (m + 1) * grid] = aggregate[m].T


def loss_body(ens, scale, place, truth, *refs):
    here, out = refs[:ens], refs[ens:]
    rows, chunk = here[0].shape
    mem = rows // truth.shape[0]
    members = mem * ens
    variables = truth.shape[0]
    target = truth[:, pl.ds(pl.multiple_of(place[0] * chunk, chunk), chunk)]
    forecasts = [
        here[k][m * variables : (m + 1) * variables] for k in range(ens) for m in range(mem)
    ]

    def ratio(d):
        return d * lax.rsqrt(d * d + smoothing * smoothing)

    spread = [jnp.zeros_like(target) for _ in forecasts]
    for i in range(members):
        for j in range(i + 1, members):
            term = ratio(forecasts[i] - forecasts[j])
            spread[i] += term
            spread[j] -= term
    gradients = [
        scale
        * (
            ratio(forecasts[i] - target) * (1.0 / members)
            - spread[i] * (1.0 / (members * (members - 1)))
        )
        for i in range(members)
    ]
    for k in range(ens):
        total = jnp.concatenate(gradients[k * mem : (k + 1) * mem], axis=0)
        out[k][...] = total.astype(bf16)


def backward_body(ens, place, w_out_t, slope, activated, *refs):
    dforecast, (dpreact, out_part) = refs[:ens], refs[ens:]
    mem, grid, _ = slope.shape
    variables = w_out_t.shape[0]
    gradients = jnp.concatenate([piece[...] for piece in dforecast], axis=1)
    gradients = gradients.astype(f32)
    out_total = None
    for m in range(mem):
        gradient = gradients[m * variables : (m + 1) * variables].astype(bf16)
        dactivated = mul(gradient, w_out_t[...], left_turned)
        dpreact[m * grid : (m + 1) * grid] = (dactivated * slope[m]).astype(bf16)
        part = mul(gradient, activated[m])
        out_total = part if out_total is None else out_total + part
    out_part[...] = out_total


def slot_of(core, k):
    return jnp.where(k == 1 + core, 2, jnp.where(k == 2 - core, 1, k))


def half_body(ens, chips, mine, place, dpreact, out_part, aggregate_t, half):
    e, chip, core = place[0], place[1], place[2]
    core = core if mine else 1 - core
    rows = aggregate_t.shape[2]
    lanes = dpreact.shape[1] // ens
    strip = 2 * (half.shape[2] - rows)
    for z in range(chips):
        columns = pl.ds(pl.multiple_of((2 * z + core) * rows, rows), rows)
        part = padded(out_part[:, columns], ens * strip).astype(half.dtype)
        for j in range(ens):
            slot = slot_of(core, j ^ e)
            half[slot, z ^ chip, rows:, :rows] = part[j * strip : j * strip + strip // 2]
            half[slot, z ^ chip, rows:, rows:] = part[j * strip + strip // 2 : (j + 1) * strip]
    left = aggregate_t[:, core].reshape(chips * rows, -1)
    for slot, k in ((0, 0), (1, 2 - core), (2, 1 + core), (3, 3)):
        columns = pl.ds(pl.multiple_of((e ^ k) * lanes, lanes), lanes)
        block = mul(left, dpreact[:, columns]).astype(half.dtype)
        for z in range(chips):
            half[slot, z ^ chip, :rows] = block[z * rows : (z + 1) * rows]


def link_window_body(m, place, dpreact, w_hidden_t, adjacency_t, on_link, daggregate):
    nodes = on_link.shape[0]
    grid = adjacency_t.shape[1]
    _, second = sides(place[2], nodes)
    total = mul(dpreact[m * grid : (m + 1) * grid], w_hidden_t[...]).astype(bf16)
    daggregate[...] = total
    on_link[...] = mul(adjacency_t[pl.ds(second, nodes)], total).astype(bf16)


def near_window_body(place, adjacency_t, *refs):
    daggregates, (on_chip, own) = refs[:-2], refs[-2:]
    mem, nodes, _ = own.shape
    first, _ = sides(place[2], nodes)
    for m in range(mem):
        total = daggregates[m][...]
        on_chip[m] = mul(adjacency_t[pl.ds(first, nodes)], total).astype(bf16)
        own[m] = mul(adjacency_t[nodes : 2 * nodes], total)


def latents_body(place, own, on_chip, *refs):
    on_link, (total, token) = refs[:-2], refs[-2:]
    for m in range(own.shape[0]):
        total[m] = own[m] + on_chip[m].astype(f32) + on_link[m][...].astype(f32)
    token[...] = jnp.zeros_like(token)


def sum_body(place, kept, received, mine, sent):
    staying = mine.shape[0]
    for k in range(kept.shape[0]):
        total = kept[k] + received[k].astype(f32)
        if k < staying:
            mine[k] = total
        else:
            sent[k - staying] = total.astype(bf16)


def chip_slots_body(place, kept, received, mine, *sent):
    count = kept.shape[1]
    for q in range(count):
        total = kept[0, q] + received[0, q].astype(f32)
        if q == 0:
            mine[...] = total
        else:
            sent[count - 1 - q][...] = total.astype(bf16)


def chip_sum_body(place, kept, *refs):
    received, out = refs[:-1], refs[-1]
    total = kept[...]
    for block in received:
        total += block[...].astype(f32)
    out[...] = total.astype(bf16)


def assemble_body(ens, place, *refs):
    pieces, (hidden, out, joined) = refs[:ens], refs[ens:]
    rows, width = hidden.shape
    lanes = width // ens
    strip = 2 * (pieces[0].shape[0] - rows)
    for k, bits in enumerate(backward_routes(ens)):
        source = neighbour(place, bits)
        piece = pieces[k][...].astype(f32)
        hidden[:, pl.ds(pl.multiple_of(source * lanes, lanes), lanes)] = piece[:rows]
        start = pl.multiple_of(source * strip, strip)
        joined[pl.ds(start, strip // 2), :] = piece[rows:, :rows]
        joined[pl.ds(start + strip // 2, strip // 2), :] = piece[rows:, rows:]
    out[...] = joined[: out.shape[0]]


def reduced(aggregate_t, dpreact, out_part, variables, place, mem, ens, chips, window):
    width = dpreact.shape[1]
    rows = width // (2 * chips)
    lanes = width // ens
    strip = 32 * pl.cdiv(out_part.shape[0], 32 * ens)
    aggregate_t = aggregate_t.reshape(chips, 2, rows, -1)
    block = (rows + strip // 2, lanes)

    def half(mine, kind, *before):
        return call(
            functools.partial(half_body, ens, chips, mine), [((ens, chips) + block, kind)],
            place, dpreact, out_part, aggregate_t, after=before, flops=dpreact.size * width,
        )[0]

    given = half(False, bf16)
    received = chip_swap(given)
    link_window, near_window = window
    parts = [link_window(0, given)]
    kept = half(True, f32, parts[0][1])
    before = []
    for staying, bits in ((2, (1, 2)), (1, (2, 1))):
        shape = (staying, chips) + block
        kept, given = call(
            sum_body, [(shape, f32), (shape, bf16)], place, kept, received, after=before
        )
        received = core_swap(given, "ens", bits)
        if staying == 2:
            parts += [link_window(m, kept) for m in range(1, mem)]
            latents_sum = near_window(parts)
            before = [daggregate for _, daggregate in parts[1:]]
    kept, *given = call(
        chip_slots_body, [(block, f32)] + [(block, bf16)] * (chips - 1), place, kept, received,
        after=[parts[0][0]], flops=6 * 10**9,
    )
    received = [core_swap(given[chips - 1 - q], "chip", (q, q)) for q in range(chips - 1, 0, -1)]
    total = call(
        chip_sum_body, [(block, bf16)], place, kept, *received,
        after=[arrived for arrived, _ in parts[1:]], flops=6 * 10**9,
    )[0]
    every = exchanged([total] * ens, backward_routes(ens))
    grad_latents, token = latents_sum(total)
    hidden, out = call(
        functools.partial(assemble_body, ens), [((rows, width), f32), ((variables, rows), f32)],
        place, *every, after=[token], last=True, scratch=[pltpu.VMEM((ens * strip, rows), f32)],
    )
    return grad_latents, hidden, out.T


def reduced_any(aggregate_t, dpreact, out_part, variables):
    part = mul(aggregate_t, dpreact)
    summed = lax.psum((part, out_part[:variables].T), "ens")
    return tuple(
        lax.psum_scatter(value, "space", scatter_dimension=0, tiled=True) for value in summed
    )


def shards(latents, edge_index, edge_weight, truth, w_hidden, output_weight):
    mem, nodes, width = latents.shape
    variables, grid = truth.shape
    ens, space = lax.axis_size("ens"), lax.axis_size("space")
    chips = space // 2
    members = mem * ens
    scale = 1.0 / math.sqrt(grid * space * members)
    e, s = lax.axis_index("ens"), lax.axis_index("space")
    place = jnp.stack([e, s // 2, s % 2]).astype(jnp.int32)
    chunk = grid // ens
    w_out_t = output_weight.T

    on_link = link_swap(latents)
    on_chip = chip_swap(latents)
    rows = 8 * pl.cdiv(variables, 8)
    adjacency, adjacency_t, w_hidden_t, own, w_hidden_here, w_out_here, truth_here = call(
        functools.partial(prepare_body, ens),
        [((grid, 3 * nodes), bf16), ((3 * nodes, grid), bf16), (w_hidden.shape[::-1], bf16)]
        + [(latents.shape, bf16), (w_hidden.shape, bf16)]
        + [((rows, width), bf16), ((rows, grid), f32)],
        place, edge_index.T, edge_weight.T, w_out_t, truth, far=[latents, w_hidden],
        scratch=[pltpu.SemaphoreType.DMA((2,))],
    )
    cells = (mem, grid, width)
    partial = call(partial_body, [(cells, f32)], place, own, on_chip, adjacency)[0]
    piece = (mem * rows, chunk)
    aggregate, preact, activated, *pieces = call(
        functools.partial(forward_body, ens),
        [(cells, bf16), (cells, f32), (cells, bf16)] + [(piece, f32)] * ens,
        place, partial, on_link, adjacency, w_hidden_here, w_out_here,
        flops=2 * mem * grid * width * (nodes + width + 128),
    )
    here = exchanged(pieces, routes(ens))
    slope = call(slope_body, [(cells, f32)], place, preact, after=pieces)[0]
    gradients = call(
        functools.partial(loss_body, ens, scale), [(piece, bf16)] * ens, place, truth_here, *here,
        after=[slope],
    )
    dforecast = exchanged(gradients, routes(ens))
    aggregate_t = call(
        turn_body, [((width, mem * grid), bf16)], place, aggregate, after=gradients
    )[0]
    dpreact, out_part = call(
        functools.partial(backward_body, ens),
        [((mem * grid, width), bf16), ((rows, width), f32)],
        place, w_out_here, slope, activated, *dforecast,
        flops=4 * mem * grid * width * 128,
    )
    band = (mem, nodes, width)

    def link_window(m, *before):
        given, daggregate = call(
            functools.partial(link_window_body, m), [(band[1:], bf16), (cells[1:], bf16)],
            place, dpreact, w_hidden_t, adjacency_t, after=before,
            flops=2 * grid * width * (width + nodes),
        )
        return link_swap(given), daggregate

    def near_window(parts):
        on_link, daggregates = zip(*parts)
        on_chip, middle = call(
            near_window_body, [(band, bf16), (band, f32)], place, adjacency_t, *daggregates,
            after=on_link[:1], flops=4 * mem * grid * width * nodes,
        )
        on_chip = chip_swap(on_chip)

        def total(*before):
            return call(
                latents_body, [(band, f32), ((8, 128), f32)], place, middle, on_chip, *on_link,
                after=before, last=True,
            )

        return total

    if width % (space * 128) == 0 and width // ens == 2 * (width // space) and ens == 4:
        window = link_window, near_window
        return reduced(aggregate_t, dpreact, out_part, variables, place, mem, ens, chips, window)
    grad_latents = near_window([link_window(m) for m in range(mem)])()[0]
    return (grad_latents, *reduced_any(aggregate_t, dpreact, out_part, variables))


def solution(mesh):
    placed = (
        P("ens", "space", None),
        P("space", None),
        P("space", None),
        P(None, "space"),
        P(),
        P(),
    )
    return jax.shard_map(
        shards,
        mesh=mesh,
        in_specs=placed,
        out_specs=(P("ens", "space", None), P("space", None), P("space", None)),
        check_vma=False,
    )
```

```python
import functools
import math

import jax
import jax.numpy as jnp
from jax import lax
from jax.experimental import pallas as pl
from jax.experimental.pallas import tpu as pltpu
from jax.sharding import PartitionSpec as P

smoothing = 0.05
f32, bf16 = jnp.float32, jnp.bfloat16
across = (((1,), (0,)), ((), ()))
right_turned = (((1,), (1,)), ((), ()))
left_turned = (((0,), (0,)), ((), ()))


def chip_swap(value):
    count = lax.axis_size("space")
    return lax.ppermute(value, "space", [(i, i ^ 1) for i in range(count)])


def link_swap(value):
    count = lax.axis_size("space")
    pairs = [(i, i + 1) for i in range(1, count - 1, 2)]
    return lax.ppermute(value, "space", pairs + [(j, i) for i, j in pairs])


def core_swap(value, axis, bits):
    ens, space = lax.axis_size("ens"), lax.axis_size("space")

    def partner(e, s):
        bit = bits[s % 2]
        return (e ^ bit) * space + s if axis == "ens" else e * space + (s ^ (2 * bit))

    return lax.ppermute(
        value,
        ("ens", "space"),
        [(e * space + s, partner(e, s)) for e in range(ens) for s in range(space)],
    )


def routes(ens):
    if ens == 4:
        return [(0, 0), (1, 2), (2, 1), (3, 3)]
    return [(k, k) for k in range(ens)]


def exchanged(values):
    others = zip(values[1:], routes(len(values))[1:])
    return [values[0]] + [core_swap(value, "ens", bits) for value, bits in others]


def neighbour(place, bits):
    return place[0] ^ jnp.where(place[2] == 0, bits[0], bits[1])


def mul(a, b, dims=across):
    return lax.dot_general(a, b, dims, preferred_element_type=f32)


def call(body, outs, place, *operands, after=(), far=(), flops=0, last=False, scratch=()):
    vmem = pl.BlockSpec(memory_space=pltpu.VMEM)
    unread = pl.BlockSpec(memory_space=pl.ANY)

    def kernel(place_ref, *refs):
        body(place_ref, *refs[len(after) :])

    return pl.pallas_call(
        kernel,
        out_shape=[
            jax.ShapeDtypeStruct(shape, kind) if last else pltpu.VMEM(shape, kind)
            for shape, kind in outs
        ],
        in_specs=[pl.BlockSpec(memory_space=pltpu.SMEM)]
        + [unread] * len(after)
        + [pl.BlockSpec(memory_space=pltpu.HBM)] * len(far)
        + [vmem] * len(operands),
        out_specs=[vmem] * len(outs),
        scratch_shapes=scratch,
        cost_estimate=pl.CostEstimate(
            flops=flops,
            transcendentals=0,
            bytes_accessed=sum(x.size * x.dtype.itemsize for x in operands)
            + sum(math.prod(shape) * jnp.dtype(kind).itemsize for shape, kind in outs),
        ),
        compiler_params=pltpu.CompilerParams(vmem_limit_bytes=20 * 1024 * 1024),
    )(
        place,
        *after,
        *[pltpu.with_memory_space_constraint(x, pltpu.HBM) for x in far],
        *[pltpu.with_memory_space_constraint(x, pltpu.VMEM) for x in operands],
    )


def sides(core, nodes):
    above, below = 2 * nodes, 0
    return (
        pl.multiple_of(jnp.where(core == 0, above, below), nodes),
        pl.multiple_of(jnp.where(core == 0, below, above), nodes),
    )


def padded(value, rows):
    if value.shape[0] == rows:
        return value
    zeros = jnp.zeros((rows - value.shape[0], value.shape[1]), value.dtype)
    return jnp.concatenate([value, zeros], axis=0)


def prepare_body(
    ens, place, latents, w_hidden, index, weight, w_out_t, truth,
    adjacency, adjacency_t, w_hidden_t, own, w_hidden_here, w_out_here, truth_here, sems
):
    copies = [
        pltpu.make_async_copy(w_hidden, w_hidden_here, sems.at[0]),
        pltpu.make_async_copy(latents, own, sems.at[1]),
    ]
    for copy in copies:
        copy.start()
    edges, grid = index.shape
    chunk = grid // ens
    rows = adjacency_t.shape[0]
    row = lax.broadcasted_iota(jnp.int32, (rows, chunk), 0)
    for k, bits in enumerate(routes(ens)):
        lanes = pl.ds(pl.multiple_of(neighbour(place, bits) * chunk, chunk), chunk)
        nodes = index[:, lanes]
        weights = weight[:, lanes].astype(bf16).astype(f32)
        block = jnp.zeros((rows, chunk), f32)
        for j in range(edges):
            block += jnp.where(nodes[j : j + 1] == row, weights[j : j + 1], 0.0)
        adjacency_t[:, k * chunk : (k + 1) * chunk] = block.astype(bf16)
        adjacency[k * chunk : (k + 1) * chunk, :] = block.T.astype(bf16)
    w_out_here[...] = padded(w_out_t[...].astype(f32), w_out_here.shape[0]).astype(bf16)
    truth_here[...] = padded(truth[...], truth_here.shape[0])
    for copy in copies:
        copy.wait()
    w_hidden_t[...] = w_hidden_here[...].T


def partial_body(place, own, on_chip, adjacency, partial):
    mem, nodes, _ = own.shape
    first, _ = sides(place[2], nodes)
    for m in range(mem):
        total = mul(adjacency[:, nodes : 2 * nodes], own[m])
        partial[m] = total + mul(adjacency[:, pl.ds(first, nodes)], on_chip[m])


def forward_body(
    ens, place, partial, on_link, adjacency, w_hidden, w_out_t, aggregate, preact, activated, *pieces
):
    mem, nodes, width = on_link.shape
    variables = w_out_t.shape[0]
    grid = adjacency.shape[0]
    chunk = grid // ens
    step = 256
    _, second = sides(place[2], nodes)
    for m in range(mem):
        total = partial[m] + mul(adjacency[:, pl.ds(second, nodes)], on_link[m])
        gathered = total.astype(bf16)
        aggregate[m] = gathered
        forecast = jnp.zeros((grid, variables), f32)
        for at in range(0, width, step):
            value = mul(gathered, w_hidden[:, at : at + step])
            preact[m, :, at : at + step] = value
            silu = (value / (1.0 + jnp.exp(-value))).astype(bf16)
            activated[m, :, at : at + step] = silu
            forecast += mul(silu, w_out_t[:, at : at + step], right_turned)
        turned = forecast.T
        for k in range(ens):
            rows = slice(m * variables, (m + 1) * variables)
            pieces[k][rows] = turned[:, k * chunk : (k + 1) * chunk]


def slope_body(place, preact, slope):
    for m in range(preact.shape[0]):
        value = preact[m]
        logistic = 1.0 / (1.0 + jnp.exp(-value))
        slope[m] = logistic * (1.0 + value * (1.0 - logistic))


def turn_body(place, aggregate, aggregate_t):
    mem, grid, _ = aggregate.shape
    for m in range(mem):
        aggregate_t[:, m * grid : (m + 1) * grid] = aggregate[m].T


def loss_body(ens, scale, place, truth, *refs):
    here, out = refs[:ens], refs[ens:]
    rows, chunk = here[0].shape
    mem = rows // truth.shape[0]
    members = mem * ens
    variables = truth.shape[0]
    target = truth[:, pl.ds(pl.multiple_of(place[0] * chunk, chunk), chunk)]
    forecasts = [
        here[k][m * variables : (m + 1) * variables] for k in range(ens) for m in range(mem)
    ]

    def ratio(d):
        return d * lax.rsqrt(d * d + smoothing * smoothing)

    spread = [jnp.zeros_like(target) for _ in forecasts]
    for i in range(members):
        for j in range(i + 1, members):
            term = ratio(forecasts[i] - forecasts[j])
            spread[i] += term
            spread[j] -= term
    gradients = [
        scale
        * (
            ratio(forecasts[i] - target) * (1.0 / members)
            - spread[i] * (1.0 / (members * (members - 1)))
        )
        for i in range(members)
    ]
    for k in range(ens):
        total = jnp.concatenate(gradients[k * mem : (k + 1) * mem], axis=0)
        out[k][...] = total.astype(bf16)


def backward_body(ens, place, w_out_t, slope, activated, *refs):
    dforecast, (dpreact, out_part) = refs[:ens], refs[ens:]
    mem, grid, _ = slope.shape
    variables = w_out_t.shape[0]
    gradients = jnp.concatenate([piece[...] for piece in dforecast], axis=1)
    gradients = gradients.astype(f32)
    out_total = None
    for m in range(mem):
        gradient = gradients[m * variables : (m + 1) * variables].astype(bf16)
        dactivated = mul(gradient, w_out_t[...], left_turned)
        dpreact[m * grid : (m + 1) * grid] = (dactivated * slope[m]).astype(bf16)
        part = mul(gradient, activated[m])
        out_total = part if out_total is None else out_total + part
    out_part[...] = padded(out_total, out_part.shape[0])


def gradient_blocks(ens, chips, core, slots, place, dpreact, out_part, aggregate_t, emit):
    e, chip = place[0], place[1]
    rows = aggregate_t.shape[2]
    lanes = dpreact.shape[1] // ens
    strip = out_part.shape[0] // ens
    half = strip // 2
    left = aggregate_t[:, core].reshape(chips * rows, -1)
    for slot in slots:
        source = e ^ (0, 2 - core, 1 + core, 3)[slot]
        columns = pl.ds(pl.multiple_of(source * lanes, lanes), lanes)
        block = mul(left, dpreact[:, columns])
        start = pl.multiple_of(source * strip, strip)
        for z in range(chips):
            to = z ^ chip
            columns = pl.ds(pl.multiple_of((2 * z + core) * rows, rows), rows)
            upper = out_part[pl.ds(start, half), columns]
            lower = out_part[pl.ds(start + half, half), columns]
            emit(slot, to, slice(0, rows), slice(0, lanes), block[z * rows : (z + 1) * rows])
            emit(slot, to, slice(rows, rows + half), slice(0, rows), upper)
            emit(slot, to, slice(rows, rows + half), slice(rows, lanes), lower)


def backward_half_body(ens, chips, place, w_out_t, slope, activated, aggregate_t, *refs):
    dforecast, (dpreact, out_part, half) = refs[:ens], refs[ens:]
    backward_body(ens, place, w_out_t, slope, activated, *dforecast, dpreact, out_part)

    def emit(slot, to, rows, lanes, value):
        half[slot - 2, to, rows, lanes] = value.astype(bf16)

    core = 1 - place[2]
    gradient_blocks(ens, chips, core, (2, 3), place, dpreact, out_part, aggregate_t, emit)


def staying_body(ens, chips, place, dpreact, out_part, aggregate_t, half, kept):
    def emit_half(slot, to, rows, lanes, value):
        half[slot, to, rows, lanes] = value.astype(bf16)

    def emit_kept(slot, to, rows, lanes, value):
        kept[slot, to, rows, lanes] = value

    operands = place, dpreact, out_part, aggregate_t
    gradient_blocks(ens, chips, 1 - place[2], (0, 1), *operands, emit_half)
    gradient_blocks(ens, chips, place[2], (0, 1), *operands, emit_kept)


def leaving_body(ens, chips, place, dpreact, out_part, aggregate_t, received, sent):
    def emit(slot, to, rows, lanes, value):
        total = value + received[slot - 2, to, rows, lanes].astype(f32)
        sent[slot - 2, to, rows, lanes] = total.astype(bf16)

    core = place[2]
    gradient_blocks(ens, chips, core, (2, 3), place, dpreact, out_part, aggregate_t, emit)


def window_body(place, dpreact, w_hidden_t, adjacency_t, on_link, on_chip, own):
    mem, nodes, _ = own.shape
    grid = adjacency_t.shape[1]
    first, second = sides(place[2], nodes)
    for m in range(mem):
        total = mul(dpreact[m * grid : (m + 1) * grid], w_hidden_t[...]).astype(bf16)
        on_link[m] = mul(adjacency_t[pl.ds(second, nodes)], total).astype(bf16)
        on_chip[m] = mul(adjacency_t[pl.ds(first, nodes)], total).astype(bf16)
        own[m] = mul(adjacency_t[nodes : 2 * nodes], total)


def latents_body(place, own, on_chip, on_link, total, token):
    for m in range(own.shape[0]):
        total[m] = own[m] + on_chip[m].astype(f32) + on_link[m].astype(f32)
    token[...] = jnp.zeros_like(token)


def staying_sum_body(place, kept, from_core, from_ens, mine, sent):
    mine[0] = kept[0] + from_core[0].astype(f32) + from_ens[0].astype(f32)
    total = kept[1] + from_core[1].astype(f32) + from_ens[1].astype(f32)
    sent[0] = total.astype(bf16)


def chip_slots_body(place, kept, received, mine, *sent):
    count = kept.shape[1]
    for q in range(count):
        total = kept[0, q] + received[0, q].astype(f32)
        if q == 0:
            mine[...] = total
        else:
            sent[count - 1 - q][...] = total.astype(bf16)


def chip_sum_body(place, kept, *refs):
    received, out = refs[:-1], refs[-1]
    total = kept[...]
    for block in received:
        total += block[...].astype(f32)
    out[...] = total.astype(bf16)


def assemble_body(ens, place, *refs):
    pieces, (hidden, out, joined) = refs[:ens], refs[ens:]
    rows, width = hidden.shape
    lanes = width // ens
    strip = 2 * (pieces[0].shape[0] - rows)
    for k, bits in enumerate(routes(ens)):
        source = neighbour(place, bits)
        piece = pieces[k][...].astype(f32)
        hidden[:, pl.ds(pl.multiple_of(source * lanes, lanes), lanes)] = piece[:rows]
        start = pl.multiple_of(source * strip, strip)
        joined[pl.ds(start, strip // 2), :] = piece[rows:, :rows]
        joined[pl.ds(start + strip // 2, strip // 2), :] = piece[rows:, rows:]
    out[...] = joined[: out.shape[0]]


def reduced(w_out_t, slope, activated, aggregate_t, dforecast, variables, place, chips, window):
    ens = len(dforecast)
    mem, grid, width = slope.shape
    rows = width // (2 * chips)
    lanes = width // ens
    strip = 32 * pl.cdiv(variables, 32 * ens)
    aggregate_t = aggregate_t.reshape(chips, 2, rows, -1)
    block = (rows + strip // 2, lanes)
    pair = (2, chips) + block
    flops = mem * grid * width * width

    dpreact, out_part, given = call(
        functools.partial(backward_half_body, ens, chips),
        [((mem * grid, width), bf16), ((ens * strip, width), f32), (pair, bf16)],
        place, w_out_t, slope, activated, aggregate_t, *dforecast,
        flops=flops // 2 + 4 * mem * grid * width * 128,
    )
    leaving = chip_swap(given)
    given, kept = call(
        functools.partial(staying_body, ens, chips), [(pair, bf16), (pair, f32)],
        place, dpreact, out_part, aggregate_t, flops=flops,
    )
    staying = chip_swap(given)
    given = call(
        functools.partial(leaving_body, ens, chips), [(pair, bf16)],
        place, dpreact, out_part, aggregate_t, leaving, after=[kept], flops=flops // 2,
    )[0]
    received = core_swap(given, "ens", (1, 2))
    latents_sum = window(dpreact, given)
    shape = (1, chips) + block
    kept, given = call(
        staying_sum_body, [(shape, f32), (shape, bf16)], place, kept, staying, received
    )
    received = core_swap(given, "ens", (2, 1))
    kept, *given = call(
        chip_slots_body, [(block, f32)] + [(block, bf16)] * (chips - 1), place, kept, received,
        flops=10**9,
    )
    received = [core_swap(given[chips - 1 - q], "chip", (q, q)) for q in range(chips - 1, 0, -1)]
    total = call(chip_sum_body, [(block, bf16)], place, kept, *received, flops=10**9)[0]
    every = exchanged([total] * ens)
    grad_latents, token = latents_sum(total)
    hidden, out = call(
        functools.partial(assemble_body, ens), [((rows, width), f32), ((variables, rows), f32)],
        place, *every, after=[token], last=True, scratch=[pltpu.VMEM((ens * strip, rows), f32)],
    )
    return grad_latents, hidden, out.T


def reduced_any(aggregate_t, dpreact, out_part, variables):
    part = mul(aggregate_t, dpreact)
    summed = lax.psum((part, out_part[:variables].T), "ens")
    return tuple(
        lax.psum_scatter(value, "space", scatter_dimension=0, tiled=True) for value in summed
    )


def shards(latents, edge_index, edge_weight, truth, w_hidden, output_weight):
    mem, nodes, width = latents.shape
    variables, grid = truth.shape
    ens, space = lax.axis_size("ens"), lax.axis_size("space")
    chips = space // 2
    members = mem * ens
    scale = 1.0 / math.sqrt(grid * space * members)
    e, s = lax.axis_index("ens"), lax.axis_index("space")
    place = jnp.stack([e, s // 2, s % 2]).astype(jnp.int32)
    chunk = grid // ens
    w_out_t = output_weight.T

    on_link = link_swap(latents)
    on_chip = chip_swap(latents)
    rows = 8 * pl.cdiv(variables, 8)
    adjacency, adjacency_t, w_hidden_t, own, w_hidden_here, w_out_here, truth_here = call(
        functools.partial(prepare_body, ens),
        [((grid, 3 * nodes), bf16), ((3 * nodes, grid), bf16), (w_hidden.shape[::-1], bf16)]
        + [(latents.shape, bf16), (w_hidden.shape, bf16)]
        + [((rows, width), bf16), ((rows, grid), f32)],
        place, edge_index.T, edge_weight.T, w_out_t, truth, far=[latents, w_hidden],
        scratch=[pltpu.SemaphoreType.DMA((2,))],
    )
    cells = (mem, grid, width)
    partial = call(partial_body, [(cells, f32)], place, own, on_chip, adjacency)[0]
    piece = (mem * rows, chunk)
    aggregate, preact, activated, *pieces = call(
        functools.partial(forward_body, ens),
        [(cells, bf16), (cells, f32), (cells, bf16)] + [(piece, f32)] * ens,
        place, partial, on_link, adjacency, w_hidden_here, w_out_here,
        flops=2 * mem * grid * width * (nodes + width + 128),
    )
    here = exchanged(pieces)
    slope = call(slope_body, [(cells, f32)], place, preact, after=pieces)[0]
    gradients = call(
        functools.partial(loss_body, ens, scale), [(piece, bf16)] * ens, place, truth_here, *here,
        after=[slope],
    )
    dforecast = exchanged(gradients)
    aggregate_t = call(
        turn_body, [((width, mem * grid), bf16)], place, aggregate, after=gradients
    )[0]
    band = (mem, nodes, width)

    def window(dpreact, *before):
        on_link, on_chip, middle = call(
            window_body, [(band, bf16)] * 2 + [(band, f32)],
            place, dpreact, w_hidden_t, adjacency_t, after=before,
            flops=2 * mem * grid * width * (width + 3 * nodes),
        )
        on_link, on_chip = link_swap(on_link), chip_swap(on_chip)

        def total(*before):
            return call(
                latents_body, [(band, f32), ((8, 128), f32)], place, middle, on_chip, on_link,
                after=before, last=True,
            )

        return total

    if width % (space * 128) == 0 and width // ens == 2 * (width // space) and ens == 4:
        return reduced(
            w_out_here, slope, activated, aggregate_t, dforecast, variables, place, chips, window
        )
    dpreact, out_part = call(
        functools.partial(backward_body, ens),
        [((mem * grid, width), bf16), ((rows, width), f32)],
        place, w_out_here, slope, activated, *dforecast,
        flops=4 * mem * grid * width * 128,
    )
    return (window(dpreact)()[0], *reduced_any(aggregate_t, dpreact, out_part, variables))


def solution(mesh):
    placed = (
        P("ens", "space", None),
        P("space", None),
        P("space", None),
        P(None, "space"),
        P(),
        P(),
    )
    return jax.shard_map(
        shards,
        mesh=mesh,
        in_specs=placed,
        out_specs=(P("ens", "space", None), P("space", None), P("space", None)),
        check_vma=False,
    )
```

```python
import functools
import math

import jax
import jax.numpy as jnp
from jax import lax
from jax.experimental import pallas as pl
from jax.experimental.pallas import tpu as pltpu
from jax.sharding import PartitionSpec as P

smoothing = 0.05
f32, bf16 = jnp.float32, jnp.bfloat16
across = (((1,), (0,)), ((), ()))
right_turned = (((1,), (1,)), ((), ()))
left_turned = (((0,), (0,)), ((), ()))


def chip_swap(value):
    count = lax.axis_size("space")
    return lax.ppermute(value, "space", [(i, i ^ 1) for i in range(count)])


def link_swap(value):
    count = lax.axis_size("space")
    pairs = [(i, i + 1) for i in range(1, count - 1, 2)]
    return lax.ppermute(value, "space", pairs + [(j, i) for i, j in pairs])


def core_swap(value, axis, bits):
    ens, space = lax.axis_size("ens"), lax.axis_size("space")

    def partner(e, s):
        bit = bits[s % 2]
        return (e ^ bit) * space + s if axis == "ens" else e * space + (s ^ (2 * bit))

    return lax.ppermute(
        value,
        ("ens", "space"),
        [(e * space + s, partner(e, s)) for e in range(ens) for s in range(space)],
    )


def routes(ens):
    if ens == 4:
        return [(0, 0), (1, 2), (2, 1), (3, 3)]
    return [(k, k) for k in range(ens)]


def exchanged(values):
    others = zip(values[1:], routes(len(values))[1:])
    return [values[0]] + [core_swap(value, "ens", bits) for value, bits in others]


def neighbour(place, bits):
    return place[0] ^ jnp.where(place[2] == 0, bits[0], bits[1])


def mul(a, b, dims=across):
    return lax.dot_general(a, b, dims, preferred_element_type=f32)


def call(body, outs, place, *operands, after=(), far=(), flops=0, last=False, scratch=()):
    vmem = pl.BlockSpec(memory_space=pltpu.VMEM)
    unread = pl.BlockSpec(memory_space=pl.ANY)

    def kernel(place_ref, *refs):
        body(place_ref, *refs[len(after) :])

    return pl.pallas_call(
        kernel,
        out_shape=[
            jax.ShapeDtypeStruct(shape, kind) if last else pltpu.VMEM(shape, kind)
            for shape, kind in outs
        ],
        in_specs=[pl.BlockSpec(memory_space=pltpu.SMEM)]
        + [unread] * len(after)
        + [pl.BlockSpec(memory_space=pltpu.HBM)] * len(far)
        + [vmem] * len(operands),
        out_specs=[vmem] * len(outs),
        scratch_shapes=scratch,
        cost_estimate=pl.CostEstimate(
            flops=flops,
            transcendentals=0,
            bytes_accessed=sum(x.size * x.dtype.itemsize for x in operands)
            + sum(math.prod(shape) * jnp.dtype(kind).itemsize for shape, kind in outs),
        ),
        compiler_params=pltpu.CompilerParams(vmem_limit_bytes=20 * 1024 * 1024),
    )(
        place,
        *after,
        *[pltpu.with_memory_space_constraint(x, pltpu.HBM) for x in far],
        *[pltpu.with_memory_space_constraint(x, pltpu.VMEM) for x in operands],
    )


def sides(core, nodes):
    above, below = 2 * nodes, 0
    return (
        pl.multiple_of(jnp.where(core == 0, above, below), nodes),
        pl.multiple_of(jnp.where(core == 0, below, above), nodes),
    )


def padded(value, rows):
    if value.shape[0] == rows:
        return value
    zeros = jnp.zeros((rows - value.shape[0], value.shape[1]), value.dtype)
    return jnp.concatenate([value, zeros], axis=0)


def prepare_body(
    ens, place, latents, w_hidden, index, weight, w_out_t, truth,
    adjacency, adjacency_t, w_hidden_t, own, w_hidden_here, w_out_here, truth_here, sems
):
    copies = [
        pltpu.make_async_copy(w_hidden, w_hidden_here, sems.at[0]),
        pltpu.make_async_copy(latents, own, sems.at[1]),
    ]
    for copy in copies:
        copy.start()
    edges, grid = index.shape
    chunk = grid // ens
    rows = adjacency_t.shape[0]
    row = lax.broadcasted_iota(jnp.int32, (rows, chunk), 0)
    for k, bits in enumerate(routes(ens)):
        lanes = pl.ds(pl.multiple_of(neighbour(place, bits) * chunk, chunk), chunk)
        nodes = index[:, lanes]
        weights = weight[:, lanes].astype(bf16).astype(f32)
        block = jnp.zeros((rows, chunk), f32)
        for j in range(edges):
            block += jnp.where(nodes[j : j + 1] == row, weights[j : j + 1], 0.0)
        adjacency_t[:, k * chunk : (k + 1) * chunk] = block.astype(bf16)
        adjacency[k * chunk : (k + 1) * chunk, :] = block.T.astype(bf16)
    w_out_here[...] = padded(w_out_t[...].astype(f32), w_out_here.shape[0]).astype(bf16)
    truth_here[...] = padded(truth[...], truth_here.shape[0])
    for copy in copies:
        copy.wait()
    w_hidden_t[...] = w_hidden_here[...].T


def partial_body(place, own, on_chip, adjacency, partial):
    mem, nodes, _ = own.shape
    first, _ = sides(place[2], nodes)
    for m in range(mem):
        total = mul(adjacency[:, nodes : 2 * nodes], own[m])
        partial[m] = total + mul(adjacency[:, pl.ds(first, nodes)], on_chip[m])


def forward_body(
    ens, place, partial, on_link, adjacency, w_hidden, w_out_t, aggregate, preact, activated, *pieces
):
    mem, nodes, width = on_link.shape
    variables = w_out_t.shape[0]
    grid = adjacency.shape[0]
    chunk = grid // ens
    step = 256
    _, second = sides(place[2], nodes)
    for m in range(mem):
        total = partial[m] + mul(adjacency[:, pl.ds(second, nodes)], on_link[m])
        gathered = total.astype(bf16)
        aggregate[m] = gathered
        forecast = jnp.zeros((grid, variables), f32)
        for at in range(0, width, step):
            value = mul(gathered, w_hidden[:, at : at + step])
            preact[m, :, at : at + step] = value
            silu = (value / (1.0 + jnp.exp(-value))).astype(bf16)
            activated[m, :, at : at + step] = silu
            forecast += mul(silu, w_out_t[:, at : at + step], right_turned)
        turned = forecast.T
        for k in range(ens):
            rows = slice(m * variables, (m + 1) * variables)
            pieces[k][rows] = turned[:, k * chunk : (k + 1) * chunk]


def slope_body(place, preact, slope):
    for m in range(preact.shape[0]):
        value = preact[m]
        logistic = 1.0 / (1.0 + jnp.exp(-value))
        slope[m] = logistic * (1.0 + value * (1.0 - logistic))


def turn_body(place, aggregate, aggregate_t):
    mem, grid, _ = aggregate.shape
    for m in range(mem):
        aggregate_t[:, m * grid : (m + 1) * grid] = aggregate[m].T


def loss_body(ens, scale, place, truth, *refs):
    here, out = refs[:ens], refs[ens:]
    rows, chunk = here[0].shape
    mem = rows // truth.shape[0]
    members = mem * ens
    variables = truth.shape[0]
    target = truth[:, pl.ds(pl.multiple_of(place[0] * chunk, chunk), chunk)]
    forecasts = [
        here[k][m * variables : (m + 1) * variables] for k in range(ens) for m in range(mem)
    ]

    def ratio(d):
        return d * lax.rsqrt(d * d + smoothing * smoothing)

    spread = [jnp.zeros_like(target) for _ in forecasts]
    for i in range(members):
        for j in range(i + 1, members):
            term = ratio(forecasts[i] - forecasts[j])
            spread[i] += term
            spread[j] -= term
    gradients = [
        scale
        * (
            ratio(forecasts[i] - target) * (1.0 / members)
            - spread[i] * (1.0 / (members * (members - 1)))
        )
        for i in range(members)
    ]
    for k in range(ens):
        total = jnp.concatenate(gradients[k * mem : (k + 1) * mem], axis=0)
        out[k][...] = total.astype(bf16)


def backward_body(ens, place, w_out_t, slope, activated, *refs):
    dforecast, (dpreact, out_part) = refs[:ens], refs[ens:]
    mem, grid, _ = slope.shape
    variables = w_out_t.shape[0]
    gradients = jnp.concatenate([piece[...] for piece in dforecast], axis=1)
    gradients = gradients.astype(f32)
    out_total = None
    for m in range(mem):
        gradient = gradients[m * variables : (m + 1) * variables].astype(bf16)
        dactivated = mul(gradient, w_out_t[...], left_turned)
        dpreact[m * grid : (m + 1) * grid] = (dactivated * slope[m]).astype(bf16)
        part = mul(gradient, activated[m])
        out_total = part if out_total is None else out_total + part
    out_part[...] = padded(out_total, out_part.shape[0])


def gradient_blocks(ens, chips, core, slots, place, dpreact, out_part, aggregate_t, emit):
    e, chip = place[0], place[1]
    rows = aggregate_t.shape[2]
    lanes = dpreact.shape[1] // ens
    strip = out_part.shape[0] // ens
    half = strip // 2
    left = aggregate_t[:, core].reshape(chips * rows, -1)
    for slot in slots:
        source = e ^ (0, 2 - core, 1 + core, 3)[slot]
        columns = pl.ds(pl.multiple_of(source * lanes, lanes), lanes)
        block = mul(left, dpreact[:, columns])
        start = pl.multiple_of(source * strip, strip)
        for z in range(chips):
            to = z ^ chip
            columns = pl.ds(pl.multiple_of((2 * z + core) * rows, rows), rows)
            upper = out_part[pl.ds(start, half), columns]
            lower = out_part[pl.ds(start + half, half), columns]
            emit(slot, to, slice(0, rows), slice(0, lanes), block[z * rows : (z + 1) * rows])
            emit(slot, to, slice(rows, rows + half), slice(0, rows), upper)
            emit(slot, to, slice(rows, rows + half), slice(rows, lanes), lower)


def backward_half_body(ens, chips, place, w_out_t, slope, activated, aggregate_t, *refs):
    dforecast, (dpreact, out_part, half) = refs[:ens], refs[ens:]
    backward_body(ens, place, w_out_t, slope, activated, *dforecast, dpreact, out_part)

    def emit(slot, to, rows, lanes, value):
        half[slot - 2, to, rows, lanes] = value.astype(bf16)

    core = 1 - place[2]
    gradient_blocks(ens, chips, core, (2, 3), place, dpreact, out_part, aggregate_t, emit)


def staying_body(ens, chips, place, dpreact, out_part, aggregate_t, half, kept):
    def emit_half(slot, to, rows, lanes, value):
        half[slot, to, rows, lanes] = value.astype(bf16)

    def emit_kept(slot, to, rows, lanes, value):
        kept[slot, to, rows, lanes] = value

    operands = place, dpreact, out_part, aggregate_t
    gradient_blocks(ens, chips, 1 - place[2], (0, 1), *operands, emit_half)
    gradient_blocks(ens, chips, place[2], (0, 1), *operands, emit_kept)


def leaving_body(ens, chips, place, dpreact, out_part, aggregate_t, received, sent):
    def emit(slot, to, rows, lanes, value):
        total = value + received[slot - 2, to, rows, lanes].astype(f32)
        sent[slot - 2, to, rows, lanes] = total.astype(bf16)

    core = place[2]
    gradient_blocks(ens, chips, core, (2, 3), place, dpreact, out_part, aggregate_t, emit)


def link_window_body(m, place, dpreact, w_hidden_t, adjacency_t, on_link, daggregate):
    nodes = on_link.shape[0]
    grid = adjacency_t.shape[1]
    _, second = sides(place[2], nodes)
    total = mul(dpreact[m * grid : (m + 1) * grid], w_hidden_t[...]).astype(bf16)
    daggregate[...] = total
    on_link[...] = mul(adjacency_t[pl.ds(second, nodes)], total).astype(bf16)


def near_window_body(place, adjacency_t, *refs):
    daggregates, (on_chip, own) = refs[:-2], refs[-2:]
    mem, nodes, _ = own.shape
    first, _ = sides(place[2], nodes)
    for m in range(mem):
        total = daggregates[m][...]
        on_chip[m] = mul(adjacency_t[pl.ds(first, nodes)], total).astype(bf16)
        own[m] = mul(adjacency_t[nodes : 2 * nodes], total)


def latents_body(place, own, on_chip, *refs):
    on_link, (total, token) = refs[:-2], refs[-2:]
    for m in range(own.shape[0]):
        total[m] = own[m] + on_chip[m].astype(f32) + on_link[m][...].astype(f32)
    token[...] = jnp.zeros_like(token)


def staying_sum_body(place, kept, from_core, from_ens, mine, sent):
    mine[0] = kept[0] + from_core[0].astype(f32) + from_ens[0].astype(f32)
    total = kept[1] + from_core[1].astype(f32) + from_ens[1].astype(f32)
    sent[0] = total.astype(bf16)


def chip_slots_body(place, kept, received, mine, *sent):
    count = kept.shape[1]
    for q in range(count):
        total = kept[0, q] + received[0, q].astype(f32)
        if q == 0:
            mine[...] = total
        else:
            sent[count - 1 - q][...] = total.astype(bf16)


def chip_sum_body(place, kept, *refs):
    received, out = refs[:-1], refs[-1]
    total = kept[...]
    for block in received:
        total += block[...].astype(f32)
    out[...] = total.astype(bf16)


def assemble_body(ens, place, *refs):
    pieces, (hidden, out, joined) = refs[:ens], refs[ens:]
    rows, width = hidden.shape
    lanes = width // ens
    strip = 2 * (pieces[0].shape[0] - rows)
    for k, bits in enumerate(routes(ens)):
        source = neighbour(place, bits)
        piece = pieces[k][...].astype(f32)
        hidden[:, pl.ds(pl.multiple_of(source * lanes, lanes), lanes)] = piece[:rows]
        start = pl.multiple_of(source * strip, strip)
        joined[pl.ds(start, strip // 2), :] = piece[rows:, :rows]
        joined[pl.ds(start + strip // 2, strip // 2), :] = piece[rows:, rows:]
    out[...] = joined[: out.shape[0]]


def reduced(
    w_out_t, slope, activated, aggregate_t, dforecast, variables, place, chips,
    link_window, near_window,
):
    ens = len(dforecast)
    mem, grid, width = slope.shape
    rows = width // (2 * chips)
    lanes = width // ens
    strip = 32 * pl.cdiv(variables, 32 * ens)
    aggregate_t = aggregate_t.reshape(chips, 2, rows, -1)
    block = (rows + strip // 2, lanes)
    pair = (2, chips) + block
    flops = mem * grid * width * width

    dpreact, out_part, given = call(
        functools.partial(backward_half_body, ens, chips),
        [((mem * grid, width), bf16), ((ens * strip, width), f32), (pair, bf16)],
        place, w_out_t, slope, activated, aggregate_t, *dforecast,
        flops=flops // 2 + 4 * mem * grid * width * 128,
    )
    leaving = chip_swap(given)
    given, kept = call(
        functools.partial(staying_body, ens, chips), [(pair, bf16), (pair, f32)],
        place, dpreact, out_part, aggregate_t, flops=flops,
    )
    staying = chip_swap(given)
    given = call(
        functools.partial(leaving_body, ens, chips), [(pair, bf16)],
        place, dpreact, out_part, aggregate_t, leaving, after=[kept], flops=flops // 2,
    )[0]
    received = core_swap(given, "ens", (1, 2))
    parts = [link_window(0, dpreact, given)]
    parts += [link_window(m, dpreact, parts[0][1]) for m in range(1, mem)]
    latents_sum = near_window(parts)
    shape = (1, chips) + block
    kept, given = call(
        staying_sum_body, [(shape, f32), (shape, bf16)], place, kept, staying, received,
        after=[daggregate for _, daggregate in parts],
    )
    received = core_swap(given, "ens", (2, 1))
    kept, *given = call(
        chip_slots_body, [(block, f32)] + [(block, bf16)] * (chips - 1), place, kept, received,
        after=[arrived for arrived, _ in parts], flops=5 * 10**9,
    )
    received = [core_swap(given[chips - 1 - q], "chip", (q, q)) for q in range(chips - 1, 0, -1)]
    total = call(chip_sum_body, [(block, bf16)], place, kept, *received, flops=5 * 10**9)[0]
    every = exchanged([total] * ens)
    grad_latents, token = latents_sum(total)
    hidden, out = call(
        functools.partial(assemble_body, ens), [((rows, width), f32), ((variables, rows), f32)],
        place, *every, after=[token], last=True, scratch=[pltpu.VMEM((ens * strip, rows), f32)],
    )
    return grad_latents, hidden, out.T


def reduced_any(aggregate_t, dpreact, out_part, variables):
    part = mul(aggregate_t, dpreact)
    summed = lax.psum((part, out_part[:variables].T), "ens")
    return tuple(
        lax.psum_scatter(value, "space", scatter_dimension=0, tiled=True) for value in summed
    )


def shards(latents, edge_index, edge_weight, truth, w_hidden, output_weight):
    mem, nodes, width = latents.shape
    variables, grid = truth.shape
    ens, space = lax.axis_size("ens"), lax.axis_size("space")
    chips = space // 2
    members = mem * ens
    scale = 1.0 / math.sqrt(grid * space * members)
    e, s = lax.axis_index("ens"), lax.axis_index("space")
    place = jnp.stack([e, s // 2, s % 2]).astype(jnp.int32)
    chunk = grid // ens
    w_out_t = output_weight.T

    on_link = link_swap(latents)
    on_chip = chip_swap(latents)
    rows = 8 * pl.cdiv(variables, 8)
    adjacency, adjacency_t, w_hidden_t, own, w_hidden_here, w_out_here, truth_here = call(
        functools.partial(prepare_body, ens),
        [((grid, 3 * nodes), bf16), ((3 * nodes, grid), bf16), (w_hidden.shape[::-1], bf16)]
        + [(latents.shape, bf16), (w_hidden.shape, bf16)]
        + [((rows, width), bf16), ((rows, grid), f32)],
        place, edge_index.T, edge_weight.T, w_out_t, truth, far=[latents, w_hidden],
        scratch=[pltpu.SemaphoreType.DMA((2,))],
    )
    cells = (mem, grid, width)
    partial = call(partial_body, [(cells, f32)], place, own, on_chip, adjacency)[0]
    piece = (mem * rows, chunk)
    aggregate, preact, activated, *pieces = call(
        functools.partial(forward_body, ens),
        [(cells, bf16), (cells, f32), (cells, bf16)] + [(piece, f32)] * ens,
        place, partial, on_link, adjacency, w_hidden_here, w_out_here,
        flops=2 * mem * grid * width * (nodes + width + 128),
    )
    here = exchanged(pieces)
    slope = call(slope_body, [(cells, f32)], place, preact, after=pieces)[0]
    gradients = call(
        functools.partial(loss_body, ens, scale), [(piece, bf16)] * ens, place, truth_here, *here,
        after=[slope],
    )
    dforecast = exchanged(gradients)
    aggregate_t = call(
        turn_body, [((width, mem * grid), bf16)], place, aggregate, after=gradients
    )[0]
    band = (mem, nodes, width)

    def link_window(m, dpreact, *before):
        given, daggregate = call(
            functools.partial(link_window_body, m), [(band[1:], bf16), (cells[1:], bf16)],
            place, dpreact, w_hidden_t, adjacency_t, after=before,
            flops=2 * grid * width * (width + nodes),
        )
        return link_swap(given), daggregate

    def near_window(parts):
        on_link, daggregates = zip(*parts)
        on_chip, middle = call(
            near_window_body, [(band, bf16), (band, f32)], place, adjacency_t, *daggregates,
            after=on_link[:1], flops=4 * mem * grid * width * nodes,
        )
        on_chip = chip_swap(on_chip)

        def total(*before):
            return call(
                latents_body, [(band, f32), ((8, 128), f32)], place, middle, on_chip, *on_link,
                after=before, last=True,
            )

        return total

    if width % (space * 128) == 0 and width // ens == 2 * (width // space) and ens == 4:
        return reduced(
            w_out_here, slope, activated, aggregate_t, dforecast, variables, place, chips,
            link_window, near_window,
        )
    dpreact, out_part = call(
        functools.partial(backward_body, ens),
        [((mem * grid, width), bf16), ((rows, width), f32)],
        place, w_out_here, slope, activated, *dforecast,
        flops=4 * mem * grid * width * 128,
    )
    grad_latents = near_window([link_window(m, dpreact) for m in range(mem)])()[0]
    return (grad_latents, *reduced_any(aggregate_t, dpreact, out_part, variables))


def solution(mesh):
    placed = (
        P("ens", "space", None),
        P("space", None),
        P("space", None),
        P(None, "space"),
        P(),
        P(),
    )
    return jax.shard_map(
        shards,
        mesh=mesh,
        in_specs=placed,
        out_specs=(P("ens", "space", None), P("space", None), P("space", None)),
        check_vma=False,
    )
```

```python
import functools
import math

import jax
import jax.numpy as jnp
from jax import lax
from jax.experimental import pallas as pl
from jax.experimental.pallas import tpu as pltpu
from jax.sharding import PartitionSpec as P

smoothing = 0.05
f32, bf16 = jnp.float32, jnp.bfloat16
across = (((1,), (0,)), ((), ()))
right_turned = (((1,), (1,)), ((), ()))
left_turned = (((0,), (0,)), ((), ()))


def chip_swap(value):
    count = lax.axis_size("space")
    return lax.ppermute(value, "space", [(i, i ^ 1) for i in range(count)])


def link_swap(value):
    count = lax.axis_size("space")
    pairs = [(i, i + 1) for i in range(1, count - 1, 2)]
    return lax.ppermute(value, "space", pairs + [(j, i) for i, j in pairs])


def core_swap(value, axis, bits):
    ens, space = lax.axis_size("ens"), lax.axis_size("space")

    def partner(e, s):
        bit = bits[s % 2]
        return (e ^ bit) * space + s if axis == "ens" else e * space + (s ^ (2 * bit))

    return lax.ppermute(
        value,
        ("ens", "space"),
        [(e * space + s, partner(e, s)) for e in range(ens) for s in range(space)],
    )


def routes(ens):
    if ens == 4:
        return [(0, 0), (1, 2), (2, 1), (3, 3)]
    return [(k, k) for k in range(ens)]


def exchanged(values):
    others = zip(values[1:], routes(len(values))[1:])
    return [values[0]] + [core_swap(value, "ens", bits) for value, bits in others]


def neighbour(place, bits):
    return place[0] ^ jnp.where(place[2] == 0, bits[0], bits[1])


def mul(a, b, dims=across):
    return lax.dot_general(a, b, dims, preferred_element_type=f32)


def call(body, outs, place, *operands, after=(), far=(), flops=0, last=False, scratch=()):
    vmem = pl.BlockSpec(memory_space=pltpu.VMEM)
    unread = pl.BlockSpec(memory_space=pl.ANY)

    def kernel(place_ref, *refs):
        body(place_ref, *refs[len(after) :])

    return pl.pallas_call(
        kernel,
        out_shape=[
            jax.ShapeDtypeStruct(shape, kind) if last else pltpu.VMEM(shape, kind)
            for shape, kind in outs
        ],
        in_specs=[pl.BlockSpec(memory_space=pltpu.SMEM)]
        + [unread] * len(after)
        + [pl.BlockSpec(memory_space=pltpu.HBM)] * len(far)
        + [vmem] * len(operands),
        out_specs=[vmem] * len(outs),
        scratch_shapes=scratch,
        cost_estimate=pl.CostEstimate(
            flops=flops,
            transcendentals=0,
            bytes_accessed=sum(x.size * x.dtype.itemsize for x in operands)
            + sum(math.prod(shape) * jnp.dtype(kind).itemsize for shape, kind in outs),
        ),
        compiler_params=pltpu.CompilerParams(vmem_limit_bytes=20 * 1024 * 1024),
    )(
        place,
        *after,
        *[pltpu.with_memory_space_constraint(x, pltpu.HBM) for x in far],
        *[pltpu.with_memory_space_constraint(x, pltpu.VMEM) for x in operands],
    )


def sides(core, nodes):
    above, below = 2 * nodes, 0
    return (
        pl.multiple_of(jnp.where(core == 0, above, below), nodes),
        pl.multiple_of(jnp.where(core == 0, below, above), nodes),
    )


def padded(value, rows):
    if value.shape[0] == rows:
        return value
    zeros = jnp.zeros((rows - value.shape[0], value.shape[1]), value.dtype)
    return jnp.concatenate([value, zeros], axis=0)


def prepare_body(
    ens, place, latents, w_hidden, index, weight, w_out_t, truth,
    adjacency, adjacency_t, w_hidden_t, own, w_hidden_here, w_out_here, truth_here, sems
):
    copies = [
        pltpu.make_async_copy(w_hidden, w_hidden_here, sems.at[0]),
        pltpu.make_async_copy(latents, own, sems.at[1]),
    ]
    for copy in copies:
        copy.start()
    edges, grid = index.shape
    chunk = grid // ens
    rows = adjacency_t.shape[0]
    row = lax.broadcasted_iota(jnp.int32, (rows, chunk), 0)
    for k, bits in enumerate(routes(ens)):
        lanes = pl.ds(pl.multiple_of(neighbour(place, bits) * chunk, chunk), chunk)
        nodes = index[:, lanes]
        weights = weight[:, lanes].astype(bf16).astype(f32)
        block = jnp.zeros((rows, chunk), f32)
        for j in range(edges):
            block += jnp.where(nodes[j : j + 1] == row, weights[j : j + 1], 0.0)
        adjacency_t[:, k * chunk : (k + 1) * chunk] = block.astype(bf16)
        adjacency[k * chunk : (k + 1) * chunk, :] = block.T.astype(bf16)
    w_out_here[...] = padded(w_out_t[...].astype(f32), w_out_here.shape[0]).astype(bf16)
    truth_here[...] = padded(truth[...], truth_here.shape[0])
    for copy in copies:
        copy.wait()
    w_hidden_t[...] = w_hidden_here[...].T


def partial_body(place, own, on_chip, adjacency, partial):
    mem, nodes, _ = own.shape
    first, _ = sides(place[2], nodes)
    for m in range(mem):
        total = mul(adjacency[:, nodes : 2 * nodes], own[m])
        partial[m] = total + mul(adjacency[:, pl.ds(first, nodes)], on_chip[m])


def forward_body(
    ens, place, partial, on_link, adjacency, w_hidden, w_out_t, aggregate, preact, activated, *pieces
):
    mem, nodes, width = on_link.shape
    variables = w_out_t.shape[0]
    grid = adjacency.shape[0]
    chunk = grid // ens
    step = 256
    _, second = sides(place[2], nodes)
    for m in range(mem):
        total = partial[m] + mul(adjacency[:, pl.ds(second, nodes)], on_link[m])
        gathered = total.astype(bf16)
        aggregate[m] = gathered
        forecast = jnp.zeros((grid, variables), f32)
        for at in range(0, width, step):
            value = mul(gathered, w_hidden[:, at : at + step])
            preact[m, :, at : at + step] = value
            silu = (value / (1.0 + jnp.exp(-value))).astype(bf16)
            activated[m, :, at : at + step] = silu
            forecast += mul(silu, w_out_t[:, at : at + step], right_turned)
        turned = forecast.T
        for k in range(ens):
            rows = slice(m * variables, (m + 1) * variables)
            pieces[k][rows] = turned[:, k * chunk : (k + 1) * chunk]


def slope_body(place, preact, slope):
    for m in range(preact.shape[0]):
        value = preact[m]
        logistic = 1.0 / (1.0 + jnp.exp(-value))
        slope[m] = logistic * (1.0 + value * (1.0 - logistic))


def turn_body(place, aggregate, aggregate_t):
    mem, grid, _ = aggregate.shape
    for m in range(mem):
        aggregate_t[:, m * grid : (m + 1) * grid] = aggregate[m].T


def loss_body(ens, scale, place, truth, *refs):
    here, out = refs[:ens], refs[ens:]
    rows, chunk = here[0].shape
    mem = rows // truth.shape[0]
    members = mem * ens
    variables = truth.shape[0]
    target = truth[:, pl.ds(pl.multiple_of(place[0] * chunk, chunk), chunk)]
    forecasts = [
        here[k][m * variables : (m + 1) * variables] for k in range(ens) for m in range(mem)
    ]

    def ratio(d):
        return d * lax.rsqrt(d * d + smoothing * smoothing)

    spread = [jnp.zeros_like(target) for _ in forecasts]
    for i in range(members):
        for j in range(i + 1, members):
            term = ratio(forecasts[i] - forecasts[j])
            spread[i] += term
            spread[j] -= term
    gradients = [
        scale
        * (
            ratio(forecasts[i] - target) * (1.0 / members)
            - spread[i] * (1.0 / (members * (members - 1)))
        )
        for i in range(members)
    ]
    for k in range(ens):
        total = jnp.concatenate(gradients[k * mem : (k + 1) * mem], axis=0)
        out[k][...] = total.astype(bf16)


def backward_body(ens, place, w_out_t, slope, activated, *refs):
    dforecast, (dpreact, out_part) = refs[:ens], refs[ens:]
    mem, grid, _ = slope.shape
    variables = w_out_t.shape[0]
    gradients = jnp.concatenate([piece[...] for piece in dforecast], axis=1)
    gradients = gradients.astype(f32)
    out_total = None
    for m in range(mem):
        gradient = gradients[m * variables : (m + 1) * variables].astype(bf16)
        dactivated = mul(gradient, w_out_t[...], left_turned)
        dpreact[m * grid : (m + 1) * grid] = (dactivated * slope[m]).astype(bf16)
        part = mul(gradient, activated[m])
        out_total = part if out_total is None else out_total + part
    out_part[...] = padded(out_total, out_part.shape[0])


def gradient_blocks(ens, chips, core, slots, place, dpreact, out_part, aggregate_t, emit):
    e, chip = place[0], place[1]
    rows = aggregate_t.shape[2]
    lanes = dpreact.shape[1] // ens
    strip = out_part.shape[0] // ens
    half = strip // 2
    left = aggregate_t[:, core].reshape(chips * rows, -1)
    for slot in slots:
        source = e ^ (0, 2 - core, 1 + core, 3)[slot]
        columns = pl.ds(pl.multiple_of(source * lanes, lanes), lanes)
        block = mul(left, dpreact[:, columns])
        start = pl.multiple_of(source * strip, strip)
        for z in range(chips):
            to = z ^ chip
            columns = pl.ds(pl.multiple_of((2 * z + core) * rows, rows), rows)
            upper = out_part[pl.ds(start, half), columns]
            lower = out_part[pl.ds(start + half, half), columns]
            emit(slot, to, slice(0, rows), slice(0, lanes), block[z * rows : (z + 1) * rows])
            emit(slot, to, slice(rows, rows + half), slice(0, rows), upper)
            emit(slot, to, slice(rows, rows + half), slice(rows, lanes), lower)


def backward_half_body(ens, chips, place, w_out_t, slope, activated, aggregate_t, *refs):
    dforecast, (dpreact, out_part, half) = refs[:ens], refs[ens:]
    backward_body(ens, place, w_out_t, slope, activated, *dforecast, dpreact, out_part)

    def emit(slot, to, rows, lanes, value):
        half[slot - 2, to, rows, lanes] = value.astype(bf16)

    core = 1 - place[2]
    gradient_blocks(ens, chips, core, (2, 3), place, dpreact, out_part, aggregate_t, emit)


def staying_body(ens, chips, place, dpreact, out_part, aggregate_t, half, kept):
    def emit_half(slot, to, rows, lanes, value):
        half[slot, to, rows, lanes] = value.astype(bf16)

    def emit_kept(slot, to, rows, lanes, value):
        kept[slot, to, rows, lanes] = value

    operands = place, dpreact, out_part, aggregate_t
    gradient_blocks(ens, chips, 1 - place[2], (0, 1), *operands, emit_half)
    gradient_blocks(ens, chips, place[2], (0, 1), *operands, emit_kept)


def leaving_body(ens, chips, place, dpreact, out_part, aggregate_t, received, sent, token):
    def emit(slot, to, rows, lanes, value):
        total = value + received[slot - 2, to, rows, lanes].astype(f32)
        sent[slot - 2, to, rows, lanes] = total.astype(bf16)

    token[...] = jnp.zeros_like(token)
    core = place[2]
    gradient_blocks(ens, chips, core, (2, 3), place, dpreact, out_part, aggregate_t, emit)


def link_window_body(m, place, dpreact, w_hidden_t, adjacency_t, on_link, daggregate):
    nodes = on_link.shape[0]
    grid = adjacency_t.shape[1]
    _, second = sides(place[2], nodes)
    total = mul(dpreact[m * grid : (m + 1) * grid], w_hidden_t[...]).astype(bf16)
    daggregate[...] = total
    on_link[...] = mul(adjacency_t[pl.ds(second, nodes)], total).astype(bf16)


def near_window_body(place, adjacency_t, *refs):
    daggregates, (on_chip, own) = refs[:-2], refs[-2:]
    mem, nodes, _ = own.shape
    first, _ = sides(place[2], nodes)
    for m in range(mem):
        total = daggregates[m][...]
        on_chip[m] = mul(adjacency_t[pl.ds(first, nodes)], total).astype(bf16)
        own[m] = mul(adjacency_t[nodes : 2 * nodes], total)


def latents_body(place, own, on_chip, *refs):
    on_link, (total, token) = refs[:-2], refs[-2:]
    for m in range(own.shape[0]):
        total[m] = own[m] + on_chip[m].astype(f32) + on_link[m][...].astype(f32)
    token[...] = jnp.zeros_like(token)


def staying_sum_body(place, kept, from_core, from_ens, mine, sent):
    mine[0] = kept[0] + from_core[0].astype(f32) + from_ens[0].astype(f32)
    total = kept[1] + from_core[1].astype(f32) + from_ens[1].astype(f32)
    sent[0] = total.astype(bf16)


def chip_slots_body(place, kept, received, mine, *sent):
    count = kept.shape[1]
    for q in range(count):
        total = kept[0, q] + received[0, q].astype(f32)
        if q == 0:
            mine[...] = total
        else:
            sent[count - 1 - q][...] = total.astype(bf16)


def chip_sum_body(place, kept, *refs):
    received, out = refs[:-1], refs[-1]
    total = kept[...]
    for block in received:
        total += block[...].astype(f32)
    out[...] = total.astype(bf16)


def assemble_body(ens, place, *refs):
    pieces, (hidden, out, joined) = refs[:ens], refs[ens:]
    rows, width = hidden.shape
    lanes = width // ens
    strip = 2 * (pieces[0].shape[0] - rows)
    for k, bits in enumerate(routes(ens)):
        source = neighbour(place, bits)
        piece = pieces[k][...].astype(f32)
        hidden[:, pl.ds(pl.multiple_of(source * lanes, lanes), lanes)] = piece[:rows]
        start = pl.multiple_of(source * strip, strip)
        joined[pl.ds(start, strip // 2), :] = piece[rows:, :rows]
        joined[pl.ds(start + strip // 2, strip // 2), :] = piece[rows:, rows:]
    out[...] = joined[: out.shape[0]]


def reduced(
    w_out_t, slope, activated, aggregate_t, dforecast, variables, place, chips,
    link_window, near_window,
):
    ens = len(dforecast)
    mem, grid, width = slope.shape
    rows = width // (2 * chips)
    lanes = width // ens
    strip = 32 * pl.cdiv(variables, 32 * ens)
    aggregate_t = aggregate_t.reshape(chips, 2, rows, -1)
    block = (rows + strip // 2, lanes)
    pair = (2, chips) + block
    flops = mem * grid * width * width

    dpreact, out_part, given = call(
        functools.partial(backward_half_body, ens, chips),
        [((mem * grid, width), bf16), ((ens * strip, width), f32), (pair, bf16)],
        place, w_out_t, slope, activated, aggregate_t, *dforecast,
        flops=flops // 2 + 4 * mem * grid * width * 128,
    )
    leaving = chip_swap(given)
    parts = [link_window(0, dpreact, given)]
    given, token = call(
        functools.partial(leaving_body, ens, chips), [(pair, bf16), ((16, 128), bf16)],
        place, dpreact, out_part, aggregate_t, leaving, after=[parts[0][1]], flops=flops // 2,
    )
    received = core_swap(given, "ens", (1, 2))
    given, kept = call(
        functools.partial(staying_body, ens, chips), [(pair, bf16), (pair, f32)],
        place, dpreact, out_part, aggregate_t, after=[chip_swap(token)], flops=flops,
    )
    staying = chip_swap(given)
    parts += [link_window(m, dpreact, given) for m in range(1, mem)]
    latents_sum = near_window(parts)
    shape = (1, chips) + block
    kept, given = call(
        staying_sum_body, [(shape, f32), (shape, bf16)], place, kept, staying, received,
        after=[daggregate for _, daggregate in parts],
    )
    received = core_swap(given, "ens", (2, 1))
    kept, *given = call(
        chip_slots_body, [(block, f32)] + [(block, bf16)] * (chips - 1), place, kept, received,
        after=[arrived for arrived, _ in parts], flops=5 * 10**9,
    )
    received = [core_swap(given[chips - 1 - q], "chip", (q, q)) for q in range(chips - 1, 0, -1)]
    total = call(chip_sum_body, [(block, bf16)], place, kept, *received, flops=5 * 10**9)[0]
    every = exchanged([total] * ens)
    grad_latents, token = latents_sum(total)
    hidden, out = call(
        functools.partial(assemble_body, ens), [((rows, width), f32), ((variables, rows), f32)],
        place, *every, after=[token], last=True, scratch=[pltpu.VMEM((ens * strip, rows), f32)],
    )
    return grad_latents, hidden, out.T


def reduced_any(aggregate_t, dpreact, out_part, variables):
    part = mul(aggregate_t, dpreact)
    summed = lax.psum((part, out_part[:variables].T), "ens")
    return tuple(
        lax.psum_scatter(value, "space", scatter_dimension=0, tiled=True) for value in summed
    )


def shards(latents, edge_index, edge_weight, truth, w_hidden, output_weight):
    mem, nodes, width = latents.shape
    variables, grid = truth.shape
    ens, space = lax.axis_size("ens"), lax.axis_size("space")
    chips = space // 2
    members = mem * ens
    scale = 1.0 / math.sqrt(grid * space * members)
    e, s = lax.axis_index("ens"), lax.axis_index("space")
    place = jnp.stack([e, s // 2, s % 2]).astype(jnp.int32)
    chunk = grid // ens
    w_out_t = output_weight.T

    on_link = link_swap(latents)
    on_chip = chip_swap(latents)
    rows = 8 * pl.cdiv(variables, 8)
    adjacency, adjacency_t, w_hidden_t, own, w_hidden_here, w_out_here, truth_here = call(
        functools.partial(prepare_body, ens),
        [((grid, 3 * nodes), bf16), ((3 * nodes, grid), bf16), (w_hidden.shape[::-1], bf16)]
        + [(latents.shape, bf16), (w_hidden.shape, bf16)]
        + [((rows, width), bf16), ((rows, grid), f32)],
        place, edge_index.T, edge_weight.T, w_out_t, truth, far=[latents, w_hidden],
        scratch=[pltpu.SemaphoreType.DMA((2,))],
    )
    cells = (mem, grid, width)
    partial = call(partial_body, [(cells, f32)], place, own, on_chip, adjacency)[0]
    piece = (mem * rows, chunk)
    aggregate, preact, activated, *pieces = call(
        functools.partial(forward_body, ens),
        [(cells, bf16), (cells, f32), (cells, bf16)] + [(piece, f32)] * ens,
        place, partial, on_link, adjacency, w_hidden_here, w_out_here,
        flops=2 * mem * grid * width * (nodes + width + 128),
    )
    here = exchanged(pieces)
    slope = call(slope_body, [(cells, f32)], place, preact, after=pieces)[0]
    gradients = call(
        functools.partial(loss_body, ens, scale), [(piece, bf16)] * ens, place, truth_here, *here,
        after=[slope],
    )
    dforecast = exchanged(gradients)
    aggregate_t = call(
        turn_body, [((width, mem * grid), bf16)], place, aggregate, after=gradients
    )[0]
    band = (mem, nodes, width)

    def link_window(m, dpreact, *before):
        given, daggregate = call(
            functools.partial(link_window_body, m), [(band[1:], bf16), (cells[1:], bf16)],
            place, dpreact, w_hidden_t, adjacency_t, after=before,
            flops=2 * grid * width * (width + nodes),
        )
        return link_swap(given), daggregate

    def near_window(parts):
        on_link, daggregates = zip(*parts)
        on_chip, middle = call(
            near_window_body, [(band, bf16), (band, f32)], place, adjacency_t, *daggregates,
            after=on_link[:1], flops=4 * mem * grid * width * nodes,
        )
        on_chip = chip_swap(on_chip)

        def total(*before):
            return call(
                latents_body, [(band, f32), ((8, 128), f32)], place, middle, on_chip, *on_link,
                after=before, last=True,
            )

        return total

    if width % (space * 128) == 0 and width // ens == 2 * (width // space) and ens == 4:
        return reduced(
            w_out_here, slope, activated, aggregate_t, dforecast, variables, place, chips,
            link_window, near_window,
        )
    dpreact, out_part = call(
        functools.partial(backward_body, ens),
        [((mem * grid, width), bf16), ((rows, width), f32)],
        place, w_out_here, slope, activated, *dforecast,
        flops=4 * mem * grid * width * 128,
    )
    grad_latents = near_window([link_window(m, dpreact) for m in range(mem)])()[0]
    return (grad_latents, *reduced_any(aggregate_t, dpreact, out_part, variables))


def solution(mesh):
    placed = (
        P("ens", "space", None),
        P("space", None),
        P("space", None),
        P(None, "space"),
        P(),
        P(),
    )
    return jax.shard_map(
        shards,
        mesh=mesh,
        in_specs=placed,
        out_specs=(P("ens", "space", None), P("space", None), P("space", None)),
        check_vma=False,
    )
```

```python
import functools
import math

import jax
import jax.numpy as jnp
from jax import lax
from jax.experimental import pallas as pl
from jax.experimental.pallas import tpu as pltpu
from jax.sharding import PartitionSpec as P

smoothing = 0.05
f32, bf16 = jnp.float32, jnp.bfloat16
across = (((1,), (0,)), ((), ()))
right_turned = (((1,), (1,)), ((), ()))
left_turned = (((0,), (0,)), ((), ()))


def chip_swap(value):
    count = lax.axis_size("space")
    return lax.ppermute(value, "space", [(i, i ^ 1) for i in range(count)])


def link_swap(value):
    count = lax.axis_size("space")
    pairs = [(i, i + 1) for i in range(1, count - 1, 2)]
    return lax.ppermute(value, "space", pairs + [(j, i) for i, j in pairs])


def core_swap(value, axis, bits):
    ens, space = lax.axis_size("ens"), lax.axis_size("space")

    def partner(e, s):
        bit = bits[s % 2]
        return (e ^ bit) * space + s if axis == "ens" else e * space + (s ^ (2 * bit))

    return lax.ppermute(
        value,
        ("ens", "space"),
        [(e * space + s, partner(e, s)) for e in range(ens) for s in range(space)],
    )


def routes(ens):
    if ens == 4:
        return [(0, 0), (1, 2), (2, 1), (3, 3)]
    return [(k, k) for k in range(ens)]


def exchanged(values):
    others = zip(values[1:], routes(len(values))[1:])
    return [values[0]] + [core_swap(value, "ens", bits) for value, bits in others]


def neighbour(place, bits):
    return place[0] ^ jnp.where(place[2] == 0, bits[0], bits[1])


def mul(a, b, dims=across):
    return lax.dot_general(a, b, dims, preferred_element_type=f32)


def call(body, outs, place, *operands, after=(), far=(), flops=0, last=False, scratch=()):
    vmem = pl.BlockSpec(memory_space=pltpu.VMEM)
    unread = pl.BlockSpec(memory_space=pl.ANY)

    def kernel(place_ref, *refs):
        body(place_ref, *refs[len(after) :])

    return pl.pallas_call(
        kernel,
        out_shape=[
            jax.ShapeDtypeStruct(shape, kind) if last else pltpu.VMEM(shape, kind)
            for shape, kind in outs
        ],
        in_specs=[pl.BlockSpec(memory_space=pltpu.SMEM)]
        + [unread] * len(after)
        + [pl.BlockSpec(memory_space=pltpu.HBM)] * len(far)
        + [vmem] * len(operands),
        out_specs=[vmem] * len(outs),
        scratch_shapes=scratch,
        cost_estimate=pl.CostEstimate(
            flops=flops,
            transcendentals=0,
            bytes_accessed=sum(x.size * x.dtype.itemsize for x in operands)
            + sum(math.prod(shape) * jnp.dtype(kind).itemsize for shape, kind in outs),
        ),
        compiler_params=pltpu.CompilerParams(vmem_limit_bytes=20 * 1024 * 1024),
    )(
        place,
        *after,
        *[pltpu.with_memory_space_constraint(x, pltpu.HBM) for x in far],
        *[pltpu.with_memory_space_constraint(x, pltpu.VMEM) for x in operands],
    )


def sides(core, nodes):
    above, below = 2 * nodes, 0
    return (
        pl.multiple_of(jnp.where(core == 0, above, below), nodes),
        pl.multiple_of(jnp.where(core == 0, below, above), nodes),
    )


def padded(value, rows):
    if value.shape[0] == rows:
        return value
    zeros = jnp.zeros((rows - value.shape[0], value.shape[1]), value.dtype)
    return jnp.concatenate([value, zeros], axis=0)


def prepare_body(
    ens, place, latents, w_hidden, index, weight, w_out_t, truth,
    adjacency, adjacency_t, w_hidden_t, own, w_hidden_here, w_out_here, truth_here, sems
):
    copies = [
        pltpu.make_async_copy(w_hidden, w_hidden_here, sems.at[0]),
        pltpu.make_async_copy(latents, own, sems.at[1]),
    ]
    for copy in copies:
        copy.start()
    edges, grid = index.shape
    chunk = grid // ens
    rows = adjacency_t.shape[0]
    row = lax.broadcasted_iota(jnp.int32, (rows, chunk), 0)
    for k, bits in enumerate(routes(ens)):
        lanes = pl.ds(pl.multiple_of(neighbour(place, bits) * chunk, chunk), chunk)
        nodes = index[:, lanes]
        weights = weight[:, lanes].astype(bf16).astype(f32)
        block = jnp.zeros((rows, chunk), f32)
        for j in range(edges):
            block += jnp.where(nodes[j : j + 1] == row, weights[j : j + 1], 0.0)
        adjacency_t[:, k * chunk : (k + 1) * chunk] = block.astype(bf16)
        adjacency[k * chunk : (k + 1) * chunk, :] = block.T.astype(bf16)
    w_out_here[...] = padded(w_out_t[...].astype(f32), w_out_here.shape[0]).astype(bf16)
    truth_here[...] = padded(truth[...], truth_here.shape[0])
    for copy in copies:
        copy.wait()
    w_hidden_t[...] = w_hidden_here[...].T


def partial_body(place, own, on_chip, adjacency, partial):
    mem, nodes, _ = own.shape
    first, _ = sides(place[2], nodes)
    for m in range(mem):
        total = mul(adjacency[:, nodes : 2 * nodes], own[m])
        partial[m] = total + mul(adjacency[:, pl.ds(first, nodes)], on_chip[m])


def forward_body(
    ens, place, partial, on_link, adjacency, w_hidden, w_out_t, aggregate, preact, activated, *pieces
):
    mem, nodes, width = on_link.shape
    variables = w_out_t.shape[0]
    grid = adjacency.shape[0]
    chunk = grid // ens
    step = 256
    _, second = sides(place[2], nodes)
    for m in range(mem):
        total = partial[m] + mul(adjacency[:, pl.ds(second, nodes)], on_link[m])
        gathered = total.astype(bf16)
        aggregate[m] = gathered
        forecast = jnp.zeros((grid, variables), f32)
        for at in range(0, width, step):
            value = mul(gathered, w_hidden[:, at : at + step])
            preact[m, :, at : at + step] = value
            silu = (value / (1.0 + jnp.exp(-value))).astype(bf16)
            activated[m, :, at : at + step] = silu
            forecast += mul(silu, w_out_t[:, at : at + step], right_turned)
        turned = forecast.T
        for k in range(ens):
            rows = slice(m * variables, (m + 1) * variables)
            pieces[k][rows] = turned[:, k * chunk : (k + 1) * chunk]


def slope_body(place, preact, slope):
    for m in range(preact.shape[0]):
        value = preact[m]
        logistic = 1.0 / (1.0 + jnp.exp(-value))
        slope[m] = logistic * (1.0 + value * (1.0 - logistic))


def turn_body(place, aggregate, aggregate_t):
    mem, grid, _ = aggregate.shape
    for m in range(mem):
        aggregate_t[:, m * grid : (m + 1) * grid] = aggregate[m].T


def loss_body(ens, scale, place, truth, *refs):
    here, out = refs[:ens], refs[ens:]
    rows, chunk = here[0].shape
    mem = rows // truth.shape[0]
    members = mem * ens
    variables = truth.shape[0]
    target = truth[:, pl.ds(pl.multiple_of(place[0] * chunk, chunk), chunk)]
    forecasts = [
        here[k][m * variables : (m + 1) * variables] for k in range(ens) for m in range(mem)
    ]

    def ratio(d):
        return d * lax.rsqrt(d * d + smoothing * smoothing)

    spread = [jnp.zeros_like(target) for _ in forecasts]
    for i in range(members):
        for j in range(i + 1, members):
            term = ratio(forecasts[i] - forecasts[j])
            spread[i] += term
            spread[j] -= term
    gradients = [
        scale
        * (
            ratio(forecasts[i] - target) * (1.0 / members)
            - spread[i] * (1.0 / (members * (members - 1)))
        )
        for i in range(members)
    ]
    for k in range(ens):
        total = jnp.concatenate(gradients[k * mem : (k + 1) * mem], axis=0)
        out[k][...] = total.astype(bf16)


def backward_body(ens, place, w_out_t, slope, activated, *refs):
    dforecast, (dpreact, out_part) = refs[:ens], refs[ens:]
    mem, grid, _ = slope.shape
    variables = w_out_t.shape[0]
    gradients = jnp.concatenate([piece[...] for piece in dforecast], axis=1)
    gradients = gradients.astype(f32)
    out_total = None
    for m in range(mem):
        gradient = gradients[m * variables : (m + 1) * variables].astype(bf16)
        dactivated = mul(gradient, w_out_t[...], left_turned)
        dpreact[m * grid : (m + 1) * grid] = (dactivated * slope[m]).astype(bf16)
        part = mul(gradient, activated[m])
        out_total = part if out_total is None else out_total + part
    out_part[...] = padded(out_total, out_part.shape[0])


def gradient_blocks(ens, chips, core, slots, place, dpreact, out_part, aggregate_t, emit):
    e, chip = place[0], place[1]
    rows = aggregate_t.shape[2]
    lanes = dpreact.shape[1] // ens
    strip = out_part.shape[0] // ens
    half = strip // 2
    left = aggregate_t[:, core].reshape(chips * rows, -1)
    for slot in slots:
        source = e ^ (0, 2 - core, 1 + core, 3)[slot]
        columns = pl.ds(pl.multiple_of(source * lanes, lanes), lanes)
        block = mul(left, dpreact[:, columns])
        start = pl.multiple_of(source * strip, strip)
        for z in range(chips):
            to = z ^ chip
            columns = pl.ds(pl.multiple_of((2 * z + core) * rows, rows), rows)
            upper = out_part[pl.ds(start, half), columns]
            lower = out_part[pl.ds(start + half, half), columns]
            emit(slot, to, slice(0, rows), slice(0, lanes), block[z * rows : (z + 1) * rows])
            emit(slot, to, slice(rows, rows + half), slice(0, rows), upper)
            emit(slot, to, slice(rows, rows + half), slice(rows, lanes), lower)


def backward_half_body(ens, chips, place, w_out_t, slope, activated, aggregate_t, *refs):
    dforecast, (dpreact, out_part, half) = refs[:ens], refs[ens:]
    backward_body(ens, place, w_out_t, slope, activated, *dforecast, dpreact, out_part)

    def emit(slot, to, rows, lanes, value):
        half[slot - 2, to, rows, lanes] = value.astype(bf16)

    core = 1 - place[2]
    gradient_blocks(ens, chips, core, (2, 3), place, dpreact, out_part, aggregate_t, emit)


def staying_body(ens, chips, place, dpreact, out_part, aggregate_t, half, kept):
    def emit_half(slot, to, rows, lanes, value):
        half[slot, to, rows, lanes] = value.astype(bf16)

    def emit_kept(slot, to, rows, lanes, value):
        kept[slot, to, rows, lanes] = value

    operands = place, dpreact, out_part, aggregate_t
    gradient_blocks(ens, chips, 1 - place[2], (0, 1), *operands, emit_half)
    gradient_blocks(ens, chips, place[2], (0, 1), *operands, emit_kept)


def leaving_body(ens, chips, place, dpreact, out_part, aggregate_t, received, sent):
    def emit(slot, to, rows, lanes, value):
        total = value + received[slot - 2, to, rows, lanes].astype(f32)
        sent[slot - 2, to, rows, lanes] = total.astype(bf16)

    core = place[2]
    gradient_blocks(ens, chips, core, (2, 3), place, dpreact, out_part, aggregate_t, emit)


def window_body(place, dpreact, w_hidden_t, adjacency_t, on_link, on_chip, own):
    mem, nodes, _ = own.shape
    grid = adjacency_t.shape[1]
    first = place[2] == 0
    for m in range(mem):
        total = mul(dpreact[m * grid : (m + 1) * grid], w_hidden_t[...]).astype(bf16)
        window = mul(adjacency_t[...], total)
        below, above = window[:nodes], window[2 * nodes :]
        on_link[m] = jnp.where(first, below, above).astype(bf16)
        on_chip[m] = jnp.where(first, above, below).astype(bf16)
        own[m] = window[nodes : 2 * nodes]


def latents_body(place, own, on_chip, on_link, total, token):
    for m in range(own.shape[0]):
        total[m] = own[m] + on_chip[m].astype(f32) + on_link[m].astype(f32)
    token[...] = jnp.zeros_like(token)


def staying_sum_body(place, kept, from_core, from_ens, mine, sent):
    mine[0] = kept[0] + from_core[0].astype(f32) + from_ens[0].astype(f32)
    total = kept[1] + from_core[1].astype(f32) + from_ens[1].astype(f32)
    sent[0] = total.astype(bf16)


def chip_slots_body(place, kept, received, mine, *sent):
    count = kept.shape[1]
    for q in range(count):
        total = kept[0, q] + received[0, q].astype(f32)
        if q == 0:
            mine[...] = total
        else:
            sent[count - 1 - q][...] = total.astype(bf16)


def chip_sum_body(place, kept, *refs):
    received, out = refs[:-1], refs[-1]
    total = kept[...]
    for block in received:
        total += block[...].astype(f32)
    out[...] = total.astype(bf16)


def assemble_body(ens, place, *refs):
    pieces, (hidden, out, joined) = refs[:ens], refs[ens:]
    rows, width = hidden.shape
    lanes = width // ens
    strip = 2 * (pieces[0].shape[0] - rows)
    for k, bits in enumerate(routes(ens)):
        source = neighbour(place, bits)
        piece = pieces[k][...].astype(f32)
        hidden[:, pl.ds(pl.multiple_of(source * lanes, lanes), lanes)] = piece[:rows]
        start = pl.multiple_of(source * strip, strip)
        joined[pl.ds(start, strip // 2), :] = piece[rows:, :rows]
        joined[pl.ds(start + strip // 2, strip // 2), :] = piece[rows:, rows:]
    out[...] = joined[: out.shape[0]]


def reduced(w_out_t, slope, activated, aggregate_t, dforecast, variables, place, chips, window):
    ens = len(dforecast)
    mem, grid, width = slope.shape
    rows = width // (2 * chips)
    lanes = width // ens
    strip = 32 * pl.cdiv(variables, 32 * ens)
    aggregate_t = aggregate_t.reshape(chips, 2, rows, -1)
    block = (rows + strip // 2, lanes)
    pair = (2, chips) + block
    flops = mem * grid * width * width

    dpreact, out_part, given = call(
        functools.partial(backward_half_body, ens, chips),
        [((mem * grid, width), bf16), ((ens * strip, width), f32), (pair, bf16)],
        place, w_out_t, slope, activated, aggregate_t, *dforecast,
        flops=flops // 2 + 4 * mem * grid * width * 128,
    )
    leaving = chip_swap(given)
    given, kept = call(
        functools.partial(staying_body, ens, chips), [(pair, bf16), (pair, f32)],
        place, dpreact, out_part, aggregate_t, flops=flops,
    )
    staying = chip_swap(given)
    given = call(
        functools.partial(leaving_body, ens, chips), [(pair, bf16)],
        place, dpreact, out_part, aggregate_t, leaving, after=[kept], flops=flops // 2,
    )[0]
    received = core_swap(given, "ens", (1, 2))
    latents_sum = window(dpreact, given)
    shape = (1, chips) + block
    kept, given = call(
        staying_sum_body, [(shape, f32), (shape, bf16)], place, kept, staying, received
    )
    received = core_swap(given, "ens", (2, 1))
    kept, *given = call(
        chip_slots_body, [(block, f32)] + [(block, bf16)] * (chips - 1), place, kept, received,
        flops=10**9,
    )
    received = [core_swap(given[chips - 1 - q], "chip", (q, q)) for q in range(chips - 1, 0, -1)]
    total = call(chip_sum_body, [(block, bf16)], place, kept, *received, flops=10**9)[0]
    every = exchanged([total] * ens)
    grad_latents, token = latents_sum(total)
    hidden, out = call(
        functools.partial(assemble_body, ens), [((rows, width), f32), ((variables, rows), f32)],
        place, *every, after=[token], last=True, scratch=[pltpu.VMEM((ens * strip, rows), f32)],
    )
    return grad_latents, hidden, out.T


def reduced_any(aggregate_t, dpreact, out_part, variables):
    part = mul(aggregate_t, dpreact)
    summed = lax.psum((part, out_part[:variables].T), "ens")
    return tuple(
        lax.psum_scatter(value, "space", scatter_dimension=0, tiled=True) for value in summed
    )


def shards(latents, edge_index, edge_weight, truth, w_hidden, output_weight):
    mem, nodes, width = latents.shape
    variables, grid = truth.shape
    ens, space = lax.axis_size("ens"), lax.axis_size("space")
    chips = space // 2
    members = mem * ens
    scale = 1.0 / math.sqrt(grid * space * members)
    e, s = lax.axis_index("ens"), lax.axis_index("space")
    place = jnp.stack([e, s // 2, s % 2]).astype(jnp.int32)
    chunk = grid // ens
    w_out_t = output_weight.T

    on_link = link_swap(latents)
    on_chip = chip_swap(latents)
    rows = 8 * pl.cdiv(variables, 8)
    adjacency, adjacency_t, w_hidden_t, own, w_hidden_here, w_out_here, truth_here = call(
        functools.partial(prepare_body, ens),
        [((grid, 3 * nodes), bf16), ((3 * nodes, grid), bf16), (w_hidden.shape[::-1], bf16)]
        + [(latents.shape, bf16), (w_hidden.shape, bf16)]
        + [((rows, width), bf16), ((rows, grid), f32)],
        place, edge_index.T, edge_weight.T, w_out_t, truth, far=[latents, w_hidden],
        scratch=[pltpu.SemaphoreType.DMA((2,))],
    )
    cells = (mem, grid, width)
    partial = call(partial_body, [(cells, f32)], place, own, on_chip, adjacency)[0]
    piece = (mem * rows, chunk)
    aggregate, preact, activated, *pieces = call(
        functools.partial(forward_body, ens),
        [(cells, bf16), (cells, f32), (cells, bf16)] + [(piece, f32)] * ens,
        place, partial, on_link, adjacency, w_hidden_here, w_out_here,
        flops=2 * mem * grid * width * (nodes + width + 128),
    )
    here = exchanged(pieces)
    slope = call(slope_body, [(cells, f32)], place, preact, after=pieces)[0]
    gradients = call(
        functools.partial(loss_body, ens, scale), [(piece, bf16)] * ens, place, truth_here, *here,
        after=[slope],
    )
    dforecast = exchanged(gradients)
    aggregate_t = call(
        turn_body, [((width, mem * grid), bf16)], place, aggregate, after=gradients
    )[0]
    band = (mem, nodes, width)

    def window(dpreact, *before):
        on_link, on_chip, middle = call(
            window_body, [(band, bf16)] * 2 + [(band, f32)],
            place, dpreact, w_hidden_t, adjacency_t, after=before,
            flops=2 * mem * grid * width * (width + 3 * nodes),
        )
        on_link, on_chip = link_swap(on_link), chip_swap(on_chip)

        def total(*before):
            return call(
                latents_body, [(band, f32), ((8, 128), f32)], place, middle, on_chip, on_link,
                after=before, last=True,
            )

        return total

    if width % (space * 128) == 0 and width // ens == 2 * (width // space) and ens == 4:
        return reduced(
            w_out_here, slope, activated, aggregate_t, dforecast, variables, place, chips, window
        )
    dpreact, out_part = call(
        functools.partial(backward_body, ens),
        [((mem * grid, width), bf16), ((rows, width), f32)],
        place, w_out_here, slope, activated, *dforecast,
        flops=4 * mem * grid * width * 128,
    )
    return (window(dpreact)()[0], *reduced_any(aggregate_t, dpreact, out_part, variables))


def solution(mesh):
    placed = (
        P("ens", "space", None),
        P("space", None),
        P("space", None),
        P(None, "space"),
        P(),
        P(),
    )
    return jax.shard_map(
        shards,
        mesh=mesh,
        in_specs=placed,
        out_specs=(P("ens", "space", None), P("space", None), P("space", None)),
        check_vma=False,
    )
```

```python
import functools
import math

import jax
import jax.numpy as jnp
from jax import lax
from jax.experimental import pallas as pl
from jax.experimental.pallas import tpu as pltpu
from jax.sharding import PartitionSpec as P

smoothing = 0.05
f32, bf16 = jnp.float32, jnp.bfloat16
across = (((1,), (0,)), ((), ()))
right_turned = (((1,), (1,)), ((), ()))
left_turned = (((0,), (0,)), ((), ()))


def chip_swap(value):
    count = lax.axis_size("space")
    return lax.ppermute(value, "space", [(i, i ^ 1) for i in range(count)])


def link_swap(value):
    count = lax.axis_size("space")
    pairs = [(i, i + 1) for i in range(1, count - 1, 2)]
    return lax.ppermute(value, "space", pairs + [(j, i) for i, j in pairs])


def core_swap(value, axis, bits):
    ens, space = lax.axis_size("ens"), lax.axis_size("space")

    def partner(e, s):
        bit = bits[s % 2]
        return (e ^ bit) * space + s if axis == "ens" else e * space + (s ^ (2 * bit))

    return lax.ppermute(
        value,
        ("ens", "space"),
        [(e * space + s, partner(e, s)) for e in range(ens) for s in range(space)],
    )


def routes(ens):
    if ens == 4:
        return [(0, 0), (1, 2), (2, 1), (3, 3)]
    return [(k, k) for k in range(ens)]


def exchanged(values):
    others = zip(values[1:], routes(len(values))[1:])
    return [values[0]] + [core_swap(value, "ens", bits) for value, bits in others]


def neighbour(place, bits):
    return place[0] ^ jnp.where(place[2] == 0, bits[0], bits[1])


def mul(a, b, dims=across):
    return lax.dot_general(a, b, dims, preferred_element_type=f32)


def call(body, outs, place, *operands, after=(), far=(), flops=0, last=False, scratch=()):
    vmem = pl.BlockSpec(memory_space=pltpu.VMEM)
    unread = pl.BlockSpec(memory_space=pl.ANY)

    def kernel(place_ref, *refs):
        body(place_ref, *refs[len(after) :])

    return pl.pallas_call(
        kernel,
        out_shape=[
            jax.ShapeDtypeStruct(shape, kind) if last else pltpu.VMEM(shape, kind)
            for shape, kind in outs
        ],
        in_specs=[pl.BlockSpec(memory_space=pltpu.SMEM)]
        + [unread] * len(after)
        + [pl.BlockSpec(memory_space=pltpu.HBM)] * len(far)
        + [vmem] * len(operands),
        out_specs=[vmem] * len(outs),
        scratch_shapes=scratch,
        cost_estimate=pl.CostEstimate(
            flops=flops,
            transcendentals=0,
            bytes_accessed=sum(x.size * x.dtype.itemsize for x in operands)
            + sum(math.prod(shape) * jnp.dtype(kind).itemsize for shape, kind in outs),
        ),
        compiler_params=pltpu.CompilerParams(vmem_limit_bytes=20 * 1024 * 1024),
    )(
        place,
        *after,
        *[pltpu.with_memory_space_constraint(x, pltpu.HBM) for x in far],
        *[pltpu.with_memory_space_constraint(x, pltpu.VMEM) for x in operands],
    )


def sides(core, nodes):
    above, below = 2 * nodes, 0
    return (
        pl.multiple_of(jnp.where(core == 0, above, below), nodes),
        pl.multiple_of(jnp.where(core == 0, below, above), nodes),
    )


def padded(value, rows):
    if value.shape[0] == rows:
        return value
    zeros = jnp.zeros((rows - value.shape[0], value.shape[1]), value.dtype)
    return jnp.concatenate([value, zeros], axis=0)


def prepare_body(
    ens, place, latents, w_hidden, index, weight, w_out_t, truth,
    adjacency, adjacency_t, w_hidden_t, own, w_hidden_here, w_out_here, truth_here, sems
):
    copies = [
        pltpu.make_async_copy(w_hidden, w_hidden_here, sems.at[0]),
        pltpu.make_async_copy(latents, own, sems.at[1]),
    ]
    for copy in copies:
        copy.start()
    edges, grid = index.shape
    chunk = grid // ens
    rows = adjacency_t.shape[0]
    row = lax.broadcasted_iota(jnp.int32, (rows, chunk), 0)
    for k, bits in enumerate(routes(ens)):
        lanes = pl.ds(pl.multiple_of(neighbour(place, bits) * chunk, chunk), chunk)
        nodes = index[:, lanes]
        weights = weight[:, lanes].astype(bf16).astype(f32)
        block = jnp.zeros((rows, chunk), f32)
        for j in range(edges):
            block += jnp.where(nodes[j : j + 1] == row, weights[j : j + 1], 0.0)
        adjacency_t[:, k * chunk : (k + 1) * chunk] = block.astype(bf16)
        adjacency[k * chunk : (k + 1) * chunk, :] = block.T.astype(bf16)
    w_out_here[...] = padded(w_out_t[...].astype(f32), w_out_here.shape[0]).astype(bf16)
    truth_here[...] = padded(truth[...], truth_here.shape[0])
    for copy in copies:
        copy.wait()
    w_hidden_t[...] = w_hidden_here[...].T


def partial_body(place, own, on_chip, adjacency, partial):
    mem, nodes, _ = own.shape
    first, _ = sides(place[2], nodes)
    for m in range(mem):
        total = mul(adjacency[:, nodes : 2 * nodes], own[m])
        partial[m] = total + mul(adjacency[:, pl.ds(first, nodes)], on_chip[m])


def forward_body(
    ens, place, partial, on_link, adjacency, w_hidden, w_out_t, aggregate, preact, activated, *pieces
):
    mem, nodes, width = on_link.shape
    variables = w_out_t.shape[0]
    grid = adjacency.shape[0]
    chunk = grid // ens
    step = 256
    _, second = sides(place[2], nodes)
    for m in range(mem):
        total = partial[m] + mul(adjacency[:, pl.ds(second, nodes)], on_link[m])
        gathered = total.astype(bf16)
        aggregate[m] = gathered
        forecast = jnp.zeros((grid, variables), f32)
        for at in range(0, width, step):
            value = mul(gathered, w_hidden[:, at : at + step])
            preact[m, :, at : at + step] = value
            silu = (value / (1.0 + jnp.exp(-value))).astype(bf16)
            activated[m, :, at : at + step] = silu
            forecast += mul(silu, w_out_t[:, at : at + step], right_turned)
        turned = forecast.T
        for k in range(ens):
            rows = slice(m * variables, (m + 1) * variables)
            pieces[k][rows] = turned[:, k * chunk : (k + 1) * chunk]


def slope_body(place, preact, slope):
    for m in range(preact.shape[0]):
        value = preact[m]
        logistic = 1.0 / (1.0 + jnp.exp(-value))
        slope[m] = logistic * (1.0 + value * (1.0 - logistic))


def turn_body(place, aggregate, aggregate_t):
    mem, grid, _ = aggregate.shape
    for m in range(mem):
        aggregate_t[:, m * grid : (m + 1) * grid] = aggregate[m].T


def loss_body(ens, scale, place, truth, *refs):
    here, out = refs[:ens], refs[ens:]
    rows, chunk = here[0].shape
    mem = rows // truth.shape[0]
    members = mem * ens
    variables = truth.shape[0]
    target = truth[:, pl.ds(pl.multiple_of(place[0] * chunk, chunk), chunk)]
    forecasts = [
        here[k][m * variables : (m + 1) * variables] for k in range(ens) for m in range(mem)
    ]

    def ratio(d):
        return d * lax.rsqrt(d * d + smoothing * smoothing)

    spread = [jnp.zeros_like(target) for _ in forecasts]
    for i in range(members):
        for j in range(i + 1, members):
            term = ratio(forecasts[i] - forecasts[j])
            spread[i] += term
            spread[j] -= term
    gradients = [
        scale
        * (
            ratio(forecasts[i] - target) * (1.0 / members)
            - spread[i] * (1.0 / (members * (members - 1)))
        )
        for i in range(members)
    ]
    for k in range(ens):
        total = jnp.concatenate(gradients[k * mem : (k + 1) * mem], axis=0)
        out[k][...] = total.astype(bf16)


def backward_body(ens, place, w_out_t, slope, activated, *refs):
    dforecast, (dpreact, out_part) = refs[:ens], refs[ens:]
    mem, grid, _ = slope.shape
    variables = w_out_t.shape[0]
    gradients = jnp.concatenate([piece[...] for piece in dforecast], axis=1)
    gradients = gradients.astype(f32)
    out_total = None
    for m in range(mem):
        gradient = gradients[m * variables : (m + 1) * variables].astype(bf16)
        dactivated = mul(gradient, w_out_t[...], left_turned)
        dpreact[m * grid : (m + 1) * grid] = (dactivated * slope[m]).astype(bf16)
        part = mul(gradient, activated[m])
        out_total = part if out_total is None else out_total + part
    out_part[...] = padded(out_total, out_part.shape[0])


def gradient_blocks(ens, chips, core, slots, place, dpreact, out_part, aggregate_t, emit):
    e, chip = place[0], place[1]
    rows = aggregate_t.shape[2]
    lanes = dpreact.shape[1] // ens
    strip = out_part.shape[0] // ens
    half = strip // 2
    left = aggregate_t[:, core].reshape(chips * rows, -1)
    for slot in slots:
        source = e ^ (0, 2 - core, 1 + core, 3)[slot]
        columns = pl.ds(pl.multiple_of(source * lanes, lanes), lanes)
        block = mul(left, dpreact[:, columns])
        start = pl.multiple_of(source * strip, strip)
        for z in range(chips):
            to = z ^ chip
            columns = pl.ds(pl.multiple_of((2 * z + core) * rows, rows), rows)
            upper = out_part[pl.ds(start, half), columns]
            lower = out_part[pl.ds(start + half, half), columns]
            emit(slot, to, slice(0, rows), slice(0, lanes), block[z * rows : (z + 1) * rows])
            emit(slot, to, slice(rows, rows + half), slice(0, rows), upper)
            emit(slot, to, slice(rows, rows + half), slice(rows, lanes), lower)


def backward_half_body(ens, chips, place, w_out_t, slope, activated, aggregate_t, *refs):
    dforecast, (dpreact, out_part, half) = refs[:ens], refs[ens:]
    backward_body(ens, place, w_out_t, slope, activated, *dforecast, dpreact, out_part)

    def emit(slot, to, rows, lanes, value):
        half[slot - 2, to, rows, lanes] = value.astype(bf16)

    core = 1 - place[2]
    gradient_blocks(ens, chips, core, (2, 3), place, dpreact, out_part, aggregate_t, emit)


def staying_body(ens, chips, place, dpreact, out_part, aggregate_t, half, kept):
    def emit_half(slot, to, rows, lanes, value):
        half[slot, to, rows, lanes] = value.astype(bf16)

    def emit_kept(slot, to, rows, lanes, value):
        kept[slot, to, rows, lanes] = value

    operands = place, dpreact, out_part, aggregate_t
    gradient_blocks(ens, chips, 1 - place[2], (0, 1), *operands, emit_half)
    gradient_blocks(ens, chips, place[2], (0, 1), *operands, emit_kept)


def leaving_body(ens, chips, place, dpreact, out_part, aggregate_t, received, sent):
    def emit(slot, to, rows, lanes, value):
        total = value + received[slot - 2, to, rows, lanes].astype(f32)
        sent[slot - 2, to, rows, lanes] = total.astype(bf16)

    core = place[2]
    gradient_blocks(ens, chips, core, (2, 3), place, dpreact, out_part, aggregate_t, emit)


def window_body(place, dpreact, w_hidden_t, adjacency_t, on_link, on_chip, own):
    mem, nodes, width = own.shape
    grid = adjacency_t.shape[1]
    step = 256
    first, second = sides(place[2], nodes)
    for m in range(mem):
        for at in range(0, width, step):
            lanes = slice(at, at + step)
            total = mul(dpreact[m * grid : (m + 1) * grid], w_hidden_t[:, lanes]).astype(bf16)
            on_link[m, :, lanes] = mul(adjacency_t[pl.ds(second, nodes)], total).astype(bf16)
            on_chip[m, :, lanes] = mul(adjacency_t[pl.ds(first, nodes)], total).astype(bf16)
            own[m, :, lanes] = mul(adjacency_t[nodes : 2 * nodes], total)


def latents_body(place, own, on_chip, on_link, total, token):
    for m in range(own.shape[0]):
        total[m] = own[m] + on_chip[m].astype(f32) + on_link[m].astype(f32)
    token[...] = jnp.zeros_like(token)


def staying_sum_body(place, kept, from_core, from_ens, mine, sent):
    mine[0] = kept[0] + from_core[0].astype(f32) + from_ens[0].astype(f32)
    total = kept[1] + from_core[1].astype(f32) + from_ens[1].astype(f32)
    sent[0] = total.astype(bf16)


def chip_slots_body(place, kept, received, mine, *sent):
    count = kept.shape[1]
    for q in range(count):
        total = kept[0, q] + received[0, q].astype(f32)
        if q == 0:
            mine[...] = total
        else:
            sent[count - 1 - q][...] = total.astype(bf16)


def chip_sum_body(place, kept, *refs):
    received, out = refs[:-1], refs[-1]
    total = kept[...]
    for block in received:
        total += block[...].astype(f32)
    out[...] = total.astype(bf16)


def assemble_body(ens, place, *refs):
    pieces, (hidden, out, joined) = refs[:ens], refs[ens:]
    rows, width = hidden.shape
    lanes = width // ens
    strip = 2 * (pieces[0].shape[0] - rows)
    for k, bits in enumerate(routes(ens)):
        source = neighbour(place, bits)
        piece = pieces[k][...].astype(f32)
        hidden[:, pl.ds(pl.multiple_of(source * lanes, lanes), lanes)] = piece[:rows]
        start = pl.multiple_of(source * strip, strip)
        joined[pl.ds(start, strip // 2), :] = piece[rows:, :rows]
        joined[pl.ds(start + strip // 2, strip // 2), :] = piece[rows:, rows:]
    out[...] = joined[: out.shape[0]]


def reduced(w_out_t, slope, activated, aggregate_t, dforecast, variables, place, chips, window):
    ens = len(dforecast)
    mem, grid, width = slope.shape
    rows = width // (2 * chips)
    lanes = width // ens
    strip = 32 * pl.cdiv(variables, 32 * ens)
    aggregate_t = aggregate_t.reshape(chips, 2, rows, -1)
    block = (rows + strip // 2, lanes)
    pair = (2, chips) + block
    flops = mem * grid * width * width

    dpreact, out_part, given = call(
        functools.partial(backward_half_body, ens, chips),
        [((mem * grid, width), bf16), ((ens * strip, width), f32), (pair, bf16)],
        place, w_out_t, slope, activated, aggregate_t, *dforecast,
        flops=flops // 2 + 4 * mem * grid * width * 128,
    )
    leaving = chip_swap(given)
    given, kept = call(
        functools.partial(staying_body, ens, chips), [(pair, bf16), (pair, f32)],
        place, dpreact, out_part, aggregate_t, flops=flops,
    )
    staying = chip_swap(given)
    given = call(
        functools.partial(leaving_body, ens, chips), [(pair, bf16)],
        place, dpreact, out_part, aggregate_t, leaving, after=[kept], flops=flops // 2,
    )[0]
    received = core_swap(given, "ens", (1, 2))
    latents_sum = window(dpreact, given)
    shape = (1, chips) + block
    kept, given = call(
        staying_sum_body, [(shape, f32), (shape, bf16)], place, kept, staying, received
    )
    received = core_swap(given, "ens", (2, 1))
    kept, *given = call(
        chip_slots_body, [(block, f32)] + [(block, bf16)] * (chips - 1), place, kept, received,
        flops=10**9,
    )
    received = [core_swap(given[chips - 1 - q], "chip", (q, q)) for q in range(chips - 1, 0, -1)]
    total = call(chip_sum_body, [(block, bf16)], place, kept, *received, flops=10**9)[0]
    every = exchanged([total] * ens)
    grad_latents, token = latents_sum(total)
    hidden, out = call(
        functools.partial(assemble_body, ens), [((rows, width), f32), ((variables, rows), f32)],
        place, *every, after=[token], last=True, scratch=[pltpu.VMEM((ens * strip, rows), f32)],
    )
    return grad_latents, hidden, out.T


def reduced_any(aggregate_t, dpreact, out_part, variables):
    part = mul(aggregate_t, dpreact)
    summed = lax.psum((part, out_part[:variables].T), "ens")
    return tuple(
        lax.psum_scatter(value, "space", scatter_dimension=0, tiled=True) for value in summed
    )


def shards(latents, edge_index, edge_weight, truth, w_hidden, output_weight):
    mem, nodes, width = latents.shape
    variables, grid = truth.shape
    ens, space = lax.axis_size("ens"), lax.axis_size("space")
    chips = space // 2
    members = mem * ens
    scale = 1.0 / math.sqrt(grid * space * members)
    e, s = lax.axis_index("ens"), lax.axis_index("space")
    place = jnp.stack([e, s // 2, s % 2]).astype(jnp.int32)
    chunk = grid // ens
    w_out_t = output_weight.T

    on_link = link_swap(latents)
    on_chip = chip_swap(latents)
    rows = 8 * pl.cdiv(variables, 8)
    adjacency, adjacency_t, w_hidden_t, own, w_hidden_here, w_out_here, truth_here = call(
        functools.partial(prepare_body, ens),
        [((grid, 3 * nodes), bf16), ((3 * nodes, grid), bf16), (w_hidden.shape[::-1], bf16)]
        + [(latents.shape, bf16), (w_hidden.shape, bf16)]
        + [((rows, width), bf16), ((rows, grid), f32)],
        place, edge_index.T, edge_weight.T, w_out_t, truth, far=[latents, w_hidden],
        scratch=[pltpu.SemaphoreType.DMA((2,))],
    )
    cells = (mem, grid, width)
    partial = call(partial_body, [(cells, f32)], place, own, on_chip, adjacency)[0]
    piece = (mem * rows, chunk)
    aggregate, preact, activated, *pieces = call(
        functools.partial(forward_body, ens),
        [(cells, bf16), (cells, f32), (cells, bf16)] + [(piece, f32)] * ens,
        place, partial, on_link, adjacency, w_hidden_here, w_out_here,
        flops=2 * mem * grid * width * (nodes + width + 128),
    )
    here = exchanged(pieces)
    slope = call(slope_body, [(cells, f32)], place, preact, after=pieces)[0]
    gradients = call(
        functools.partial(loss_body, ens, scale), [(piece, bf16)] * ens, place, truth_here, *here,
        after=[slope],
    )
    dforecast = exchanged(gradients)
    aggregate_t = call(
        turn_body, [((width, mem * grid), bf16)], place, aggregate, after=gradients
    )[0]
    band = (mem, nodes, width)

    def window(dpreact, *before):
        on_link, on_chip, middle = call(
            window_body, [(band, bf16)] * 2 + [(band, f32)],
            place, dpreact, w_hidden_t, adjacency_t, after=before,
            flops=2 * mem * grid * width * (width + 3 * nodes),
        )
        on_link, on_chip = link_swap(on_link), chip_swap(on_chip)

        def total(*before):
            return call(
                latents_body, [(band, f32), ((8, 128), f32)], place, middle, on_chip, on_link,
                after=before, last=True,
            )

        return total

    if width % (space * 128) == 0 and width // ens == 2 * (width // space) and ens == 4:
        return reduced(
            w_out_here, slope, activated, aggregate_t, dforecast, variables, place, chips, window
        )
    dpreact, out_part = call(
        functools.partial(backward_body, ens),
        [((mem * grid, width), bf16), ((rows, width), f32)],
        place, w_out_here, slope, activated, *dforecast,
        flops=4 * mem * grid * width * 128,
    )
    return (window(dpreact)()[0], *reduced_any(aggregate_t, dpreact, out_part, variables))


def solution(mesh):
    placed = (
        P("ens", "space", None),
        P("space", None),
        P("space", None),
        P(None, "space"),
        P(),
        P(),
    )
    return jax.shard_map(
        shards,
        mesh=mesh,
        in_specs=placed,
        out_specs=(P("ens", "space", None), P("space", None), P("space", None)),
        check_vma=False,
    )
```

```python
import functools
import math

import jax
import jax.numpy as jnp
from jax import lax
from jax.experimental import pallas as pl
from jax.experimental.pallas import tpu as pltpu
from jax.sharding import PartitionSpec as P

smoothing = 0.05
f32, bf16 = jnp.float32, jnp.bfloat16
across = (((1,), (0,)), ((), ()))
right_turned = (((1,), (1,)), ((), ()))
left_turned = (((0,), (0,)), ((), ()))


def chip_swap(value):
    count = lax.axis_size("space")
    return lax.ppermute(value, "space", [(i, i ^ 1) for i in range(count)])


def link_swap(value):
    count = lax.axis_size("space")
    pairs = [(i, i + 1) for i in range(1, count - 1, 2)]
    return lax.ppermute(value, "space", pairs + [(j, i) for i, j in pairs])


def core_swap(value, axis, bits):
    ens, space = lax.axis_size("ens"), lax.axis_size("space")

    def partner(e, s):
        bit = bits[s % 2]
        return (e ^ bit) * space + s if axis == "ens" else e * space + (s ^ (2 * bit))

    return lax.ppermute(
        value,
        ("ens", "space"),
        [(e * space + s, partner(e, s)) for e in range(ens) for s in range(space)],
    )


def routes(ens):
    if ens == 4:
        return [(0, 0), (1, 2), (2, 1), (3, 3)]
    return [(k, k) for k in range(ens)]


def exchanged(values):
    others = zip(values[1:], routes(len(values))[1:])
    return [values[0]] + [core_swap(value, "ens", bits) for value, bits in others]


def neighbour(place, bits):
    return place[0] ^ jnp.where(place[2] == 0, bits[0], bits[1])


def mul(a, b, dims=across):
    return lax.dot_general(a, b, dims, preferred_element_type=f32)


def call(body, outs, place, *operands, after=(), far=(), flops=0, last=False, scratch=()):
    vmem = pl.BlockSpec(memory_space=pltpu.VMEM)
    unread = pl.BlockSpec(memory_space=pl.ANY)

    def kernel(place_ref, *refs):
        body(place_ref, *refs[len(after) :])

    return pl.pallas_call(
        kernel,
        out_shape=[
            jax.ShapeDtypeStruct(shape, kind) if last else pltpu.VMEM(shape, kind)
            for shape, kind in outs
        ],
        in_specs=[pl.BlockSpec(memory_space=pltpu.SMEM)]
        + [unread] * len(after)
        + [pl.BlockSpec(memory_space=pltpu.HBM)] * len(far)
        + [vmem] * len(operands),
        out_specs=[vmem] * len(outs),
        scratch_shapes=scratch,
        cost_estimate=pl.CostEstimate(
            flops=flops,
            transcendentals=0,
            bytes_accessed=sum(x.size * x.dtype.itemsize for x in operands)
            + sum(math.prod(shape) * jnp.dtype(kind).itemsize for shape, kind in outs),
        ),
        compiler_params=pltpu.CompilerParams(vmem_limit_bytes=20 * 1024 * 1024),
    )(
        place,
        *after,
        *[pltpu.with_memory_space_constraint(x, pltpu.HBM) for x in far],
        *[pltpu.with_memory_space_constraint(x, pltpu.VMEM) for x in operands],
    )


def sides(core, nodes):
    above, below = 2 * nodes, 0
    return (
        pl.multiple_of(jnp.where(core == 0, above, below), nodes),
        pl.multiple_of(jnp.where(core == 0, below, above), nodes),
    )


def padded(value, rows):
    if value.shape[0] == rows:
        return value
    zeros = jnp.zeros((rows - value.shape[0], value.shape[1]), value.dtype)
    return jnp.concatenate([value, zeros], axis=0)


def prepare_body(
    ens, place, latents, w_hidden, index, weight, w_out_t, truth,
    adjacency, adjacency_t, w_hidden_t, own, w_hidden_here, w_out_here, truth_here, sems
):
    copies = [
        pltpu.make_async_copy(w_hidden, w_hidden_here, sems.at[0]),
        pltpu.make_async_copy(latents, own, sems.at[1]),
    ]
    for copy in copies:
        copy.start()
    edges, grid = index.shape
    chunk = grid // ens
    rows = adjacency_t.shape[0]
    row = lax.broadcasted_iota(jnp.int32, (rows, chunk), 0)
    for k, bits in enumerate(routes(ens)):
        lanes = pl.ds(pl.multiple_of(neighbour(place, bits) * chunk, chunk), chunk)
        nodes = index[:, lanes]
        weights = weight[:, lanes].astype(bf16).astype(f32)
        block = jnp.zeros((rows, chunk), f32)
        for j in range(edges):
            block += jnp.where(nodes[j : j + 1] == row, weights[j : j + 1], 0.0)
        adjacency_t[:, k * chunk : (k + 1) * chunk] = block.astype(bf16)
        adjacency[k * chunk : (k + 1) * chunk, :] = block.T.astype(bf16)
    w_out_here[...] = padded(w_out_t[...].astype(f32), w_out_here.shape[0]).astype(bf16)
    truth_here[...] = padded(truth[...], truth_here.shape[0])
    for copy in copies:
        copy.wait()
    w_hidden_t[...] = w_hidden_here[...].T


def partial_body(place, own, on_chip, adjacency, partial):
    mem, nodes, _ = own.shape
    first, _ = sides(place[2], nodes)
    for m in range(mem):
        total = mul(adjacency[:, nodes : 2 * nodes], own[m])
        partial[m] = total + mul(adjacency[:, pl.ds(first, nodes)], on_chip[m])


def forward_body(
    ens, place, partial, on_link, adjacency, w_hidden, w_out_t, aggregate, preact, activated, *pieces
):
    mem, nodes, width = on_link.shape
    variables = w_out_t.shape[0]
    grid = adjacency.shape[0]
    chunk = grid // ens
    step = 512
    _, second = sides(place[2], nodes)
    for m in range(mem):
        total = partial[m] + mul(adjacency[:, pl.ds(second, nodes)], on_link[m])
        gathered = total.astype(bf16)
        aggregate[m] = gathered
        forecast = jnp.zeros((grid, variables), f32)
        for at in range(0, width, step):
            value = mul(gathered, w_hidden[:, at : at + step])
            preact[m, :, at : at + step] = value
            silu = (value / (1.0 + jnp.exp(-value))).astype(bf16)
            activated[m, :, at : at + step] = silu
            forecast += mul(silu, w_out_t[:, at : at + step], right_turned)
        turned = forecast.T
        for k in range(ens):
            rows = slice(m * variables, (m + 1) * variables)
            pieces[k][rows] = turned[:, k * chunk : (k + 1) * chunk]


def slope_body(place, preact, slope):
    for m in range(preact.shape[0]):
        value = preact[m]
        logistic = 1.0 / (1.0 + jnp.exp(-value))
        slope[m] = logistic * (1.0 + value * (1.0 - logistic))


def turn_body(place, aggregate, aggregate_t):
    mem, grid, _ = aggregate.shape
    for m in range(mem):
        aggregate_t[:, m * grid : (m + 1) * grid] = aggregate[m].T


def loss_body(ens, scale, place, truth, *refs):
    here, out = refs[:ens], refs[ens:]
    rows, chunk = here[0].shape
    mem = rows // truth.shape[0]
    members = mem * ens
    variables = truth.shape[0]
    target = truth[:, pl.ds(pl.multiple_of(place[0] * chunk, chunk), chunk)]
    forecasts = [
        here[k][m * variables : (m + 1) * variables] for k in range(ens) for m in range(mem)
    ]

    def ratio(d):
        return d * lax.rsqrt(d * d + smoothing * smoothing)

    spread = [jnp.zeros_like(target) for _ in forecasts]
    for i in range(members):
        for j in range(i + 1, members):
            term = ratio(forecasts[i] - forecasts[j])
            spread[i] += term
            spread[j] -= term
    gradients = [
        scale
        * (
            ratio(forecasts[i] - target) * (1.0 / members)
            - spread[i] * (1.0 / (members * (members - 1)))
        )
        for i in range(members)
    ]
    for k in range(ens):
        total = jnp.concatenate(gradients[k * mem : (k + 1) * mem], axis=0)
        out[k][...] = total.astype(bf16)


def backward_body(ens, place, w_out_t, slope, activated, *refs):
    dforecast, (dpreact, out_part) = refs[:ens], refs[ens:]
    mem, grid, _ = slope.shape
    variables = w_out_t.shape[0]
    gradients = jnp.concatenate([piece[...] for piece in dforecast], axis=1)
    gradients = gradients.astype(f32)
    out_total = None
    for m in range(mem):
        gradient = gradients[m * variables : (m + 1) * variables].astype(bf16)
        dactivated = mul(gradient, w_out_t[...], left_turned)
        dpreact[m * grid : (m + 1) * grid] = (dactivated * slope[m]).astype(bf16)
        part = mul(gradient, activated[m])
        out_total = part if out_total is None else out_total + part
    out_part[...] = padded(out_total, out_part.shape[0])


def gradient_blocks(ens, chips, core, slots, place, dpreact, out_part, aggregate_t, emit):
    e, chip = place[0], place[1]
    rows = aggregate_t.shape[2]
    lanes = dpreact.shape[1] // ens
    strip = out_part.shape[0] // ens
    half = strip // 2
    left = aggregate_t[:, core].reshape(chips * rows, -1)
    for slot in slots:
        source = e ^ (0, 2 - core, 1 + core, 3)[slot]
        columns = pl.ds(pl.multiple_of(source * lanes, lanes), lanes)
        block = mul(left, dpreact[:, columns])
        start = pl.multiple_of(source * strip, strip)
        for z in range(chips):
            to = z ^ chip
            columns = pl.ds(pl.multiple_of((2 * z + core) * rows, rows), rows)
            upper = out_part[pl.ds(start, half), columns]
            lower = out_part[pl.ds(start + half, half), columns]
            emit(slot, to, slice(0, rows), slice(0, lanes), block[z * rows : (z + 1) * rows])
            emit(slot, to, slice(rows, rows + half), slice(0, rows), upper)
            emit(slot, to, slice(rows, rows + half), slice(rows, lanes), lower)


def backward_half_body(ens, chips, place, w_out_t, slope, activated, aggregate_t, *refs):
    dforecast, (dpreact, out_part, half) = refs[:ens], refs[ens:]
    backward_body(ens, place, w_out_t, slope, activated, *dforecast, dpreact, out_part)

    def emit(slot, to, rows, lanes, value):
        half[slot - 2, to, rows, lanes] = value.astype(bf16)

    core = 1 - place[2]
    gradient_blocks(ens, chips, core, (2, 3), place, dpreact, out_part, aggregate_t, emit)


def staying_body(ens, chips, place, dpreact, out_part, aggregate_t, half, kept):
    def emit_half(slot, to, rows, lanes, value):
        half[slot, to, rows, lanes] = value.astype(bf16)

    def emit_kept(slot, to, rows, lanes, value):
        kept[slot, to, rows, lanes] = value

    operands = place, dpreact, out_part, aggregate_t
    gradient_blocks(ens, chips, 1 - place[2], (0, 1), *operands, emit_half)
    gradient_blocks(ens, chips, place[2], (0, 1), *operands, emit_kept)


def leaving_body(ens, chips, place, dpreact, out_part, aggregate_t, received, sent):
    def emit(slot, to, rows, lanes, value):
        total = value + received[slot - 2, to, rows, lanes].astype(f32)
        sent[slot - 2, to, rows, lanes] = total.astype(bf16)

    core = place[2]
    gradient_blocks(ens, chips, core, (2, 3), place, dpreact, out_part, aggregate_t, emit)


def window_body(place, dpreact, w_hidden_t, adjacency_t, on_link, on_chip, own):
    mem, nodes, _ = own.shape
    grid = adjacency_t.shape[1]
    first, second = sides(place[2], nodes)
    for m in range(mem):
        total = mul(dpreact[m * grid : (m + 1) * grid], w_hidden_t[...]).astype(bf16)
        on_link[m] = mul(adjacency_t[pl.ds(second, nodes)], total).astype(bf16)
        on_chip[m] = mul(adjacency_t[pl.ds(first, nodes)], total).astype(bf16)
        own[m] = mul(adjacency_t[nodes : 2 * nodes], total)


def latents_body(place, own, on_chip, on_link, total, token):
    for m in range(own.shape[0]):
        total[m] = own[m] + on_chip[m].astype(f32) + on_link[m].astype(f32)
    token[...] = jnp.zeros_like(token)


def staying_sum_body(place, kept, from_core, from_ens, mine, sent):
    mine[0] = kept[0] + from_core[0].astype(f32) + from_ens[0].astype(f32)
    total = kept[1] + from_core[1].astype(f32) + from_ens[1].astype(f32)
    sent[0] = total.astype(bf16)


def chip_slots_body(place, kept, received, mine, *sent):
    count = kept.shape[1]
    for q in range(count):
        total = kept[0, q] + received[0, q].astype(f32)
        if q == 0:
            mine[...] = total
        else:
            sent[count - 1 - q][...] = total.astype(bf16)


def chip_sum_body(place, kept, *refs):
    received, out = refs[:-1], refs[-1]
    total = kept[...]
    for block in received:
        total += block[...].astype(f32)
    out[...] = total.astype(bf16)


def assemble_body(ens, place, *refs):
    pieces, (hidden, out, joined) = refs[:ens], refs[ens:]
    rows, width = hidden.shape
    lanes = width // ens
    strip = 2 * (pieces[0].shape[0] - rows)
    for k, bits in enumerate(routes(ens)):
        source = neighbour(place, bits)
        piece = pieces[k][...].astype(f32)
        hidden[:, pl.ds(pl.multiple_of(source * lanes, lanes), lanes)] = piece[:rows]
        start = pl.multiple_of(source * strip, strip)
        joined[pl.ds(start, strip // 2), :] = piece[rows:, :rows]
        joined[pl.ds(start + strip // 2, strip // 2), :] = piece[rows:, rows:]
    out[...] = joined[: out.shape[0]]


def reduced(w_out_t, slope, activated, aggregate_t, dforecast, variables, place, chips, window):
    ens = len(dforecast)
    mem, grid, width = slope.shape
    rows = width // (2 * chips)
    lanes = width // ens
    strip = 32 * pl.cdiv(variables, 32 * ens)
    aggregate_t = aggregate_t.reshape(chips, 2, rows, -1)
    block = (rows + strip // 2, lanes)
    pair = (2, chips) + block
    flops = mem * grid * width * width

    dpreact, out_part, given = call(
        functools.partial(backward_half_body, ens, chips),
        [((mem * grid, width), bf16), ((ens * strip, width), f32), (pair, bf16)],
        place, w_out_t, slope, activated, aggregate_t, *dforecast,
        flops=flops // 2 + 4 * mem * grid * width * 128,
    )
    leaving = chip_swap(given)
    given, kept = call(
        functools.partial(staying_body, ens, chips), [(pair, bf16), (pair, f32)],
        place, dpreact, out_part, aggregate_t, flops=flops,
    )
    staying = chip_swap(given)
    given = call(
        functools.partial(leaving_body, ens, chips), [(pair, bf16)],
        place, dpreact, out_part, aggregate_t, leaving, after=[kept], flops=flops // 2,
    )[0]
    received = core_swap(given, "ens", (1, 2))
    latents_sum = window(dpreact, given)
    shape = (1, chips) + block
    kept, given = call(
        staying_sum_body, [(shape, f32), (shape, bf16)], place, kept, staying, received
    )
    received = core_swap(given, "ens", (2, 1))
    kept, *given = call(
        chip_slots_body, [(block, f32)] + [(block, bf16)] * (chips - 1), place, kept, received,
        flops=10**9,
    )
    received = [core_swap(given[chips - 1 - q], "chip", (q, q)) for q in range(chips - 1, 0, -1)]
    total = call(chip_sum_body, [(block, bf16)], place, kept, *received, flops=10**9)[0]
    every = exchanged([total] * ens)
    grad_latents, token = latents_sum(total)
    hidden, out = call(
        functools.partial(assemble_body, ens), [((rows, width), f32), ((variables, rows), f32)],
        place, *every, after=[token], last=True, scratch=[pltpu.VMEM((ens * strip, rows), f32)],
    )
    return grad_latents, hidden, out.T


def reduced_any(aggregate_t, dpreact, out_part, variables):
    part = mul(aggregate_t, dpreact)
    summed = lax.psum((part, out_part[:variables].T), "ens")
    return tuple(
        lax.psum_scatter(value, "space", scatter_dimension=0, tiled=True) for value in summed
    )


def shards(latents, edge_index, edge_weight, truth, w_hidden, output_weight):
    mem, nodes, width = latents.shape
    variables, grid = truth.shape
    ens, space = lax.axis_size("ens"), lax.axis_size("space")
    chips = space // 2
    members = mem * ens
    scale = 1.0 / math.sqrt(grid * space * members)
    e, s = lax.axis_index("ens"), lax.axis_index("space")
    place = jnp.stack([e, s // 2, s % 2]).astype(jnp.int32)
    chunk = grid // ens
    w_out_t = output_weight.T

    on_link = link_swap(latents)
    on_chip = chip_swap(latents)
    rows = 8 * pl.cdiv(variables, 8)
    adjacency, adjacency_t, w_hidden_t, own, w_hidden_here, w_out_here, truth_here = call(
        functools.partial(prepare_body, ens),
        [((grid, 3 * nodes), bf16), ((3 * nodes, grid), bf16), (w_hidden.shape[::-1], bf16)]
        + [(latents.shape, bf16), (w_hidden.shape, bf16)]
        + [((rows, width), bf16), ((rows, grid), f32)],
        place, edge_index.T, edge_weight.T, w_out_t, truth, far=[latents, w_hidden],
        scratch=[pltpu.SemaphoreType.DMA((2,))],
    )
    cells = (mem, grid, width)
    partial = call(partial_body, [(cells, f32)], place, own, on_chip, adjacency)[0]
    piece = (mem * rows, chunk)
    aggregate, preact, activated, *pieces = call(
        functools.partial(forward_body, ens),
        [(cells, bf16), (cells, f32), (cells, bf16)] + [(piece, f32)] * ens,
        place, partial, on_link, adjacency, w_hidden_here, w_out_here,
        flops=2 * mem * grid * width * (nodes + width + 128),
    )
    here = exchanged(pieces)
    slope = call(slope_body, [(cells, f32)], place, preact, after=pieces)[0]
    gradients = call(
        functools.partial(loss_body, ens, scale), [(piece, bf16)] * ens, place, truth_here, *here,
        after=[slope],
    )
    dforecast = exchanged(gradients)
    aggregate_t = call(
        turn_body, [((width, mem * grid), bf16)], place, aggregate, after=gradients
    )[0]
    band = (mem, nodes, width)

    def window(dpreact, *before):
        on_link, on_chip, middle = call(
            window_body, [(band, bf16)] * 2 + [(band, f32)],
            place, dpreact, w_hidden_t, adjacency_t, after=before,
            flops=2 * mem * grid * width * (width + 3 * nodes),
        )
        on_link, on_chip = link_swap(on_link), chip_swap(on_chip)

        def total(*before):
            return call(
                latents_body, [(band, f32), ((8, 128), f32)], place, middle, on_chip, on_link,
                after=before, last=True,
            )

        return total

    if width % (space * 128) == 0 and width // ens == 2 * (width // space) and ens == 4:
        return reduced(
            w_out_here, slope, activated, aggregate_t, dforecast, variables, place, chips, window
        )
    dpreact, out_part = call(
        functools.partial(backward_body, ens),
        [((mem * grid, width), bf16), ((rows, width), f32)],
        place, w_out_here, slope, activated, *dforecast,
        flops=4 * mem * grid * width * 128,
    )
    return (window(dpreact)()[0], *reduced_any(aggregate_t, dpreact, out_part, variables))


def solution(mesh):
    placed = (
        P("ens", "space", None),
        P("space", None),
        P("space", None),
        P(None, "space"),
        P(),
        P(),
    )
    return jax.shard_map(
        shards,
        mesh=mesh,
        in_specs=placed,
        out_specs=(P("ens", "space", None), P("space", None), P("space", None)),
        check_vma=False,
    )
```

```python
import functools
import math

import jax
import jax.numpy as jnp
from jax import lax
from jax.experimental import pallas as pl
from jax.experimental.pallas import tpu as pltpu
from jax.sharding import PartitionSpec as P

smoothing = 0.05
f32, bf16 = jnp.float32, jnp.bfloat16
across = (((1,), (0,)), ((), ()))
right_turned = (((1,), (1,)), ((), ()))
left_turned = (((0,), (0,)), ((), ()))


def chip_swap(value):
    count = lax.axis_size("space")
    return lax.ppermute(value, "space", [(i, i ^ 1) for i in range(count)])


def link_swap(value):
    count = lax.axis_size("space")
    pairs = [(i, i + 1) for i in range(1, count - 1, 2)]
    return lax.ppermute(value, "space", pairs + [(j, i) for i, j in pairs])


def core_swap(value, axis, bits):
    ens, space = lax.axis_size("ens"), lax.axis_size("space")

    def partner(e, s):
        bit = bits[s % 2]
        return (e ^ bit) * space + s if axis == "ens" else e * space + (s ^ (2 * bit))

    return lax.ppermute(
        value,
        ("ens", "space"),
        [(e * space + s, partner(e, s)) for e in range(ens) for s in range(space)],
    )


def routes(ens):
    if ens == 4:
        return [(0, 0), (1, 2), (2, 1), (3, 3)]
    return [(k, k) for k in range(ens)]


def exchanged(values):
    others = zip(values[1:], routes(len(values))[1:])
    return [values[0]] + [core_swap(value, "ens", bits) for value, bits in others]


def neighbour(place, bits):
    return place[0] ^ jnp.where(place[2] == 0, bits[0], bits[1])


def mul(a, b, dims=across):
    return lax.dot_general(a, b, dims, preferred_element_type=f32)


def call(body, outs, place, *operands, after=(), far=(), flops=0, last=False, scratch=()):
    vmem = pl.BlockSpec(memory_space=pltpu.VMEM)
    unread = pl.BlockSpec(memory_space=pl.ANY)

    def kernel(place_ref, *refs):
        body(place_ref, *refs[len(after) :])

    return pl.pallas_call(
        kernel,
        out_shape=[
            jax.ShapeDtypeStruct(shape, kind) if last else pltpu.VMEM(shape, kind)
            for shape, kind in outs
        ],
        in_specs=[pl.BlockSpec(memory_space=pltpu.SMEM)]
        + [unread] * len(after)
        + [pl.BlockSpec(memory_space=pltpu.HBM)] * len(far)
        + [vmem] * len(operands),
        out_specs=[vmem] * len(outs),
        scratch_shapes=scratch,
        cost_estimate=pl.CostEstimate(
            flops=flops,
            transcendentals=0,
            bytes_accessed=sum(x.size * x.dtype.itemsize for x in operands)
            + sum(math.prod(shape) * jnp.dtype(kind).itemsize for shape, kind in outs),
        ),
        compiler_params=pltpu.CompilerParams(vmem_limit_bytes=20 * 1024 * 1024),
    )(
        place,
        *after,
        *[pltpu.with_memory_space_constraint(x, pltpu.HBM) for x in far],
        *[pltpu.with_memory_space_constraint(x, pltpu.VMEM) for x in operands],
    )


def sides(core, nodes):
    above, below = 2 * nodes, 0
    return (
        pl.multiple_of(jnp.where(core == 0, above, below), nodes),
        pl.multiple_of(jnp.where(core == 0, below, above), nodes),
    )


def padded(value, rows):
    if value.shape[0] == rows:
        return value
    zeros = jnp.zeros((rows - value.shape[0], value.shape[1]), value.dtype)
    return jnp.concatenate([value, zeros], axis=0)


def prepare_body(
    ens, place, latents, w_hidden, index, weight, w_out_t, truth,
    adjacency, adjacency_t, w_hidden_t, own, w_hidden_here, w_out_here, truth_here, sems
):
    copies = [
        pltpu.make_async_copy(w_hidden, w_hidden_here, sems.at[0]),
        pltpu.make_async_copy(latents, own, sems.at[1]),
    ]
    for copy in copies:
        copy.start()
    edges, grid = index.shape
    chunk = grid // ens
    rows = adjacency_t.shape[0]
    row = lax.broadcasted_iota(jnp.int32, (rows, chunk), 0)
    for k, bits in enumerate(routes(ens)):
        lanes = pl.ds(pl.multiple_of(neighbour(place, bits) * chunk, chunk), chunk)
        nodes = index[:, lanes]
        weights = weight[:, lanes].astype(bf16).astype(f32)
        block = jnp.zeros((rows, chunk), f32)
        for j in range(edges):
            block += jnp.where(nodes[j : j + 1] == row, weights[j : j + 1], 0.0)
        adjacency_t[:, k * chunk : (k + 1) * chunk] = block.astype(bf16)
        adjacency[k * chunk : (k + 1) * chunk, :] = block.T.astype(bf16)
    w_out_here[...] = padded(w_out_t[...].astype(f32), w_out_here.shape[0]).astype(bf16)
    truth_here[...] = padded(truth[...], truth_here.shape[0])
    for copy in copies:
        copy.wait()
    w_hidden_t[...] = w_hidden_here[...].T


def partial_body(place, own, on_chip, adjacency, partial):
    mem, nodes, _ = own.shape
    first, _ = sides(place[2], nodes)
    for m in range(mem):
        total = mul(adjacency[:, nodes : 2 * nodes], own[m])
        partial[m] = total + mul(adjacency[:, pl.ds(first, nodes)], on_chip[m])


def forward_body(
    ens, place, partial, on_link, adjacency, w_hidden, w_out_t, aggregate, preact, activated, *pieces
):
    mem, nodes, width = on_link.shape
    variables = w_out_t.shape[0]
    grid = adjacency.shape[0]
    chunk = grid // ens
    step = 1024
    _, second = sides(place[2], nodes)
    for m in range(mem):
        total = partial[m] + mul(adjacency[:, pl.ds(second, nodes)], on_link[m])
        gathered = total.astype(bf16)
        aggregate[m] = gathered
        forecast = jnp.zeros((grid, variables), f32)
        for at in range(0, width, step):
            value = mul(gathered, w_hidden[:, at : at + step])
            preact[m, :, at : at + step] = value
            silu = (value / (1.0 + jnp.exp(-value))).astype(bf16)
            activated[m, :, at : at + step] = silu
            forecast += mul(silu, w_out_t[:, at : at + step], right_turned)
        turned = forecast.T
        for k in range(ens):
            rows = slice(m * variables, (m + 1) * variables)
            pieces[k][rows] = turned[:, k * chunk : (k + 1) * chunk]


def slope_body(place, preact, slope):
    for m in range(preact.shape[0]):
        value = preact[m]
        logistic = 1.0 / (1.0 + jnp.exp(-value))
        slope[m] = logistic * (1.0 + value * (1.0 - logistic))


def turn_body(place, aggregate, aggregate_t):
    mem, grid, _ = aggregate.shape
    for m in range(mem):
        aggregate_t[:, m * grid : (m + 1) * grid] = aggregate[m].T


def loss_body(ens, scale, place, truth, *refs):
    here, out = refs[:ens], refs[ens:]
    rows, chunk = here[0].shape
    mem = rows // truth.shape[0]
    members = mem * ens
    variables = truth.shape[0]
    target = truth[:, pl.ds(pl.multiple_of(place[0] * chunk, chunk), chunk)]
    forecasts = [
        here[k][m * variables : (m + 1) * variables] for k in range(ens) for m in range(mem)
    ]

    def ratio(d):
        return d * lax.rsqrt(d * d + smoothing * smoothing)

    spread = [jnp.zeros_like(target) for _ in forecasts]
    for i in range(members):
        for j in range(i + 1, members):
            term = ratio(forecasts[i] - forecasts[j])
            spread[i] += term
            spread[j] -= term
    gradients = [
        scale
        * (
            ratio(forecasts[i] - target) * (1.0 / members)
            - spread[i] * (1.0 / (members * (members - 1)))
        )
        for i in range(members)
    ]
    for k in range(ens):
        total = jnp.concatenate(gradients[k * mem : (k + 1) * mem], axis=0)
        out[k][...] = total.astype(bf16)


def backward_body(ens, place, w_out_t, slope, activated, *refs):
    dforecast, (dpreact, out_part) = refs[:ens], refs[ens:]
    mem, grid, _ = slope.shape
    variables = w_out_t.shape[0]
    gradients = jnp.concatenate([piece[...] for piece in dforecast], axis=1)
    gradients = gradients.astype(f32)
    out_total = None
    for m in range(mem):
        gradient = gradients[m * variables : (m + 1) * variables].astype(bf16)
        dactivated = mul(gradient, w_out_t[...], left_turned)
        dpreact[m * grid : (m + 1) * grid] = (dactivated * slope[m]).astype(bf16)
        part = mul(gradient, activated[m])
        out_total = part if out_total is None else out_total + part
    out_part[...] = padded(out_total, out_part.shape[0])


def gradient_blocks(ens, chips, core, slots, place, dpreact, out_part, aggregate_t, emit):
    e, chip = place[0], place[1]
    rows = aggregate_t.shape[2]
    lanes = dpreact.shape[1] // ens
    strip = out_part.shape[0] // ens
    half = strip // 2
    left = aggregate_t[:, core].reshape(chips * rows, -1)
    for slot in slots:
        source = e ^ (0, 2 - core, 1 + core, 3)[slot]
        columns = pl.ds(pl.multiple_of(source * lanes, lanes), lanes)
        block = mul(left, dpreact[:, columns])
        start = pl.multiple_of(source * strip, strip)
        for z in range(chips):
            to = z ^ chip
            columns = pl.ds(pl.multiple_of((2 * z + core) * rows, rows), rows)
            upper = out_part[pl.ds(start, half), columns]
            lower = out_part[pl.ds(start + half, half), columns]
            emit(slot, to, slice(0, rows), slice(0, lanes), block[z * rows : (z + 1) * rows])
            emit(slot, to, slice(rows, rows + half), slice(0, rows), upper)
            emit(slot, to, slice(rows, rows + half), slice(rows, lanes), lower)


def backward_half_body(ens, chips, place, w_out_t, slope, activated, aggregate_t, *refs):
    dforecast, (dpreact, out_part, half) = refs[:ens], refs[ens:]
    backward_body(ens, place, w_out_t, slope, activated, *dforecast, dpreact, out_part)

    def emit(slot, to, rows, lanes, value):
        half[slot - 2, to, rows, lanes] = value.astype(bf16)

    core = 1 - place[2]
    gradient_blocks(ens, chips, core, (2, 3), place, dpreact, out_part, aggregate_t, emit)


def staying_body(ens, chips, place, dpreact, out_part, aggregate_t, half, kept):
    def emit_half(slot, to, rows, lanes, value):
        half[slot, to, rows, lanes] = value.astype(bf16)

    def emit_kept(slot, to, rows, lanes, value):
        kept[slot, to, rows, lanes] = value

    operands = place, dpreact, out_part, aggregate_t
    gradient_blocks(ens, chips, 1 - place[2], (0, 1), *operands, emit_half)
    gradient_blocks(ens, chips, place[2], (0, 1), *operands, emit_kept)


def leaving_body(ens, chips, place, dpreact, out_part, aggregate_t, received, sent):
    def emit(slot, to, rows, lanes, value):
        total = value + received[slot - 2, to, rows, lanes].astype(f32)
        sent[slot - 2, to, rows, lanes] = total.astype(bf16)

    core = place[2]
    gradient_blocks(ens, chips, core, (2, 3), place, dpreact, out_part, aggregate_t, emit)


def window_body(place, dpreact, w_hidden_t, adjacency_t, on_link, on_chip, own):
    mem, nodes, _ = own.shape
    grid = adjacency_t.shape[1]
    first, second = sides(place[2], nodes)
    for m in range(mem):
        total = mul(dpreact[m * grid : (m + 1) * grid], w_hidden_t[...]).astype(bf16)
        on_link[m] = mul(adjacency_t[pl.ds(second, nodes)], total).astype(bf16)
        on_chip[m] = mul(adjacency_t[pl.ds(first, nodes)], total).astype(bf16)
        own[m] = mul(adjacency_t[nodes : 2 * nodes], total)


def latents_body(place, own, on_chip, on_link, total, token):
    for m in range(own.shape[0]):
        total[m] = own[m] + on_chip[m].astype(f32) + on_link[m].astype(f32)
    token[...] = jnp.zeros_like(token)


def staying_sum_body(place, kept, from_core, from_ens, mine, sent):
    mine[0] = kept[0] + from_core[0].astype(f32) + from_ens[0].astype(f32)
    total = kept[1] + from_core[1].astype(f32) + from_ens[1].astype(f32)
    sent[0] = total.astype(bf16)


def chip_slots_body(place, kept, received, mine, *sent):
    count = kept.shape[1]
    for q in range(count):
        total = kept[0, q] + received[0, q].astype(f32)
        if q == 0:
            mine[...] = total
        else:
            sent[count - 1 - q][...] = total.astype(bf16)


def chip_sum_body(place, kept, *refs):
    received, out = refs[:-1], refs[-1]
    total = kept[...]
    for block in received:
        total += block[...].astype(f32)
    out[...] = total.astype(bf16)


def assemble_body(ens, place, *refs):
    pieces, (hidden, out, joined) = refs[:ens], refs[ens:]
    rows, width = hidden.shape
    lanes = width // ens
    strip = 2 * (pieces[0].shape[0] - rows)
    for k, bits in enumerate(routes(ens)):
        source = neighbour(place, bits)
        piece = pieces[k][...].astype(f32)
        hidden[:, pl.ds(pl.multiple_of(source * lanes, lanes), lanes)] = piece[:rows]
        start = pl.multiple_of(source * strip, strip)
        joined[pl.ds(start, strip // 2), :] = piece[rows:, :rows]
        joined[pl.ds(start + strip // 2, strip // 2), :] = piece[rows:, rows:]
    out[...] = joined[: out.shape[0]]


def reduced(w_out_t, slope, activated, aggregate_t, dforecast, variables, place, chips, window):
    ens = len(dforecast)
    mem, grid, width = slope.shape
    rows = width // (2 * chips)
    lanes = width // ens
    strip = 32 * pl.cdiv(variables, 32 * ens)
    aggregate_t = aggregate_t.reshape(chips, 2, rows, -1)
    block = (rows + strip // 2, lanes)
    pair = (2, chips) + block
    flops = mem * grid * width * width

    dpreact, out_part, given = call(
        functools.partial(backward_half_body, ens, chips),
        [((mem * grid, width), bf16), ((ens * strip, width), f32), (pair, bf16)],
        place, w_out_t, slope, activated, aggregate_t, *dforecast,
        flops=flops // 2 + 4 * mem * grid * width * 128,
    )
    leaving = chip_swap(given)
    given, kept = call(
        functools.partial(staying_body, ens, chips), [(pair, bf16), (pair, f32)],
        place, dpreact, out_part, aggregate_t, flops=flops,
    )
    staying = chip_swap(given)
    given = call(
        functools.partial(leaving_body, ens, chips), [(pair, bf16)],
        place, dpreact, out_part, aggregate_t, leaving, after=[kept], flops=flops // 2,
    )[0]
    received = core_swap(given, "ens", (1, 2))
    latents_sum = window(dpreact, given)
    shape = (1, chips) + block
    kept, given = call(
        staying_sum_body, [(shape, f32), (shape, bf16)], place, kept, staying, received
    )
    received = core_swap(given, "ens", (2, 1))
    kept, *given = call(
        chip_slots_body, [(block, f32)] + [(block, bf16)] * (chips - 1), place, kept, received,
        flops=10**9,
    )
    received = [core_swap(given[chips - 1 - q], "chip", (q, q)) for q in range(chips - 1, 0, -1)]
    total = call(chip_sum_body, [(block, bf16)], place, kept, *received, flops=10**9)[0]
    every = exchanged([total] * ens)
    grad_latents, token = latents_sum(total)
    hidden, out = call(
        functools.partial(assemble_body, ens), [((rows, width), f32), ((variables, rows), f32)],
        place, *every, after=[token], last=True, scratch=[pltpu.VMEM((ens * strip, rows), f32)],
    )
    return grad_latents, hidden, out.T


def reduced_any(aggregate_t, dpreact, out_part, variables):
    part = mul(aggregate_t, dpreact)
    summed = lax.psum((part, out_part[:variables].T), "ens")
    return tuple(
        lax.psum_scatter(value, "space", scatter_dimension=0, tiled=True) for value in summed
    )


def shards(latents, edge_index, edge_weight, truth, w_hidden, output_weight):
    mem, nodes, width = latents.shape
    variables, grid = truth.shape
    ens, space = lax.axis_size("ens"), lax.axis_size("space")
    chips = space // 2
    members = mem * ens
    scale = 1.0 / math.sqrt(grid * space * members)
    e, s = lax.axis_index("ens"), lax.axis_index("space")
    place = jnp.stack([e, s // 2, s % 2]).astype(jnp.int32)
    chunk = grid // ens
    w_out_t = output_weight.T

    on_link = link_swap(latents)
    on_chip = chip_swap(latents)
    rows = 8 * pl.cdiv(variables, 8)
    adjacency, adjacency_t, w_hidden_t, own, w_hidden_here, w_out_here, truth_here = call(
        functools.partial(prepare_body, ens),
        [((grid, 3 * nodes), bf16), ((3 * nodes, grid), bf16), (w_hidden.shape[::-1], bf16)]
        + [(latents.shape, bf16), (w_hidden.shape, bf16)]
        + [((rows, width), bf16), ((rows, grid), f32)],
        place, edge_index.T, edge_weight.T, w_out_t, truth, far=[latents, w_hidden],
        scratch=[pltpu.SemaphoreType.DMA((2,))],
    )
    cells = (mem, grid, width)
    partial = call(partial_body, [(cells, f32)], place, own, on_chip, adjacency)[0]
    piece = (mem * rows, chunk)
    aggregate, preact, activated, *pieces = call(
        functools.partial(forward_body, ens),
        [(cells, bf16), (cells, f32), (cells, bf16)] + [(piece, f32)] * ens,
        place, partial, on_link, adjacency, w_hidden_here, w_out_here,
        flops=2 * mem * grid * width * (nodes + width + 128),
    )
    here = exchanged(pieces)
    slope = call(slope_body, [(cells, f32)], place, preact, after=pieces)[0]
    gradients = call(
        functools.partial(loss_body, ens, scale), [(piece, bf16)] * ens, place, truth_here, *here,
        after=[slope],
    )
    dforecast = exchanged(gradients)
    aggregate_t = call(
        turn_body, [((width, mem * grid), bf16)], place, aggregate, after=gradients
    )[0]
    band = (mem, nodes, width)

    def window(dpreact, *before):
        on_link, on_chip, middle = call(
            window_body, [(band, bf16)] * 2 + [(band, f32)],
            place, dpreact, w_hidden_t, adjacency_t, after=before,
            flops=2 * mem * grid * width * (width + 3 * nodes),
        )
        on_link, on_chip = link_swap(on_link), chip_swap(on_chip)

        def total(*before):
            return call(
                latents_body, [(band, f32), ((8, 128), f32)], place, middle, on_chip, on_link,
                after=before, last=True,
            )

        return total

    if width % (space * 128) == 0 and width // ens == 2 * (width // space) and ens == 4:
        return reduced(
            w_out_here, slope, activated, aggregate_t, dforecast, variables, place, chips, window
        )
    dpreact, out_part = call(
        functools.partial(backward_body, ens),
        [((mem * grid, width), bf16), ((rows, width), f32)],
        place, w_out_here, slope, activated, *dforecast,
        flops=4 * mem * grid * width * 128,
    )
    return (window(dpreact)()[0], *reduced_any(aggregate_t, dpreact, out_part, variables))


def solution(mesh):
    placed = (
        P("ens", "space", None),
        P("space", None),
        P("space", None),
        P(None, "space"),
        P(),
        P(),
    )
    return jax.shard_map(
        shards,
        mesh=mesh,
        in_specs=placed,
        out_specs=(P("ens", "space", None), P("space", None), P("space", None)),
        check_vma=False,
    )
```

```python
import functools
import math

import jax
import jax.numpy as jnp
from jax import lax
from jax.experimental import pallas as pl
from jax.experimental.pallas import tpu as pltpu
from jax.sharding import PartitionSpec as P

smoothing = 0.05
f32, bf16 = jnp.float32, jnp.bfloat16
across = (((1,), (0,)), ((), ()))
right_turned = (((1,), (1,)), ((), ()))
left_turned = (((0,), (0,)), ((), ()))


def chip_swap(value):
    count = lax.axis_size("space")
    return lax.ppermute(value, "space", [(i, i ^ 1) for i in range(count)])


def link_swap(value):
    count = lax.axis_size("space")
    pairs = [(i, i + 1) for i in range(1, count - 1, 2)]
    return lax.ppermute(value, "space", pairs + [(j, i) for i, j in pairs])


def core_swap(value, axis, bits):
    ens, space = lax.axis_size("ens"), lax.axis_size("space")

    def partner(e, s):
        bit = bits[s % 2]
        return (e ^ bit) * space + s if axis == "ens" else e * space + (s ^ (2 * bit))

    return lax.ppermute(
        value,
        ("ens", "space"),
        [(e * space + s, partner(e, s)) for e in range(ens) for s in range(space)],
    )


def routes(ens):
    if ens == 4:
        return [(0, 0), (1, 2), (2, 1), (3, 3)]
    return [(k, k) for k in range(ens)]


def exchanged(values):
    others = zip(values[1:], routes(len(values))[1:])
    return [values[0]] + [core_swap(value, "ens", bits) for value, bits in others]


def neighbour(place, bits):
    return place[0] ^ jnp.where(place[2] == 0, bits[0], bits[1])


def mul(a, b, dims=across):
    return lax.dot_general(a, b, dims, preferred_element_type=f32)


def call(body, outs, place, *operands, after=(), far=(), flops=0, last=False, scratch=()):
    vmem = pl.BlockSpec(memory_space=pltpu.VMEM)
    unread = pl.BlockSpec(memory_space=pl.ANY)

    def kernel(place_ref, *refs):
        body(place_ref, *refs[len(after) :])

    return pl.pallas_call(
        kernel,
        out_shape=[
            jax.ShapeDtypeStruct(shape, kind) if last else pltpu.VMEM(shape, kind)
            for shape, kind in outs
        ],
        in_specs=[pl.BlockSpec(memory_space=pltpu.SMEM)]
        + [unread] * len(after)
        + [pl.BlockSpec(memory_space=pltpu.HBM)] * len(far)
        + [vmem] * len(operands),
        out_specs=[vmem] * len(outs),
        scratch_shapes=scratch,
        cost_estimate=pl.CostEstimate(
            flops=flops,
            transcendentals=0,
            bytes_accessed=sum(x.size * x.dtype.itemsize for x in operands)
            + sum(math.prod(shape) * jnp.dtype(kind).itemsize for shape, kind in outs),
        ),
        compiler_params=pltpu.CompilerParams(vmem_limit_bytes=20 * 1024 * 1024),
    )(
        place,
        *after,
        *[pltpu.with_memory_space_constraint(x, pltpu.HBM) for x in far],
        *[pltpu.with_memory_space_constraint(x, pltpu.VMEM) for x in operands],
    )


def sides(core, nodes):
    above, below = 2 * nodes, 0
    return (
        pl.multiple_of(jnp.where(core == 0, above, below), nodes),
        pl.multiple_of(jnp.where(core == 0, below, above), nodes),
    )


def padded(value, rows):
    if value.shape[0] == rows:
        return value
    zeros = jnp.zeros((rows - value.shape[0], value.shape[1]), value.dtype)
    return jnp.concatenate([value, zeros], axis=0)


def prepare_body(
    ens, place, latents, w_hidden, index, weight, w_out_t, truth,
    adjacency, adjacency_t, w_hidden_t, own, w_hidden_here, w_out_here, truth_here, sems
):
    copies = [
        pltpu.make_async_copy(w_hidden, w_hidden_here, sems.at[0]),
        pltpu.make_async_copy(latents, own, sems.at[1]),
    ]
    for copy in copies:
        copy.start()
    edges, grid = index.shape
    chunk = grid // ens
    rows = adjacency_t.shape[0]
    row = lax.broadcasted_iota(jnp.int32, (rows, chunk), 0)
    for k, bits in enumerate(routes(ens)):
        lanes = pl.ds(pl.multiple_of(neighbour(place, bits) * chunk, chunk), chunk)
        nodes = index[:, lanes]
        weights = weight[:, lanes].astype(bf16).astype(f32)
        block = jnp.zeros((rows, chunk), f32)
        for j in range(edges):
            block += jnp.where(nodes[j : j + 1] == row, weights[j : j + 1], 0.0)
        adjacency_t[:, k * chunk : (k + 1) * chunk] = block.astype(bf16)
        adjacency[k * chunk : (k + 1) * chunk, :] = block.T.astype(bf16)
    w_out_here[...] = padded(w_out_t[...].astype(f32), w_out_here.shape[0]).astype(bf16)
    truth_here[...] = padded(truth[...], truth_here.shape[0])
    for copy in copies:
        copy.wait()
    w_hidden_t[...] = w_hidden_here[...].T


def partial_body(place, own, on_chip, adjacency, partial):
    mem, nodes, _ = own.shape
    first, _ = sides(place[2], nodes)
    for m in range(mem):
        total = mul(adjacency[:, nodes : 2 * nodes], own[m])
        partial[m] = total + mul(adjacency[:, pl.ds(first, nodes)], on_chip[m])


def forward_body(
    ens, place, partial, on_link, adjacency, w_hidden, w_out_t, aggregate, preact, activated, *pieces
):
    mem, nodes, width = on_link.shape
    variables = w_out_t.shape[0]
    grid = adjacency.shape[0]
    chunk = grid // ens
    step = 1024
    _, second = sides(place[2], nodes)
    for m in range(mem):
        total = partial[m] + mul(adjacency[:, pl.ds(second, nodes)], on_link[m])
        gathered = total.astype(bf16)
        aggregate[m] = gathered
        forecast = jnp.zeros((grid, variables), f32)
        for at in range(0, width, step):
            value = mul(gathered, w_hidden[:, at : at + step])
            preact[m, :, at : at + step] = value
            silu = (value / (1.0 + jnp.exp(-value))).astype(bf16)
            activated[m, :, at : at + step] = silu
            forecast += mul(silu, w_out_t[:, at : at + step], right_turned)
        turned = forecast.T
        for k in range(ens):
            rows = slice(m * variables, (m + 1) * variables)
            pieces[k][rows] = turned[:, k * chunk : (k + 1) * chunk]


def slope_body(place, preact, slope):
    for m in range(preact.shape[0]):
        value = preact[m]
        logistic = 1.0 / (1.0 + jnp.exp(-value))
        slope[m] = logistic * (1.0 + value * (1.0 - logistic))


def turn_body(place, aggregate, aggregate_t):
    mem, grid, _ = aggregate.shape
    for m in range(mem):
        aggregate_t[:, m * grid : (m + 1) * grid] = aggregate[m].T


def loss_body(ens, scale, place, truth, *refs):
    here, out = refs[:ens], refs[ens:]
    rows, chunk = here[0].shape
    mem = rows // truth.shape[0]
    members = mem * ens
    variables = truth.shape[0]
    target = truth[:, pl.ds(pl.multiple_of(place[0] * chunk, chunk), chunk)]
    forecasts = [
        here[k][m * variables : (m + 1) * variables] for k in range(ens) for m in range(mem)
    ]

    def ratio(d):
        return d * lax.rsqrt(d * d + smoothing * smoothing)

    spread = [jnp.zeros_like(target) for _ in forecasts]
    for i in range(members):
        for j in range(i + 1, members):
            term = ratio(forecasts[i] - forecasts[j])
            spread[i] += term
            spread[j] -= term
    gradients = [
        scale
        * (
            ratio(forecasts[i] - target) * (1.0 / members)
            - spread[i] * (1.0 / (members * (members - 1)))
        )
        for i in range(members)
    ]
    for k in range(ens):
        total = jnp.concatenate(gradients[k * mem : (k + 1) * mem], axis=0)
        out[k][...] = total.astype(bf16)


def backward_body(ens, place, w_out_t, slope, activated, *refs):
    dforecast, (dpreact, out_part) = refs[:ens], refs[ens:]
    mem, grid, _ = slope.shape
    variables = w_out_t.shape[0]
    gradients = jnp.concatenate([piece[...] for piece in dforecast], axis=1)
    gradients = gradients.astype(f32)
    out_total = None
    for m in range(mem):
        gradient = gradients[m * variables : (m + 1) * variables].astype(bf16)
        dactivated = mul(gradient, w_out_t[...], left_turned)
        dpreact[m * grid : (m + 1) * grid] = (dactivated * slope[m]).astype(bf16)
        part = mul(gradient, activated[m])
        out_total = part if out_total is None else out_total + part
    out_part[...] = padded(out_total, out_part.shape[0])


def gradient_blocks(ens, chips, core, slots, place, dpreact, out_part, aggregate_t, emit):
    e, chip = place[0], place[1]
    rows = aggregate_t.shape[2]
    lanes = dpreact.shape[1] // ens
    strip = out_part.shape[0] // ens
    half = strip // 2
    left = aggregate_t[:, core].reshape(chips * rows, -1)
    for slot in slots:
        source = e ^ (0, 2 - core, 1 + core, 3)[slot]
        columns = pl.ds(pl.multiple_of(source * lanes, lanes), lanes)
        block = mul(left, dpreact[:, columns])
        start = pl.multiple_of(source * strip, strip)
        for z in range(chips):
            to = z ^ chip
            columns = pl.ds(pl.multiple_of((2 * z + core) * rows, rows), rows)
            upper = out_part[pl.ds(start, half), columns]
            lower = out_part[pl.ds(start + half, half), columns]
            emit(slot, to, slice(0, rows), slice(0, lanes), block[z * rows : (z + 1) * rows])
            emit(slot, to, slice(rows, rows + half), slice(0, rows), upper)
            emit(slot, to, slice(rows, rows + half), slice(rows, lanes), lower)


def backward_half_body(ens, chips, place, w_out_t, slope, activated, aggregate_t, *refs):
    dforecast, (dpreact, out_part, half) = refs[:ens], refs[ens:]
    backward_body(ens, place, w_out_t, slope, activated, *dforecast, dpreact, out_part)

    def emit(slot, to, rows, lanes, value):
        half[slot - 2, to, rows, lanes] = value.astype(bf16)

    core = 1 - place[2]
    gradient_blocks(ens, chips, core, (2, 3), place, dpreact, out_part, aggregate_t, emit)


def staying_body(ens, chips, place, dpreact, out_part, aggregate_t, half, kept):
    def emit_half(slot, to, rows, lanes, value):
        half[slot, to, rows, lanes] = value.astype(bf16)

    def emit_kept(slot, to, rows, lanes, value):
        kept[slot, to, rows, lanes] = value

    operands = place, dpreact, out_part, aggregate_t
    gradient_blocks(ens, chips, 1 - place[2], (0, 1), *operands, emit_half)
    gradient_blocks(ens, chips, place[2], (0, 1), *operands, emit_kept)


def leaving_body(ens, chips, place, dpreact, out_part, aggregate_t, received, sent):
    def emit(slot, to, rows, lanes, value):
        total = value + received[slot - 2, to, rows, lanes].astype(f32)
        sent[slot - 2, to, rows, lanes] = total.astype(bf16)

    core = place[2]
    gradient_blocks(ens, chips, core, (2, 3), place, dpreact, out_part, aggregate_t, emit)


def window_body(place, dpreact, w_hidden_t, adjacency_t, on_link, on_chip, own):
    mem, nodes, _ = own.shape
    grid = adjacency_t.shape[1]
    first, second = sides(place[2], nodes)
    daggregate = mul(dpreact[...], w_hidden_t[...]).astype(bf16)
    for m in range(mem):
        total = daggregate[m * grid : (m + 1) * grid]
        on_link[m] = mul(adjacency_t[pl.ds(second, nodes)], total).astype(bf16)
        on_chip[m] = mul(adjacency_t[pl.ds(first, nodes)], total).astype(bf16)
        own[m] = mul(adjacency_t[nodes : 2 * nodes], total)


def latents_body(place, own, on_chip, on_link, total, token):
    for m in range(own.shape[0]):
        total[m] = own[m] + on_chip[m].astype(f32) + on_link[m].astype(f32)
    token[...] = jnp.zeros_like(token)


def staying_sum_body(place, kept, from_core, from_ens, mine, sent):
    mine[0] = kept[0] + from_core[0].astype(f32) + from_ens[0].astype(f32)
    total = kept[1] + from_core[1].astype(f32) + from_ens[1].astype(f32)
    sent[0] = total.astype(bf16)


def chip_slots_body(place, kept, received, mine, *sent):
    count = kept.shape[1]
    for q in range(count):
        total = kept[0, q] + received[0, q].astype(f32)
        if q == 0:
            mine[...] = total
        else:
            sent[count - 1 - q][...] = total.astype(bf16)


def chip_sum_body(place, kept, *refs):
    received, out = refs[:-1], refs[-1]
    total = kept[...]
    for block in received:
        total += block[...].astype(f32)
    out[...] = total.astype(bf16)


def assemble_body(ens, place, *refs):
    pieces, (hidden, out, joined) = refs[:ens], refs[ens:]
    rows, width = hidden.shape
    lanes = width // ens
    strip = 2 * (pieces[0].shape[0] - rows)
    for k, bits in enumerate(routes(ens)):
        source = neighbour(place, bits)
        piece = pieces[k][...].astype(f32)
        hidden[:, pl.ds(pl.multiple_of(source * lanes, lanes), lanes)] = piece[:rows]
        start = pl.multiple_of(source * strip, strip)
        joined[pl.ds(start, strip // 2), :] = piece[rows:, :rows]
        joined[pl.ds(start + strip // 2, strip // 2), :] = piece[rows:, rows:]
    out[...] = joined[: out.shape[0]]


def reduced(w_out_t, slope, activated, aggregate_t, dforecast, variables, place, chips, window):
    ens = len(dforecast)
    mem, grid, width = slope.shape
    rows = width // (2 * chips)
    lanes = width // ens
    strip = 32 * pl.cdiv(variables, 32 * ens)
    aggregate_t = aggregate_t.reshape(chips, 2, rows, -1)
    block = (rows + strip // 2, lanes)
    pair = (2, chips) + block
    flops = mem * grid * width * width

    dpreact, out_part, given = call(
        functools.partial(backward_half_body, ens, chips),
        [((mem * grid, width), bf16), ((ens * strip, width), f32), (pair, bf16)],
        place, w_out_t, slope, activated, aggregate_t, *dforecast,
        flops=flops // 2 + 4 * mem * grid * width * 128,
    )
    leaving = chip_swap(given)
    given, kept = call(
        functools.partial(staying_body, ens, chips), [(pair, bf16), (pair, f32)],
        place, dpreact, out_part, aggregate_t, flops=flops,
    )
    staying = chip_swap(given)
    given = call(
        functools.partial(leaving_body, ens, chips), [(pair, bf16)],
        place, dpreact, out_part, aggregate_t, leaving, after=[kept], flops=flops // 2,
    )[0]
    received = core_swap(given, "ens", (1, 2))
    latents_sum = window(dpreact, given)
    shape = (1, chips) + block
    kept, given = call(
        staying_sum_body, [(shape, f32), (shape, bf16)], place, kept, staying, received
    )
    received = core_swap(given, "ens", (2, 1))
    kept, *given = call(
        chip_slots_body, [(block, f32)] + [(block, bf16)] * (chips - 1), place, kept, received,
        flops=10**9,
    )
    received = [core_swap(given[chips - 1 - q], "chip", (q, q)) for q in range(chips - 1, 0, -1)]
    total = call(chip_sum_body, [(block, bf16)], place, kept, *received, flops=10**9)[0]
    every = exchanged([total] * ens)
    grad_latents, token = latents_sum(total)
    hidden, out = call(
        functools.partial(assemble_body, ens), [((rows, width), f32), ((variables, rows), f32)],
        place, *every, after=[token], last=True, scratch=[pltpu.VMEM((ens * strip, rows), f32)],
    )
    return grad_latents, hidden, out.T


def reduced_any(aggregate_t, dpreact, out_part, variables):
    part = mul(aggregate_t, dpreact)
    summed = lax.psum((part, out_part[:variables].T), "ens")
    return tuple(
        lax.psum_scatter(value, "space", scatter_dimension=0, tiled=True) for value in summed
    )


def shards(latents, edge_index, edge_weight, truth, w_hidden, output_weight):
    mem, nodes, width = latents.shape
    variables, grid = truth.shape
    ens, space = lax.axis_size("ens"), lax.axis_size("space")
    chips = space // 2
    members = mem * ens
    scale = 1.0 / math.sqrt(grid * space * members)
    e, s = lax.axis_index("ens"), lax.axis_index("space")
    place = jnp.stack([e, s // 2, s % 2]).astype(jnp.int32)
    chunk = grid // ens
    w_out_t = output_weight.T

    on_link = link_swap(latents)
    on_chip = chip_swap(latents)
    rows = 8 * pl.cdiv(variables, 8)
    adjacency, adjacency_t, w_hidden_t, own, w_hidden_here, w_out_here, truth_here = call(
        functools.partial(prepare_body, ens),
        [((grid, 3 * nodes), bf16), ((3 * nodes, grid), bf16), (w_hidden.shape[::-1], bf16)]
        + [(latents.shape, bf16), (w_hidden.shape, bf16)]
        + [((rows, width), bf16), ((rows, grid), f32)],
        place, edge_index.T, edge_weight.T, w_out_t, truth, far=[latents, w_hidden],
        scratch=[pltpu.SemaphoreType.DMA((2,))],
    )
    cells = (mem, grid, width)
    partial = call(partial_body, [(cells, f32)], place, own, on_chip, adjacency)[0]
    piece = (mem * rows, chunk)
    aggregate, preact, activated, *pieces = call(
        functools.partial(forward_body, ens),
        [(cells, bf16), (cells, f32), (cells, bf16)] + [(piece, f32)] * ens,
        place, partial, on_link, adjacency, w_hidden_here, w_out_here,
        flops=2 * mem * grid * width * (nodes + width + 128),
    )
    here = exchanged(pieces)
    slope = call(slope_body, [(cells, f32)], place, preact, after=pieces)[0]
    gradients = call(
        functools.partial(loss_body, ens, scale), [(piece, bf16)] * ens, place, truth_here, *here,
        after=[slope],
    )
    dforecast = exchanged(gradients)
    aggregate_t = call(
        turn_body, [((width, mem * grid), bf16)], place, aggregate, after=gradients
    )[0]
    band = (mem, nodes, width)

    def window(dpreact, *before):
        on_link, on_chip, middle = call(
            window_body, [(band, bf16)] * 2 + [(band, f32)],
            place, dpreact, w_hidden_t, adjacency_t, after=before,
            flops=2 * mem * grid * width * (width + 3 * nodes),
        )
        on_link, on_chip = link_swap(on_link), chip_swap(on_chip)

        def total(*before):
            return call(
                latents_body, [(band, f32), ((8, 128), f32)], place, middle, on_chip, on_link,
                after=before, last=True,
            )

        return total

    if width % (space * 128) == 0 and width // ens == 2 * (width // space) and ens == 4:
        return reduced(
            w_out_here, slope, activated, aggregate_t, dforecast, variables, place, chips, window
        )
    dpreact, out_part = call(
        functools.partial(backward_body, ens),
        [((mem * grid, width), bf16), ((rows, width), f32)],
        place, w_out_here, slope, activated, *dforecast,
        flops=4 * mem * grid * width * 128,
    )
    return (window(dpreact)()[0], *reduced_any(aggregate_t, dpreact, out_part, variables))


def solution(mesh):
    placed = (
        P("ens", "space", None),
        P("space", None),
        P("space", None),
        P(None, "space"),
        P(),
        P(),
    )
    return jax.shard_map(
        shards,
        mesh=mesh,
        in_specs=placed,
        out_specs=(P("ens", "space", None), P("space", None), P("space", None)),
        check_vma=False,
    )
```
